32 devices in a mesh: groups: 2 (over x), owners: 16 (over z, y, core).
Axes of the slice: x: 2, y: 2, z: 4, core: 2. Of those that a mesh axis runs over, the one named last changes fastest.
Arguments:
- embeddings: bfloat16 [32768, 1024], P(('groups', 'owners')), parts along dimension 0, may hold values from -30 to 30
- cluster_id: int32 [32768], P(('groups', 'owners')), parts along dimension 0, may hold values from 0 to 127, as said below
- valid: int32 [32768], P(('groups', 'owners')), parts along dimension 0, may hold values 0 or 1
Outputs:
- nearest: float32 [32768], P(('groups', 'owners')), parts along dimension 0
The draws below stay inside these ranges and needn't reach their ends.
There are 2 independent parts, one for each index of `groups`. The reference program is written for one: setup_inputs(seed, part) draws one part's arguments, and reference() takes and returns one part's arrays. A program takes and returns all parts, laid end to end along the dimension named above; each array names one. Nothing has to cross between parts.
Inputs may be any that keep to these rules, and one draw needn't show every extreme that they name: `cluster_id`: among the 1024 rows of one device no cluster appears more than 16 times, and one cluster appears exactly 16 times among the rows of every device.
All inputs are finite; a program needn't handle non-finite values. No bound on the sum of `valid` on one device may be relied on, other than what follows from the above.
Results may differ from the reference program's by a relative error of at most 0.00053.
Values may be sent and summed in bfloat16 or wider, within the bound.
No kernel may reach another device: no remote copies, remote signals or barrier semaphores. Data moves between devices by JAX's collectives and lax.ppermute only.
A program may use at most 128 MiB of HBM per device.

```python
import math
import jax
import jax.numpy as jnp
from jax import lax

D = 1024
CL_DEV = 8
SLOT = 16
ROWS_DEV = 1024
ROWS = 16384
CLUSTERS = 128
MEMBERS = 256
N_OWNERS = 16


def cluster_rows(key):
    base = jax.random.fold_in(key, 101)
    giant = jax.random.randint(jax.random.fold_in(base, 0), (), 0, CLUSTERS)
    others = (giant + 1 + jnp.arange((CLUSTERS - 1) * SLOT, dtype=jnp.int32) // SLOT) % CLUSTERS

    def one_block(block_key):
        first_key, second_key = jax.random.split(block_key)
        shuffled = jax.random.permutation(first_key, (CLUSTERS - 1) * SLOT)
        chosen = others[shuffled[:ROWS_DEV - SLOT]]
        labels = jnp.concatenate([jnp.full((SLOT,), giant, jnp.int32), chosen.astype(jnp.int32)])
        return labels[jax.random.permutation(second_key, ROWS_DEV)]
    block_keys = jax.random.split(jax.random.fold_in(base, 1), ROWS // ROWS_DEV)
    return jax.vmap(one_block)(block_keys).reshape(-1).astype(jnp.int32)


def draw_cluster_id(key, part):
    return cluster_rows(key)


def draw_embeddings(key, part):
    labels = cluster_rows(key)
    key = jax.random.fold_in(key, 7)
    copies = max(1, MEMBERS // 8)
    proto_index = jax.random.randint(jax.random.fold_in(key, 1), (ROWS,), 0, copies)
    proto_label = labels * copies + proto_index
    proto_key = jax.random.fold_in(key, 3)
    protos = jax.vmap(lambda label: jax.random.normal(jax.random.fold_in(proto_key, label), (D,), jnp.float32))(proto_label)
    spread = jax.random.uniform(jax.random.fold_in(key, 4), (ROWS, 1), jnp.float32, 0.25, 3.0)
    gains = jnp.exp(jax.random.uniform(jax.random.fold_in(key, 5), (ROWS, 1), jnp.float32, 0.0, math.log(10.0)))
    noise = jax.random.normal(jax.random.fold_in(key, 2), (ROWS, D), jnp.float32)
    values = (protos + spread * noise) * gains * 0.1
    return jnp.clip(values, -30.0, 30.0).astype(jnp.bfloat16)


def place_ends(result, key, smallest, high):
    shape = result.shape
    spot = [jax.random.randint(jax.random.fold_in(key, axis), (), 0, shape[axis]) for axis in range(len(shape))]
    result = result.at[tuple(spot)].set(smallest)
    longest = shape.index(max(shape))
    spot[longest] = (spot[longest] + 1) % shape[longest]
    return result.at[tuple(spot)].set(high)


def setup_inputs(seed: int = 0, part: int = 0) -> dict:
    streams_of = jax.random.split(jax.random.key(seed), 4)
    part_keys = jax.random.split(jax.random.fold_in(streams_of[3], part), 4)
    return {
        "embeddings": draw_embeddings(jax.random.fold_in(jax.random.fold_in(streams_of[3], part), 71), part),
        "cluster_id": draw_cluster_id(jax.random.fold_in(jax.random.fold_in(streams_of[3], part), 71), part),
        "valid": place_ends((jax.random.randint(part_keys[2], (ROWS,), 0, 8) < 7).astype(jnp.int32), jax.random.fold_in(part_keys[2], 1), 0, 1),
    }


def reference(embeddings, cluster_id, valid):
    clusters = CL_DEV * N_OWNERS
    members = N_OWNERS * SLOT
    values = embeddings.astype(jnp.float32)
    squares = lax.optimization_barrier(jnp.sum(values * values, axis=1, keepdims=True))
    scale = lax.rsqrt(squares + 1e-06)
    unit_rows = (values * scale).astype(jnp.bfloat16)
    grouped = cluster_id.reshape(N_OWNERS, ROWS_DEV)
    one_hot = (grouped[:, :, None] == jnp.arange(clusters, dtype=jnp.int32)[None, None, :]).astype(jnp.int32)
    ranking = lax.optimization_barrier(jnp.sum(jnp.cumsum(one_hot, axis=1) * one_hot, axis=2)) - 1
    source = jnp.arange(N_OWNERS, dtype=jnp.int32)[:, None]
    place = ((grouped * N_OWNERS + source) * SLOT + ranking).reshape(-1).astype(jnp.int32)
    table = jnp.full((clusters * members,), ROWS, jnp.int32).at[place].set(jnp.arange(ROWS, dtype=jnp.int32))
    padded_units = jnp.concatenate([unit_rows, jnp.zeros((1, D), jnp.bfloat16)], axis=0)
    padded_live = jnp.concatenate([valid, jnp.zeros((1,), jnp.int32)], axis=0)
    diagonal = jnp.eye(members, dtype=bool)

    def one_cluster(start):
        picks = lax.dynamic_slice_in_dim(table, (start * members).astype(jnp.int32), members)
        chosen = padded_units[picks].astype(jnp.float32)
        flags = padded_live[picks] == 1
        scores = jnp.dot(chosen, chosen.T, precision=lax.Precision.HIGHEST)
        allowed = flags[:, None] & flags[None, :] & ~diagonal
        return lax.optimization_barrier(jnp.max(jnp.where(allowed, scores, -1.0), axis=1))
    maxima = lax.map(one_cluster, jnp.arange(clusters, dtype=jnp.int32)).reshape(-1)
    return jnp.where(valid == 1, maxima[place], 0.0)
```

```python
import functools

import jax
import jax.numpy as jnp
from jax import lax
from jax.experimental import pallas as pl
from jax.experimental.pallas import tpu as pltpu
from jax.sharding import PartitionSpec as P

CL_DEV = 8
SLOT = 16
LANES = 128
FAST = 64
SPILL = 32
STEP = 256
VMEM = 48 * 1024 * 1024
BF = jnp.bfloat16
F32 = jnp.float32


def iota(shape, dim):
    return lax.broadcasted_iota(jnp.int32, shape, dim)


def ahead(chunk):
    return (iota((chunk, chunk), 0) < iota((chunk, chunk), 1)).astype(BF)


def count_ahead(flags):
    rows = flags.shape[1]
    chunk = min(rows, 1024)
    before = ahead(chunk)
    offset = jnp.zeros((flags.shape[0], 1), F32)
    pieces = []
    for start in range(0, rows, chunk):
        part = flags[:, start : start + chunk]
        pieces.append(jnp.dot(part, before, preferred_element_type=F32) + offset)
        offset = offset + jnp.sum(part.astype(F32), axis=1, keepdims=True)
    return jnp.concatenate(pieces, axis=1) if len(pieces) > 1 else pieces[0]


def pack_kernel(
    owners, cid_ref, valid_ref, rows_ref, blocks_ref, spill_ref, code_ref, unit_ref, dest_ref, meta_ref
):
    rows = rows_ref.shape[0]
    step = pl.program_id(0)

    @pl.when(step == 0)
    def _():
        cid = cid_ref[...]
        live = valid_ref[...] == 1
        owner = lax.shift_right_logical(cid, 3)
        local = cid & (CL_DEV - 1)
        mine = (iota((owners, rows), 0) == owner) & live
        mine_f = mine.astype(F32)
        rank = count_ahead(mine_f.astype(BF))
        pos = jnp.sum(mine_f * rank, axis=0, keepdims=True).astype(jnp.int32)
        fits = live & (pos < FAST - 1)
        over = live & (pos >= FAST - 1)
        over_f = jnp.broadcast_to(over.astype(F32), (8, rows))
        spot = count_ahead(over_f.astype(BF))[0:1].astype(jnp.int32)
        spilled = over & (spot < SPILL)
        lost = jnp.max((over & (spot >= SPILL)).astype(F32), axis=1, keepdims=True)
        code = jnp.where(fits, pos, jnp.where(spilled, FAST + spot, LANES - 1))
        code_ref[...] = code
        dest = jnp.where(
            fits, owner * FAST + pos, jnp.where(spilled, owners * FAST + spot, -1)
        )
        dest_ref[...] = dest
        names = jnp.where(mine, (local + 1).astype(F32), 0.0).astype(BF)
        places = (iota((LANES, rows), 0) == code).astype(F32).astype(BF)
        meta = lax.dot_general(
            names, places, (((1,), (1,)), ((), ())), preferred_element_type=F32
        )
        meta_ref[...] = jnp.where(iota((owners, LANES), 1) == LANES - 1, lost, meta)

        def one_chunk(index, carry):
            at = pl.ds(pl.multiple_of(index * LANES, LANES), LANES)
            values = rows_ref[at, :].astype(F32)
            squares = jnp.sum(values * values, axis=1, keepdims=True)
            unit_ref[at, :] = (values * lax.rsqrt(squares + 1e-06)).astype(BF)
            return carry

        lax.fori_loop(0, rows // LANES, one_chunk, 0)
        choose = (iota((SPILL, rows), 0) + owners * FAST == dest).astype(F32).astype(BF)
        spill_ref[...] = jnp.dot(choose, unit_ref[...], preferred_element_type=F32).astype(BF)

    choose = (iota((STEP, rows), 0) + step * STEP == dest_ref[...]).astype(F32).astype(BF)
    packed = jnp.dot(choose, unit_ref[...], preferred_element_type=F32)
    blocks_ref[...] = packed.astype(BF)
    per_step = STEP // FAST
    for block in range(per_step):
        end = (block + 1) * FAST
        meta = meta_ref[pl.ds(step * per_step + block, 1), :]
        tail = packed[end - 16 : end, :LANES]
        blocks_ref[end - 16 : end, :LANES] = jnp.where(
            iota((16, LANES), 0) == 15, meta, tail
        ).astype(BF)


def pack(embeddings, cluster_id, valid, owners):
    rows, width = embeddings.shape
    return pl.pallas_call(
        functools.partial(pack_kernel, owners),
        grid=(owners * FAST // STEP,),
        out_shape=(
            jax.ShapeDtypeStruct((owners * FAST, width), BF),
            jax.ShapeDtypeStruct((SPILL, width), BF),
            jax.ShapeDtypeStruct((1, rows), jnp.int32),
        ),
        in_specs=[
            pl.BlockSpec((1, rows), lambda i: (0, 0)),
            pl.BlockSpec((1, rows), lambda i: (0, 0)),
            pl.BlockSpec((rows, width), lambda i: (0, 0)),
        ],
        out_specs=(
            pl.BlockSpec((STEP, width), lambda i: (i, 0)),
            pl.BlockSpec((SPILL, width), lambda i: (0, 0)),
            pl.BlockSpec((1, rows), lambda i: (0, 0)),
        ),
        scratch_shapes=[
            pltpu.VMEM((rows, width), BF),
            pltpu.VMEM((1, rows), jnp.int32),
            pltpu.VMEM((owners, LANES), F32),
        ],
        compiler_params=pltpu.CompilerParams(vmem_limit_bytes=VMEM),
        name="pack",
    )(cluster_id.reshape(1, rows), valid.reshape(1, rows), embeddings)


def score_kernel(
    owners, got_ref, extra_ref, best_ref, lost_ref, all_ref, side_ref, top_ref, line_ref, sems
):
    step = pl.program_id(0)
    slots = owners * FAST
    total = all_ref.shape[0]

    @pl.when(step == 0)
    def _():
        first = pltpu.make_async_copy(got_ref, all_ref.at[pl.ds(0, slots)], sems.at[0])
        second = pltpu.make_async_copy(
            extra_ref, all_ref.at[pl.ds(slots, owners * SPILL)], sems.at[1]
        )
        first.start()
        second.start()
        first.wait()
        second.wait()
        last = iota((owners, 1), 0) * FAST + (FAST - 1)
        pick = (iota((owners, slots), 1) == last).astype(F32).astype(BF)
        names = jnp.dot(pick, all_ref[pl.ds(0, slots), pl.ds(0, LANES)], preferred_element_type=F32)
        lost_ref[0, 0] = jnp.max(
            jnp.where(iota((owners, LANES), 1) == LANES - 1, names, 0.0)
        ).astype(jnp.int32)
        names = names.astype(BF)
        ones = jnp.ones((LANES, LANES), BF)
        for start, size, first_lane in ((0, FAST, 0), (slots, SPILL, FAST)):
            count = owners * size
            base = iota((count, 1), 0)
            source = base // size
            lane = first_lane + base - source * size
            of_source = (iota((count, owners), 1) == source).astype(F32).astype(BF)
            spread = jnp.dot(of_source, names, preferred_element_type=F32)
            spread = jnp.where(iota((count, LANES), 1) == lane, spread, 0.0).astype(BF)
            side = jnp.dot(spread, ones, preferred_element_type=F32)
            side_ref[pl.ds(start, count), :] = jnp.where(side == 0.0, -1.0, side)
            base = iota((1, count), 1)
            source = base // size
            lane = first_lane + base - source * size
            at_lane = (iota((LANES, count), 0) == lane).astype(F32).astype(BF)
            spread = jnp.dot(names, at_lane, preferred_element_type=F32)
            spread = jnp.where(iota((owners, count), 0) == source, spread, 0.0)
            top_ref[:, pl.ds(start, count)] = jnp.sum(spread, axis=0, keepdims=True)

    here = pl.ds(pl.multiple_of(step * STEP, STEP), STEP)
    right = all_ref[here, :]
    top = top_ref[:, here]
    apart = iota((STEP, STEP), 0) - iota((STEP, STEP), 1)
    result = jnp.full((1, STEP), -1.0, F32)
    for block in range(total // STEP):
        at = slice(block * STEP, (block + 1) * STEP)
        scores = lax.dot_general(
            all_ref[at, :], right, (((1,), (1,)), ((), ())), preferred_element_type=F32
        )
        side = jnp.concatenate([side_ref[at, :]] * (STEP // LANES), axis=1)
        allowed = (side == top) & (apart != (step - block) * STEP)
        masked = jnp.where(allowed, scores, -1.0)
        result = jnp.maximum(result, jnp.max(masked, axis=0, keepdims=True))
    line_ref[:, here] = result

    @pl.when(step == pl.num_programs(0) - 1)
    def _():
        lanes = iota((1, LANES), 1)
        for source in range(owners):
            row, shift = divmod(source * FAST, LANES)
            main = pltpu.roll(line_ref[:, row * LANES : (row + 1) * LANES], (LANES - shift) % LANES, 1)
            row, shift = divmod(slots + source * SPILL, LANES)
            extra = pltpu.roll(
                line_ref[:, row * LANES : (row + 1) * LANES], (LANES + FAST - shift) % LANES, 1
            )
            best_ref[source] = jnp.where(lanes < FAST, main, extra)


def score(got, extra, owners):
    width = got.shape[1]
    total = owners * (FAST + SPILL)
    return pl.pallas_call(
        functools.partial(score_kernel, owners),
        grid=(total // STEP,),
        out_shape=(
            jax.ShapeDtypeStruct((owners, 1, LANES), F32),
            jax.ShapeDtypeStruct((1, 1), jnp.int32),
        ),
        in_specs=[pl.BlockSpec(memory_space=pl.ANY), pl.BlockSpec(memory_space=pl.ANY)],
        out_specs=(
            pl.BlockSpec((owners, 1, LANES), lambda i: (0, 0, 0)),
            pl.BlockSpec(memory_space=pltpu.SMEM),
        ),
        scratch_shapes=[
            pltpu.VMEM((total, width), BF),
            pltpu.VMEM((total, LANES), F32),
            pltpu.VMEM((1, total), F32),
            pltpu.VMEM((1, total), F32),
            pltpu.SemaphoreType.DMA((2,)),
        ],
        compiler_params=pltpu.CompilerParams(vmem_limit_bytes=VMEM),
        name="score",
    )(got, extra)


def place_kernel(owners, back_ref, cid_ref, code_ref, valid_ref, out_ref):
    for start in range(0, cid_ref.shape[0], 8):
        at = slice(start, start + 8)
        owner = lax.shift_right_logical(cid_ref[at, :], 3)
        code = code_ref[at, :]
        result = jnp.zeros((8, LANES), F32)
        for source in range(owners):
            line = jnp.broadcast_to(back_ref[source], (8, LANES))
            value = jnp.take_along_axis(line, code, axis=1, mode="promise_in_bounds")
            result = jnp.where(owner == source, value, result)
        out_ref[at, :] = jnp.where(valid_ref[at, :] == 1, result, 0.0)


def place(back, cluster_id, code, valid, owners):
    rows = cluster_id.shape[0]
    shape = (rows // LANES, LANES)
    return pl.pallas_call(
        functools.partial(place_kernel, owners),
        out_shape=jax.ShapeDtypeStruct(shape, F32),
        name="place",
    )(back, cluster_id.reshape(shape), code.reshape(shape), valid.reshape(shape)).reshape(rows)


def every_slot(embeddings, cluster_id, valid, owners):
    width = embeddings.shape[1]
    clusters = CL_DEV * owners
    values = embeddings.astype(F32)
    squares = jnp.sum(values * values, axis=1, keepdims=True)
    unit_rows = (values * lax.rsqrt(squares + 1e-06)).astype(BF)
    one_hot = (cluster_id[:, None] == jnp.arange(clusters, dtype=jnp.int32)[None, :]).astype(jnp.int32)
    ranking = jnp.sum(jnp.cumsum(one_hot, axis=0) * one_hot, axis=1) - 1
    target = cluster_id * SLOT + ranking
    outgoing = jnp.zeros((clusters * SLOT, width), BF).at[target].set(unit_rows)
    live_out = jnp.zeros((clusters * SLOT,), BF).at[target].set(valid.astype(BF))
    got = lax.all_to_all(
        outgoing.reshape(owners, CL_DEV * SLOT, width), "owners", split_axis=0, concat_axis=0, tiled=True
    )
    live = lax.all_to_all(
        live_out.reshape(owners, CL_DEV, SLOT), "owners", split_axis=0, concat_axis=0, tiled=True
    )
    got = got.reshape(owners, CL_DEV, SLOT, width).transpose(1, 0, 2, 3)
    got = got.reshape(CL_DEV, owners * SLOT, width)
    live = live.transpose(1, 0, 2).reshape(CL_DEV, owners * SLOT) > 0.5
    diagonal = jnp.eye(owners * SLOT, dtype=bool)

    def one_cluster(args):
        rows, flags = args
        scores = jnp.einsum("md,nd->mn", rows, rows, preferred_element_type=F32)
        allowed = flags[:, None] & flags[None, :] & ~diagonal
        return jnp.max(jnp.where(allowed, scores, -1.0), axis=1)

    best = lax.map(one_cluster, (got, live)).reshape(CL_DEV, owners, SLOT).transpose(1, 0, 2)
    back = lax.all_to_all(best, "owners", split_axis=0, concat_axis=0, tiled=True)
    return jnp.where(valid == 1, back.reshape(-1)[target], 0.0)


def shards(embeddings, cluster_id, valid):
    owners = lax.axis_size("owners")
    width = embeddings.shape[1]
    blocks, spill, code = pack(embeddings, cluster_id, valid, owners)
    extra = lax.all_gather(spill, "owners", axis=0, tiled=True)
    got = lax.all_to_all(
        blocks.reshape(owners, FAST, width), "owners", split_axis=0, concat_axis=0, tiled=True
    )
    best, lost = score(got.reshape(owners * FAST, width), extra, owners)
    back = lax.all_to_all(best, "owners", split_axis=0, concat_axis=0, tiled=True)
    nearest = place(back, cluster_id, code, valid, owners)
    return lax.cond(
        lost[0, 0] > 0,
        lambda: every_slot(embeddings, cluster_id, valid, owners),
        lambda: nearest,
    )


def solution(mesh):
    placed = (P(("groups", "owners"), None), P(("groups", "owners")), P(("groups", "owners")))
    return jax.shard_map(
        shards, mesh=mesh, in_specs=placed, out_specs=P(("groups", "owners")), check_vma=False
    )
```

```python
import functools

import jax
import jax.numpy as jnp
from jax import lax
from jax.experimental import pallas as pl
from jax.experimental.pallas import tpu as pltpu
from jax.sharding import PartitionSpec as P

CL_DEV = 8
SLOT = 16
LANES = 128
FAST = 64
SPILL = 32
KEPT = 8
TILE = 1024
STEP = 256
SPAN = 384
VMEM = 48 * 1024 * 1024
BF = jnp.bfloat16
F32 = jnp.float32


def iota(shape, dim):
    return lax.broadcasted_iota(jnp.int32, shape, dim)


def bits(mask):
    return mask.astype(F32).astype(BF)


def product(left, right):
    return jnp.dot(left, right, preferred_element_type=F32)


def product_t(left, right):
    return lax.dot_general(left, right, (((1,), (1,)), ((), ())), preferred_element_type=F32)


def before():
    return bits(iota((LANES, LANES), 0) < iota((LANES, LANES), 1))


def running(flags):
    inside = product(flags, before())
    whole = product(flags, jnp.ones((LANES, LANES), BF))
    rows = flags.shape[0]
    offset = jnp.zeros((1, LANES), F32)
    offsets = []
    for row in range(rows):
        offsets.append(offset)
        offset = offset + whole[row : row + 1]
    return inside + jnp.concatenate(offsets, axis=0)


def pack_kernel(
    owners, cid_ref, valid_ref, rows_ref, blocks_ref, spill_ref, code_ref, held, unit, choose, out, in_sems, out_sems
):
    rows, width = held.shape
    lines = rows // LANES
    parts = rows // STEP
    slots = owners * FAST
    tile = min(slots, TILE)
    loads = []
    for part in range(parts):
        at = pl.ds(part * STEP, STEP)
        loads.append(pltpu.make_async_copy(rows_ref.at[at], held.at[at], in_sems.at[part]))
        loads[-1].start()

    cid = cid_ref[...]
    live = valid_ref[...] == 1
    owner = lax.shift_right_logical(cid, 3)
    name = (cid & (CL_DEV - 1)) + 1
    target = jnp.where(live, owner, -1)
    index = iota((owners, LANES), 0)
    mine = [(index == target[line : line + 1]).astype(F32) for line in range(lines)]
    stacked = jnp.concatenate(mine, axis=0).astype(BF)
    inside = product(stacked, before())
    whole = product(stacked, jnp.ones((LANES, LANES), BF))
    offset = jnp.zeros((owners, LANES), F32)
    ranks = []
    for line in range(lines):
        at = slice(line * owners, (line + 1) * owners)
        ranks.append(jnp.sum(mine[line] * (inside[at] + offset), axis=0, keepdims=True))
        offset = offset + whole[at]
    pos = jnp.concatenate(ranks, axis=0).astype(jnp.int32)
    fits = live & (pos < FAST - 1)
    over = live & (pos >= FAST - 1)
    spot = running(bits(over)).astype(jnp.int32)
    spilled = over & (spot < SPILL)
    lost = jnp.max((over & (spot >= SPILL)).astype(F32))
    code = jnp.where(fits, pos, jnp.where(spilled, FAST + spot, LANES - 1))
    code_ref[...] = code
    slot = owner * FAST + pos
    slot = jnp.where(slot < tile, slot, slot + SPILL)
    dest = jnp.where(fits, slot, jnp.where(spilled, tile + spot, -1))

    names = jnp.concatenate(
        [mine[line] * name[line : line + 1].astype(F32) for line in range(lines)], axis=1
    ).astype(BF)
    index = iota((LANES, LANES), 0)
    places = jnp.concatenate([bits(index == code[line : line + 1]) for line in range(lines)], axis=1)
    meta = product_t(names, places)
    lane = iota((owners, LANES), 1)
    spills = jnp.where((lane >= FAST) & (lane < FAST + SPILL) & (meta > 0.0), 1.0, 0.0)
    if owners < LANES:
        spills = jnp.concatenate([spills, jnp.zeros((LANES - owners, LANES), F32)], axis=0)
    counts = product_t(jnp.ones((8, LANES), BF), spills.astype(BF))[0:1]
    meta = jnp.where(lane == LANES - 1, lost, meta)
    meta = jnp.concatenate([meta, jnp.broadcast_to(counts, (owners, LANES))], axis=1).astype(BF)

    def fill(begin, count):
        index = iota((count, LANES), 0) + begin
        for line in range(lines):
            at = slice(line * LANES, (line + 1) * LANES)
            choose[:count, at] = bits(index == dest[line : line + 1])

    fill(0, tile + SPILL)
    for part in range(parts):
        loads[part].wait()

        def one_chunk(number, carry):
            at = pl.ds(pl.multiple_of(part * STEP + number * 64, 64), 64)
            values = held[at, :].astype(F32)
            squares = jnp.sum(values * values, axis=1, keepdims=True)
            unit[at, :] = (values * lax.rsqrt(squares + 1e-06)).astype(BF)
            return carry

        lax.fori_loop(0, STEP // 64, one_chunk, 0)

    stores = []
    for first in range(0, slots, tile):
        count = tile
        base = first + SPILL
        if first == 0:
            count = tile + SPILL
            base = 0
        else:
            fill(base, count)
        for column in range(0, width, STEP):
            at = slice(column, column + STEP)
            packed = product(choose[:count, :], unit[:, at])
            if column == 0:
                line = iota((count, owners), 0) + first
                line = jnp.where(line < first + tile, line, -1)
                last = iota((count, owners), 1) * FAST + (FAST - 1)
                packed = packed + product(bits(line == last), meta)
            out[pl.ds(base, count), at] = packed.astype(BF)
            moves = [(out.at[pl.ds(base, tile), at], blocks_ref.at[pl.ds(first, tile), at])]
            if first == 0:
                moves.append((out.at[pl.ds(tile, SPILL), at], spill_ref.at[:, at]))
            for source, sink in moves:
                stores.append(pltpu.make_async_copy(source, sink, out_sems.at[len(stores)]))
                stores[-1].start()
    for store in stores:
        store.wait()


def pack(embeddings, cluster_id, valid, owners):
    rows, width = embeddings.shape
    slots = owners * FAST
    tile = min(slots, TILE)
    lines = (rows // LANES, LANES)
    return pl.pallas_call(
        functools.partial(pack_kernel, owners),
        out_shape=(
            pltpu.HBM((slots, width), BF),
            pltpu.HBM((SPILL, width), BF),
            jax.ShapeDtypeStruct(lines, jnp.int32),
        ),
        in_specs=[
            pl.BlockSpec(memory_space=pltpu.VMEM),
            pl.BlockSpec(memory_space=pltpu.VMEM),
            pl.BlockSpec(memory_space=pltpu.HBM),
        ],
        out_specs=(
            pl.BlockSpec(memory_space=pltpu.HBM),
            pl.BlockSpec(memory_space=pltpu.HBM),
            pl.BlockSpec(memory_space=pltpu.VMEM),
        ),
        scratch_shapes=[
            pltpu.VMEM((rows, width), BF),
            pltpu.VMEM((rows, width), BF),
            pltpu.VMEM((tile + SPILL, rows), BF),
            pltpu.VMEM((slots + SPILL, width), BF),
            pltpu.SemaphoreType.DMA((rows // STEP,)),
            pltpu.SemaphoreType.DMA(((slots // tile + 1) * (width // STEP),)),
        ],
        compiler_params=pltpu.CompilerParams(vmem_limit_bytes=VMEM),
        name="pack",
    )(cluster_id.reshape(lines), valid.reshape(lines), embeddings)


def spread(spill, owners):
    bit = owners // 2
    while bit:
        other = lax.ppermute(spill, "owners", [(i, i ^ bit) for i in range(owners)])
        spill = jnp.concatenate([spill, other], axis=0)
        bit //= 2
    return spill


def spread_source(place, owners, me):
    source = jnp.zeros_like(place)
    width = owners.bit_length() - 1
    for bit in range(width):
        source = source + lax.shift_left(lax.shift_right_logical(place, bit) & 1, width - 1 - bit)
    return source ^ me


def score_kernel(owners, got_ref, extra_ref, best_ref, lost_ref, tags, rows, extra, side, top, line, sems):
    slots = owners * FAST
    total, width = rows.shape
    kept = total - slots
    spills = owners * SPILL
    me = lax.axis_index("owners")
    tag_copy = pltpu.make_async_copy(
        got_ref.at[:, pl.ds(FAST - 16, 16), pl.ds(0, 2 * LANES)], tags, sems.at[0]
    )
    tag_copy.start()
    extra_copy = pltpu.make_async_copy(extra_ref, extra, sems.at[1])
    extra_copy.start()
    moves = []
    for source in range(owners):
        moves.append(
            pltpu.make_async_copy(
                got_ref.at[source], rows.at[pl.ds(source * FAST, FAST)], sems.at[2 + source]
            )
        )
        moves[-1].start()
    tag_copy.wait()
    flat = tags[...].reshape(owners * 16, 2 * LANES)
    pick = bits(iota((owners, owners * 16), 1) == iota((owners, owners * 16), 0) * 16 + 15)
    picked = product(pick, flat)
    names, counts = picked[:, :LANES], picked[:, LANES:]
    lane = iota((owners, LANES), 1)
    lost = jnp.max(jnp.where(lane == LANES - 1, names, 0.0))
    crowded = jnp.max(jnp.sum(counts, axis=0, keepdims=True)) > kept
    lost_ref[0, 0] = ((lost > 0.0) | crowded).astype(jnp.int32)
    in_spill = (lane >= FAST) & (lane < FAST + SPILL) & (names > 0.0)
    rank = running(bits(in_spill))
    names_b = names.astype(BF)

    def along_rows(count, size, source, first_lane):
        base = iota((count, 1), 0)
        of_source = bits(iota((count, owners), 1) == source)
        wide = product(of_source, names_b)
        here = iota((count, LANES), 1) == first_lane + base % size
        return product(jnp.where(here, wide, 0.0).astype(BF), jnp.ones((LANES, LANES), BF))

    def along_lanes(values, count, size, source, first_lane):
        at_lane = (iota((LANES, count), 0) == first_lane + iota((1, count), 1) % size).astype(F32)
        wide = jnp.dot(values, at_lane, preferred_element_type=F32, precision=lax.Precision.HIGHEST)
        wide = jnp.where(iota((owners, count), 0) == source, wide, 0.0)
        return jnp.sum(wide, axis=0, keepdims=True)

    found = along_rows(slots, FAST, iota((slots, 1), 0) // FAST, 0)
    side[pl.ds(0, slots), :] = jnp.where(found == 0.0, -1.0, found)
    lines_of = iota((1, slots), 1) // FAST
    top[:, pl.ds(0, slots)] = along_lanes(names, slots, FAST, lines_of, 0)

    sources = spread_source(iota((1, spills), 1) // SPILL, owners, me)
    ranks = along_lanes(jnp.where(in_spill, rank + 1.0, 0.0), spills, SPILL, sources, FAST)
    select = bits(iota((kept, spills), 0).astype(F32) + 1.0 == ranks)
    sources = spread_source(iota((spills, 1), 0) // SPILL, owners, me)
    found = along_rows(spills, SPILL, sources, FAST)
    found = product(select, found.astype(BF))
    side[pl.ds(slots, kept), :] = jnp.where(found == 0.0, -1.0, found)
    sources = spread_source(iota((1, spills), 1) // SPILL, owners, me)
    found = along_lanes(names, spills, SPILL, sources, FAST)
    found = product_t(jnp.broadcast_to(found, (8, spills)).astype(BF), select)
    top[:, pl.ds(slots, kept)] = found[0:1]
    extra_copy.wait()
    rows[pl.ds(slots, kept), :] = product(select, extra[...]).astype(BF)
    for move in moves:
        move.wait()

    unlike = iota((LANES, LANES), 0) != iota((LANES, LANES), 1)

    def columns(first, square):
        here = pl.ds(first, SPAN)
        scores = product_t(rows[...], rows[here, :])
        tops = top[:, here]
        result = [jnp.full((1, LANES), -1.0, F32)] * (SPAN // LANES)
        for block in range(total // LANES):
            at = slice(block * LANES, (block + 1) * LANES)
            for part in range(SPAN // LANES):
                lanes = slice(part * LANES, (part + 1) * LANES)
                allowed = side[at, :] == tops[:, lanes]
                diagonal = square(block, part)
                if diagonal is not None:
                    allowed = allowed & (unlike | diagonal)
                masked = jnp.where(allowed, scores[at, lanes], -1.0)
                result[part] = jnp.maximum(result[part], jnp.max(masked, axis=0, keepdims=True))
        line[:, here] = jnp.concatenate(result, axis=1)

    if total // SPAN <= 4:
        for number in range(total // SPAN):
            columns(
                number * SPAN,
                lambda block, part: False if block == number * (SPAN // LANES) + part else None,
            )
    else:

        @pl.loop(0, total // SPAN)
        def _(number):
            columns(
                pl.multiple_of(number * SPAN, SPAN),
                lambda block, part: block != number * (SPAN // LANES) + part,
            )

    back = [jnp.full((8, LANES), -1.0, F32)] * (owners // 8)
    for piece in range(kept // LANES):
        lines = line[:, slots + piece * LANES : slots + (piece + 1) * LANES]
        lines = jnp.broadcast_to(lines, (8, LANES))
        where = rank.astype(jnp.int32) - piece * LANES
        inside = (where >= 0) & (where < LANES)
        where = jnp.where(inside, where, 0)
        for number in range(owners // 8):
            at = slice(number * 8, number * 8 + 8)
            value = jnp.take_along_axis(lines, where[at], axis=1, mode="promise_in_bounds")
            back[number] = jnp.where(inside[at], value, back[number])
    back = jnp.concatenate(back, axis=0)
    lanes = iota((1, LANES), 1)
    for source in range(owners):
        row, shift = divmod(source * FAST, LANES)
        main = line[:, row * LANES : (row + 1) * LANES]
        if shift:
            main = pltpu.roll(main, LANES - shift, 1)
        best_ref[source] = jnp.where(lanes < FAST, main, back[source : source + 1])


def score(got, extra, owners):
    width = got.shape[2]
    total = owners * FAST + owners * KEPT
    return pl.pallas_call(
        functools.partial(score_kernel, owners),
        out_shape=(
            jax.ShapeDtypeStruct((owners, 1, LANES), F32),
            jax.ShapeDtypeStruct((1, 1), jnp.int32),
        ),
        in_specs=[pl.BlockSpec(memory_space=pltpu.HBM), pl.BlockSpec(memory_space=pltpu.HBM)],
        out_specs=(
            pl.BlockSpec(memory_space=pltpu.VMEM),
            pl.BlockSpec(memory_space=pltpu.SMEM),
        ),
        scratch_shapes=[
            pltpu.VMEM((owners, 16, 2 * LANES), BF),
            pltpu.VMEM((total, width), BF),
            pltpu.VMEM((owners * SPILL, width), BF),
            pltpu.VMEM((total, LANES), F32),
            pltpu.VMEM((1, total), F32),
            pltpu.VMEM((1, total), F32),
            pltpu.SemaphoreType.DMA((2 + owners,)),
        ],
        compiler_params=pltpu.CompilerParams(vmem_limit_bytes=VMEM),
        name="score",
    )(got, extra)


def place_kernel(owners, back_ref, cid_ref, code_ref, valid_ref, out_ref):
    for start in range(0, cid_ref.shape[0], 8):
        at = slice(start, start + 8)
        owner = lax.shift_right_logical(cid_ref[at, :], 3)
        code = code_ref[at, :]
        result = jnp.zeros((8, LANES), F32)
        for source in range(owners):
            line = jnp.broadcast_to(back_ref[source], (8, LANES))
            value = jnp.take_along_axis(line, code, axis=1, mode="promise_in_bounds")
            result = jnp.where(owner == source, value, result)
        out_ref[at, :] = jnp.where(valid_ref[at, :] == 1, result, 0.0)


def place(back, cluster_id, code, valid, owners):
    rows = cluster_id.shape[0]
    shape = (rows // LANES, LANES)
    return pl.pallas_call(
        functools.partial(place_kernel, owners),
        out_shape=jax.ShapeDtypeStruct(shape, F32),
        name="place",
    )(back, cluster_id.reshape(shape), code, valid.reshape(shape)).reshape(rows)


def every_slot(embeddings, cluster_id, valid, owners):
    width = embeddings.shape[1]
    clusters = CL_DEV * owners
    values = embeddings.astype(F32)
    squares = jnp.sum(values * values, axis=1, keepdims=True)
    unit_rows = (values * lax.rsqrt(squares + 1e-06)).astype(BF)
    one_hot = (cluster_id[:, None] == jnp.arange(clusters, dtype=jnp.int32)[None, :]).astype(jnp.int32)
    ranking = jnp.sum(jnp.cumsum(one_hot, axis=0) * one_hot, axis=1) - 1
    target = cluster_id * SLOT + ranking
    outgoing = jnp.zeros((clusters * SLOT, width), BF).at[target].set(unit_rows)
    live_out = jnp.zeros((clusters * SLOT,), BF).at[target].set(valid.astype(BF))
    got = lax.all_to_all(
        outgoing.reshape(owners, CL_DEV * SLOT, width), "owners", split_axis=0, concat_axis=0, tiled=True
    )
    live = lax.all_to_all(
        live_out.reshape(owners, CL_DEV, SLOT), "owners", split_axis=0, concat_axis=0, tiled=True
    )
    got = got.reshape(owners, CL_DEV, SLOT, width).transpose(1, 0, 2, 3)
    got = got.reshape(CL_DEV, owners * SLOT, width)
    live = live.transpose(1, 0, 2).reshape(CL_DEV, owners * SLOT) > 0.5
    diagonal = jnp.eye(owners * SLOT, dtype=bool)

    def one_cluster(args):
        rows, flags = args
        scores = jnp.einsum("md,nd->mn", rows, rows, preferred_element_type=F32)
        allowed = flags[:, None] & flags[None, :] & ~diagonal
        return jnp.max(jnp.where(allowed, scores, -1.0), axis=1)

    best = lax.map(one_cluster, (got, live)).reshape(CL_DEV, owners, SLOT).transpose(1, 0, 2)
    back = lax.all_to_all(best, "owners", split_axis=0, concat_axis=0, tiled=True)
    return jnp.where(valid == 1, back.reshape(-1)[target], 0.0)


def shards(embeddings, cluster_id, valid):
    owners = lax.axis_size("owners")
    width = embeddings.shape[1]
    blocks, spill, code = pack(embeddings, cluster_id, valid, owners)
    extra = spread(spill, owners)
    got = lax.all_to_all(
        blocks.reshape(owners, FAST, width), "owners", split_axis=0, concat_axis=0, tiled=True
    )
    best, lost = score(got, extra, owners)
    back = lax.all_to_all(best, "owners", split_axis=0, concat_axis=0, tiled=True)
    nearest = place(back, cluster_id, code, valid, owners)
    return lax.cond(
        lost[0, 0] > 0,
        lambda: every_slot(embeddings, cluster_id, valid, owners),
        lambda: nearest,
    )


def solution(mesh):
    placed = (P(("groups", "owners"), None), P(("groups", "owners")), P(("groups", "owners")))
    return jax.shard_map(
        shards, mesh=mesh, in_specs=placed, out_specs=P(("groups", "owners")), check_vma=False
    )
```

```python
import functools

import jax
import jax.numpy as jnp
from jax import lax
from jax.experimental import pallas as pl
from jax.experimental.pallas import tpu as pltpu
from jax.sharding import PartitionSpec as P

CL_DEV = 8
SLOT = 16
LANES = 128
NEAR = 96
FAR = 80
TILE = 1408
STEP = 256
VMEM = 56 * 1024 * 1024
BF = jnp.bfloat16
F32 = jnp.float32


def iota(shape, dim):
    return lax.broadcasted_iota(jnp.int32, shape, dim)


def bits(mask):
    return mask.astype(F32).astype(BF)


def product(left, right):
    return jnp.dot(left, right, preferred_element_type=F32)


def product_t(left, right):
    return lax.dot_general(left, right, (((1,), (1,)), ((), ())), preferred_element_type=F32)


def before():
    return bits(iota((LANES, LANES), 0) < iota((LANES, LANES), 1))


def size_of(owners, k):
    half = owners // 2
    return (NEAR, k * NEAR) if k < half else (FAR, half * NEAR + (k - half) * FAR)


def regions(owners):
    half = owners // 2
    return ((0, half, NEAR, 0), (half, half, FAR, half * NEAR))


def start_of(owners, k):
    half = owners // 2
    return jnp.where(k < half, k * NEAR, half * NEAR + (k - half) * FAR)


def pack_kernel(owners, cid_ref, valid_ref, rows_ref, *refs):
    blocks = refs[:owners]
    code_ref, held, unit, choose, out, in_sems, out_sems = refs[owners:]
    rows, width = held.shape
    lines = rows // LANES
    parts = rows // STEP
    total = out.shape[0]
    tile = choose.shape[0]
    me = lax.axis_index("owners")
    loads = []
    for part in range(parts):
        at = pl.ds(part * STEP, STEP)
        loads.append(pltpu.make_async_copy(rows_ref.at[at], held.at[at], in_sems.at[part]))
        loads[-1].start()

    cid = cid_ref[...]
    live = valid_ref[...] == 1
    step = lax.shift_right_logical(cid, 3) ^ me
    name = (cid & (CL_DEV - 1)) + 1
    target = jnp.where(live, step, -1)
    index = iota((owners, LANES), 0)
    mine = [(index == target[line : line + 1]).astype(F32) for line in range(lines)]
    stacked = jnp.concatenate(mine, axis=0).astype(BF)
    inside = product(stacked, before())
    whole = product(stacked, jnp.ones((LANES, LANES), BF))
    offset = jnp.zeros((owners, LANES), F32)
    ranks = []
    for line in range(lines):
        at = slice(line * owners, (line + 1) * owners)
        ranks.append(jnp.sum(mine[line] * (inside[at] + offset), axis=0, keepdims=True))
        offset = offset + whole[at]
    pos = jnp.concatenate(ranks, axis=0).astype(jnp.int32)
    room = jnp.where(step < owners // 2, NEAR - 1, FAR - 1)
    fits = live & (pos < room)
    lost = jnp.max((live & (pos >= room)).astype(F32))
    code = jnp.where(fits, pos, LANES - 1)
    code_ref[...] = code
    dest = jnp.where(fits, start_of(owners, step) + pos, -1)

    names = jnp.concatenate(
        [mine[line] * name[line : line + 1].astype(F32) for line in range(lines)], axis=1
    ).astype(BF)
    index = iota((LANES, LANES), 0)
    places = jnp.concatenate([bits(index == code[line : line + 1]) for line in range(lines)], axis=1)
    meta = product_t(names, places)
    meta = jnp.where(iota((owners, LANES), 1) == LANES - 1, lost, meta).astype(BF)

    def fill(begin, count):
        index = iota((count, LANES), 0) + begin
        for line in range(lines):
            at = slice(line * LANES, (line + 1) * LANES)
            choose[:, at] = bits(index == dest[line : line + 1])

    fill(0, tile)
    for part in range(parts):
        loads[part].wait()

        def one_chunk(number, carry):
            at = pl.ds(pl.multiple_of(part * STEP + number * 64, 64), 64)
            values = held[at, :].astype(F32)
            squares = jnp.sum(values * values, axis=1, keepdims=True)
            unit[at, :] = (values * lax.rsqrt(squares + 1e-06)).astype(BF)
            return carry

        lax.fori_loop(0, STEP // 64, one_chunk, 0)

    stores = []
    for first in range(0, total, tile):
        if first:
            fill(first, tile)
        for column in range(0, width, STEP):
            at = slice(column, column + STEP)
            packed = product(choose[...], unit[:, at])
            if column == 0:
                line = iota((tile, owners), 0) + first
                last = start_of(owners, iota((1, owners), 1) + 1) - 1
                packed = jnp.concatenate(
                    [packed[:, :LANES] + product(bits(line == last), meta), packed[:, LANES:]], axis=1
                )
            out[pl.ds(first, tile), at] = packed.astype(BF)
            for k in range(owners):
                size, start = size_of(owners, k)
                if first < start + size <= first + tile:
                    stores.append(
                        pltpu.make_async_copy(
                            out.at[pl.ds(start, size), at], blocks[k].at[:, at], out_sems.at[len(stores)]
                        )
                    )
                    stores[-1].start()
    for store in stores:
        store.wait()


def total_of(owners):
    return owners // 2 * (NEAR + FAR)


def pack(embeddings, cluster_id, valid, owners):
    rows, width = embeddings.shape
    total = total_of(owners)
    tile = min(total, TILE)
    lines = (rows // LANES, LANES)
    sizes = [size_of(owners, k)[0] for k in range(owners)]
    *blocks, code = pl.pallas_call(
        functools.partial(pack_kernel, owners),
        out_shape=[pltpu.HBM((size, width), BF) for size in sizes]
        + [jax.ShapeDtypeStruct(lines, jnp.int32)],
        in_specs=[
            pl.BlockSpec(memory_space=pltpu.VMEM),
            pl.BlockSpec(memory_space=pltpu.VMEM),
            pl.BlockSpec(memory_space=pltpu.HBM),
        ],
        out_specs=[pl.BlockSpec(memory_space=pltpu.HBM)] * owners
        + [pl.BlockSpec(memory_space=pltpu.VMEM)],
        scratch_shapes=[
            pltpu.VMEM((rows, width), BF),
            pltpu.VMEM((rows, width), BF),
            pltpu.VMEM((tile, rows), BF),
            pltpu.VMEM((total, width), BF),
            pltpu.SemaphoreType.DMA((rows // STEP,)),
            pltpu.SemaphoreType.DMA((owners * (width // STEP),)),
        ],
        compiler_params=pltpu.CompilerParams(vmem_limit_bytes=VMEM),
        name="pack",
    )(cluster_id.reshape(lines), valid.reshape(lines), embeddings)
    return blocks, code


def swap(block, k, owners):
    if k == 0:
        return block
    return lax.ppermute(block, "owners", [(i, i ^ k) for i in range(owners)])


def score_kernel(owners, *refs):
    got = refs[:owners]
    best = refs[owners : 2 * owners]
    lost_ref, tags, rows, side, top, line, tag_sems, sems = refs[2 * owners :]
    total, width = rows.shape
    tag_copies, moves = [], []
    for k in range(owners):
        size, start = size_of(owners, k)
        tag_copies.append(
            pltpu.make_async_copy(
                got[k].at[pl.ds(size - 16, 16), pl.ds(0, LANES)], tags.at[k], tag_sems.at[k]
            )
        )
        tag_copies[-1].start()
    for k in range(owners):
        size, start = size_of(owners, k)
        moves.append(pltpu.make_async_copy(got[k], rows.at[pl.ds(start, size)], sems.at[k]))
        moves[-1].start()
    for copy in tag_copies:
        copy.wait()
    flat = tags[...].reshape(owners * 16, LANES)
    pick = bits(iota((owners, owners * 16), 1) == iota((owners, owners * 16), 0) * 16 + 15)
    names = product(pick, flat)
    lost = jnp.max(jnp.where(iota((owners, LANES), 1) == LANES - 1, names, 0.0))
    lost_ref[0, 0] = (lost > 0.0).astype(jnp.int32)
    names = names.astype(BF)
    for first, blocks, size, start in regions(owners):
        count = blocks * size
        base = iota((count, 1), 0)
        wide = product(bits(iota((count, owners), 1) == first + base // size), names)
        wide = jnp.where(iota((count, LANES), 1) == base % size, wide, 0.0).astype(BF)
        found = product(wide, jnp.ones((LANES, LANES), BF))
        side[pl.ds(start, count), :] = jnp.where(found == 0.0, -1.0, found)
        base = iota((1, count), 1)
        wide = product(names, bits(iota((LANES, count), 0) == base % size))
        wide = jnp.where(iota((owners, count), 0) == first + base // size, wide, 0.0)
        top[:, pl.ds(start, count)] = jnp.sum(wide, axis=0, keepdims=True)
    for move in moves:
        move.wait()

    unlike = iota((LANES, LANES), 0) != iota((LANES, LANES), 1)

    def columns(first, span, square):
        here = pl.ds(first, span)
        scores = product_t(rows[...], rows[here, :])
        tops = top[:, here]
        result = [jnp.full((1, LANES), -1.0, F32)] * (span // LANES)
        for block in range(total // LANES):
            at = slice(block * LANES, (block + 1) * LANES)
            for part in range(span // LANES):
                lanes = slice(part * LANES, (part + 1) * LANES)
                allowed = side[at, :] == tops[:, lanes]
                diagonal = square(block, part)
                if diagonal is not None:
                    allowed = allowed & (unlike | diagonal)
                masked = jnp.where(allowed, scores[at, lanes], -1.0)
                result[part] = jnp.maximum(result[part], jnp.max(masked, axis=0, keepdims=True))
        line[:, here] = jnp.concatenate(result, axis=1)

    if total <= 2048:
        for first in range(0, total, STEP):
            columns(
                first,
                min(STEP, total - first),
                lambda block, part: False if block == first // LANES + part else None,
            )
    else:

        @pl.loop(0, total // STEP)
        def _(number):
            columns(
                pl.multiple_of(number * STEP, STEP),
                STEP,
                lambda block, part: block != number * (STEP // LANES) + part,
            )

    for k in range(owners):
        size, start = size_of(owners, k)
        base, shift = divmod(start, LANES)
        base *= LANES
        piece = line[:, base : min(base + 2 * LANES, total)]
        if shift:
            piece = pltpu.roll(piece, piece.shape[1] - shift, 1)
        best[k][...] = piece[:, :LANES]


def score(got, owners):
    width = got[0].shape[1]
    total = total_of(owners)
    *best, lost = pl.pallas_call(
        functools.partial(score_kernel, owners),
        out_shape=[jax.ShapeDtypeStruct((1, LANES), F32)] * owners
        + [jax.ShapeDtypeStruct((1, 1), jnp.int32)],
        in_specs=[pl.BlockSpec(memory_space=pltpu.HBM)] * owners,
        out_specs=[pl.BlockSpec(memory_space=pltpu.VMEM)] * owners
        + [pl.BlockSpec(memory_space=pltpu.SMEM)],
        scratch_shapes=[
            pltpu.VMEM((owners, 16, LANES), BF),
            pltpu.VMEM((total, width), BF),
            pltpu.VMEM((total, LANES), F32),
            pltpu.VMEM((1, total), F32),
            pltpu.VMEM((1, total), F32),
            pltpu.SemaphoreType.DMA((owners,)),
            pltpu.SemaphoreType.DMA((owners,)),
        ],
        compiler_params=pltpu.CompilerParams(vmem_limit_bytes=VMEM),
        name="score",
    )(*got)
    return best, lost


def place_kernel(owners, *refs):
    back = refs[:owners]
    cid_ref, code_ref, valid_ref, out_ref = refs[owners:]
    me = lax.axis_index("owners")
    for start in range(0, cid_ref.shape[0], 8):
        at = slice(start, start + 8)
        step = lax.shift_right_logical(cid_ref[at, :], 3) ^ me
        code = code_ref[at, :]
        result = jnp.zeros((8, LANES), F32)
        for k in range(owners):
            line = jnp.broadcast_to(back[k][...], (8, LANES))
            value = jnp.take_along_axis(line, code, axis=1, mode="promise_in_bounds")
            result = jnp.where(step == k, value, result)
        out_ref[at, :] = jnp.where(valid_ref[at, :] == 1, result, 0.0)


def place(back, cluster_id, code, valid, owners):
    rows = cluster_id.shape[0]
    shape = (rows // LANES, LANES)
    return pl.pallas_call(
        functools.partial(place_kernel, owners),
        out_shape=jax.ShapeDtypeStruct(shape, F32),
        name="place",
    )(*back, cluster_id.reshape(shape), code, valid.reshape(shape)).reshape(rows)


def every_slot(embeddings, cluster_id, valid, owners):
    width = embeddings.shape[1]
    clusters = CL_DEV * owners
    values = embeddings.astype(F32)
    squares = jnp.sum(values * values, axis=1, keepdims=True)
    unit_rows = (values * lax.rsqrt(squares + 1e-06)).astype(BF)
    one_hot = (cluster_id[:, None] == jnp.arange(clusters, dtype=jnp.int32)[None, :]).astype(jnp.int32)
    ranking = jnp.sum(jnp.cumsum(one_hot, axis=0) * one_hot, axis=1) - 1
    target = cluster_id * SLOT + ranking
    outgoing = jnp.zeros((clusters * SLOT, width), BF).at[target].set(unit_rows)
    live_out = jnp.zeros((clusters * SLOT,), BF).at[target].set(valid.astype(BF))
    got = lax.all_to_all(
        outgoing.reshape(owners, CL_DEV * SLOT, width), "owners", split_axis=0, concat_axis=0, tiled=True
    )
    live = lax.all_to_all(
        live_out.reshape(owners, CL_DEV, SLOT), "owners", split_axis=0, concat_axis=0, tiled=True
    )
    got = got.reshape(owners, CL_DEV, SLOT, width).transpose(1, 0, 2, 3)
    got = got.reshape(CL_DEV, owners * SLOT, width)
    live = live.transpose(1, 0, 2).reshape(CL_DEV, owners * SLOT) > 0.5
    diagonal = jnp.eye(owners * SLOT, dtype=bool)

    def one_cluster(args):
        rows, flags = args
        scores = jnp.einsum("md,nd->mn", rows, rows, preferred_element_type=F32)
        allowed = flags[:, None] & flags[None, :] & ~diagonal
        return jnp.max(jnp.where(allowed, scores, -1.0), axis=1)

    best = lax.map(one_cluster, (got, live)).reshape(CL_DEV, owners, SLOT).transpose(1, 0, 2)
    back = lax.all_to_all(best, "owners", split_axis=0, concat_axis=0, tiled=True)
    return jnp.where(valid == 1, back.reshape(-1)[target], 0.0)


def shards(embeddings, cluster_id, valid):
    owners = lax.axis_size("owners")
    blocks, code = pack(embeddings, cluster_id, valid, owners)
    got = list(blocks)
    for k in reversed(range(owners)):
        got[k] = swap(blocks[k], k, owners)
    best, lost = score(got, owners)
    back = [swap(best[k], k, owners) for k in range(owners)]
    nearest = place(back, cluster_id, code, valid, owners)
    return lax.cond(
        lost[0, 0] > 0,
        lambda: every_slot(embeddings, cluster_id, valid, owners),
        lambda: nearest,
    )


def solution(mesh):
    placed = (P(("groups", "owners"), None), P(("groups", "owners")), P(("groups", "owners")))
    return jax.shard_map(
        shards, mesh=mesh, in_specs=placed, out_specs=P(("groups", "owners")), check_vma=False
    )
```

```python
import functools

import jax
import jax.numpy as jnp
from jax import lax
from jax.experimental import pallas as pl
from jax.experimental.pallas import tpu as pltpu
from jax.sharding import PartitionSpec as P

CL_DEV = 8
SLOT = 16
LANES = 128
SIZE = 80
TILE = 1280
STEP = 256
MB = 1024 * 1024
BF = jnp.bfloat16
F32 = jnp.float32
ANY = pl.BlockSpec(memory_space=pltpu.HBM)
IN_VMEM = pl.BlockSpec(memory_space=pltpu.VMEM)


def iota(shape, dim):
    return lax.broadcasted_iota(jnp.int32, shape, dim)


def bits(mask):
    return mask.astype(F32).astype(BF)


def product(left, right):
    return jnp.dot(left, right, preferred_element_type=F32)


def product_t(left, right):
    return lax.dot_general(left, right, (((1,), (1,)), ((), ())), preferred_element_type=F32)


def before():
    return bits(iota((LANES, LANES), 0) < iota((LANES, LANES), 1))


def fill(choose, dest, begin):
    index = iota((choose.shape[0], LANES), 0) + begin
    for line in range(dest.shape[0]):
        at = slice(line * LANES, (line + 1) * LANES)
        choose[:, at] = bits(index == dest[line : line + 1])


def first_kernel(
    owners, cid_ref, valid_ref, rows_ref, blocks_ref, rest_ref, dest_ref, code_ref, held, unit, choose, out, in_sems, out_sems
):
    rows, width = held.shape
    total, early = out.shape
    tile = choose.shape[0]
    lines = rows // LANES
    parts = rows // STEP
    loads = []
    for part in range(parts):
        at = pl.ds(part * STEP, STEP)
        loads.append(pltpu.make_async_copy(rows_ref.at[at], held.at[at], in_sems.at[part]))
        loads[-1].start()

    cid = cid_ref[...]
    live = valid_ref[...] == 1
    owner = lax.shift_right_logical(cid, 3)
    name = (cid & (CL_DEV - 1)) + 1
    target = jnp.where(live, owner, -1)
    index = iota((owners, LANES), 0)
    mine = [(index == target[line : line + 1]).astype(F32) for line in range(lines)]
    stacked = jnp.concatenate(mine, axis=0).astype(BF)
    inside = product(stacked, before())
    whole = product(stacked, jnp.ones((LANES, LANES), BF))
    offset = jnp.zeros((owners, LANES), F32)
    ranks = []
    for line in range(lines):
        at = slice(line * owners, (line + 1) * owners)
        ranks.append(jnp.sum(mine[line] * (inside[at] + offset), axis=0, keepdims=True))
        offset = offset + whole[at]
    pos = jnp.concatenate(ranks, axis=0).astype(jnp.int32)
    fits = live & (pos < SIZE - 1)
    lost = jnp.max((live & (pos >= SIZE - 1)).astype(F32))
    code = jnp.where(fits, pos, LANES - 1)
    code_ref[...] = code
    dest = jnp.where(fits, owner * SIZE + pos, -1)
    dest_ref[...] = dest

    names = jnp.concatenate(
        [mine[line] * name[line : line + 1].astype(F32) for line in range(lines)], axis=1
    ).astype(BF)
    index = iota((LANES, LANES), 0)
    places = jnp.concatenate([bits(index == code[line : line + 1]) for line in range(lines)], axis=1)
    meta = product_t(names, places)
    meta = jnp.where(iota((owners, LANES), 1) == LANES - 1, lost, meta).astype(BF)

    fill(choose, dest, 0)
    for part in range(parts):
        loads[part].wait()

        def one_chunk(number, carry):
            at = pl.ds(pl.multiple_of(part * STEP + number * 64, 64), 64)
            values = held[at, :].astype(F32)
            squares = jnp.sum(values * values, axis=1, keepdims=True)
            unit[at, :] = (values * lax.rsqrt(squares + 1e-06)).astype(BF)
            return carry

        lax.fori_loop(0, STEP // 64, one_chunk, 0)

    stores = [pltpu.make_async_copy(unit.at[:, pl.ds(early, width - early)], rest_ref, out_sems.at[0])]
    stores[0].start()
    for first in range(0, total, tile):
        if first:
            fill(choose, dest, first)
        for column in range(0, early, STEP):
            at = slice(column, column + STEP)
            packed = product(choose[...], unit[:, at])
            if column == 0:
                line = iota((tile, owners), 0) + first
                last = (iota((1, owners), 1) + 1) * SIZE - 1
                packed = jnp.concatenate(
                    [packed[:, :LANES] + product(bits(line == last), meta), packed[:, LANES:]], axis=1
                )
            out[pl.ds(first, tile), at] = packed.astype(BF)
            where = (pl.ds(first, tile), at)
            stores.append(
                pltpu.make_async_copy(out.at[where], blocks_ref.at[where], out_sems.at[len(stores)])
            )
            stores[-1].start()
    for store in stores:
        store.wait()


def second_kernel(dest_ref, unit_ref, blocks_ref, choose, out, sems):
    total, late = out.shape
    tile = choose.shape[0]
    stores = []
    for first in range(0, total, tile):
        fill(choose, dest_ref[...], first)
        out[pl.ds(first, tile), :] = product(choose[...], unit_ref[...]).astype(BF)
        at = pl.ds(first, tile)
        stores.append(pltpu.make_async_copy(out.at[at], blocks_ref.at[at], sems.at[len(stores)]))
        stores[-1].start()
    for store in stores:
        store.wait()


def early_of(width):
    return width * 3 // 4


def pack(embeddings, cluster_id, valid, owners):
    rows, width = embeddings.shape
    early = early_of(width)
    total = owners * SIZE
    tile = min(total, TILE)
    lines = (rows // LANES, LANES)
    blocks, rest, dest, code = pl.pallas_call(
        functools.partial(first_kernel, owners),
        out_shape=(
            pltpu.HBM((total, early), BF),
            pltpu.HBM((rows, width - early), BF),
            jax.ShapeDtypeStruct(lines, jnp.int32),
            jax.ShapeDtypeStruct(lines, jnp.int32),
        ),
        in_specs=[IN_VMEM, IN_VMEM, ANY],
        out_specs=(ANY, ANY, IN_VMEM, IN_VMEM),
        scratch_shapes=[
            pltpu.VMEM((rows, width), BF),
            pltpu.VMEM((rows, width), BF),
            pltpu.VMEM((tile, rows), BF),
            pltpu.VMEM((total, early), BF),
            pltpu.SemaphoreType.DMA((rows // STEP,)),
            pltpu.SemaphoreType.DMA((1 + total // tile * (early // STEP),)),
        ],
        compiler_params=pltpu.CompilerParams(vmem_limit_bytes=48 * MB),
        name="pack_first",
    )(cluster_id.reshape(lines), valid.reshape(lines), embeddings)
    later = pl.pallas_call(
        second_kernel,
        out_shape=pltpu.HBM((total, width - early), BF),
        in_specs=[IN_VMEM, IN_VMEM],
        out_specs=ANY,
        scratch_shapes=[
            pltpu.VMEM((tile, rows), BF),
            pltpu.VMEM((total, width - early), BF),
            pltpu.SemaphoreType.DMA((total // tile,)),
        ],
        compiler_params=pltpu.CompilerParams(vmem_limit_bytes=40 * MB),
        name="pack_second",
    )(dest, rest)
    return blocks, later, code


def load_tags(owners, got_ref, tags, sem):
    return pltpu.make_async_copy(got_ref.at[:, pl.ds(SIZE - 16, 16), pl.ds(0, LANES)], tags, sem)


def read_tags(owners, tags, lost_ref, side, top):
    flat = tags[...].reshape(owners * 16, LANES)
    pick = bits(iota((owners, owners * 16), 1) == iota((owners, owners * 16), 0) * 16 + 15)
    names = product(pick, flat)
    lost = jnp.max(jnp.where(iota((owners, LANES), 1) == LANES - 1, names, 0.0))
    lost_ref[0, 0] = (lost > 0.0).astype(jnp.int32)
    names = names.astype(BF)
    count = owners * SIZE
    base = iota((count, 1), 0)
    wide = product(bits(iota((count, owners), 1) == base // SIZE), names)
    wide = jnp.where(iota((count, LANES), 1) == base % SIZE, wide, 0.0).astype(BF)
    found = product(wide, jnp.ones((LANES, LANES), BF))
    side[...] = jnp.where(found == 0.0, -1.0, found)
    base = iota((1, count), 1)
    wide = product(names, bits(iota((LANES, count), 0) == base % SIZE))
    wide = jnp.where(iota((owners, count), 0) == base // SIZE, wide, 0.0)
    top[...] = jnp.sum(wide, axis=0, keepdims=True)


def masked(scores, side, tops, block, part, square):
    allowed = side[block * LANES : (block + 1) * LANES, :] == tops[:, part * LANES : (part + 1) * LANES]
    if square is not None:
        unlike = iota((LANES, LANES), 0) != iota((LANES, LANES), 1)
        allowed = allowed & (unlike | square)
    here = scores[block * LANES : (block + 1) * LANES, part * LANES : (part + 1) * LANES]
    return jnp.where(allowed, here, -4.0)


def fetch_rows(got_ref, rows, sems):
    moves = []
    for source in range(got_ref.shape[0]):
        moves.append(
            pltpu.make_async_copy(
                got_ref.at[source], rows.at[pl.ds(source * SIZE, SIZE)], sems.at[source]
            )
        )
        moves[-1].start()
    return moves


def give_back(owners, line, best_ref):
    total = line.shape[1]
    for source in range(owners):
        base, shift = divmod(source * SIZE, LANES)
        base *= LANES
        piece = line[:, base : min(base + 2 * LANES, total)]
        if shift:
            piece = pltpu.roll(piece, piece.shape[1] - shift, 1)
        best_ref[source] = piece[:, :LANES]


def spans(total):
    return [(first, min(STEP, total - first)) for first in range(0, total, STEP)]


def part_kernel(owners, got_ref, part_ref, lost_ref, tags, rows, side, top, sems):
    total = rows.shape[0]
    tag_copy = load_tags(owners, got_ref, tags, sems.at[owners])
    tag_copy.start()
    moves = fetch_rows(got_ref, rows, sems)
    tag_copy.wait()
    read_tags(owners, tags, lost_ref, side, top)
    for move in moves:
        move.wait()
    for first, span in spans(total):
        scores = product_t(rows[...], rows[first : first + span, :])
        tops = top[:, first : first + span]
        for block in range(total // LANES):
            for part in range(span // LANES):
                square = False if block * LANES == first + part * LANES else None
                part_ref[
                    block * LANES : (block + 1) * LANES,
                    first + part * LANES : first + (part + 1) * LANES,
                ] = masked(scores, side, tops, block, part, square)


def last_kernel(owners, got_ref, part_ref, best_ref, rows, line, sems):
    total = rows.shape[0]
    for move in fetch_rows(got_ref, rows, sems):
        move.wait()
    for first, span in spans(total):
        scores = product_t(rows[...], rows[first : first + span, :])
        result = jnp.full((8, span), -1.0, F32)
        for block in range(total // 8):
            at = slice(block * 8, (block + 1) * 8)
            result = jnp.maximum(result, scores[at] + part_ref[at, first : first + span])
        line[:, first : first + span] = jnp.max(result, axis=0, keepdims=True)
    give_back(owners, line, best_ref)


def score(got, later, owners):
    early, late = got.shape[2], later.shape[2]
    total = owners * SIZE
    part, lost = pl.pallas_call(
        functools.partial(part_kernel, owners),
        out_shape=(
            jax.ShapeDtypeStruct((total, total), F32),
            jax.ShapeDtypeStruct((1, 1), jnp.int32),
        ),
        in_specs=[ANY],
        out_specs=(IN_VMEM, pl.BlockSpec(memory_space=pltpu.SMEM)),
        scratch_shapes=[
            pltpu.VMEM((owners, 16, LANES), BF),
            pltpu.VMEM((total, early), BF),
            pltpu.VMEM((total, LANES), F32),
            pltpu.VMEM((1, total), F32),
            pltpu.SemaphoreType.DMA((owners + 1,)),
        ],
        compiler_params=pltpu.CompilerParams(vmem_limit_bytes=32 * MB),
        name="score_first",
    )(got)
    best = pl.pallas_call(
        functools.partial(last_kernel, owners),
        out_shape=jax.ShapeDtypeStruct((owners, 1, LANES), F32),
        in_specs=[ANY, IN_VMEM],
        out_specs=IN_VMEM,
        scratch_shapes=[
            pltpu.VMEM((total, late), BF),
            pltpu.VMEM((1, total), F32),
            pltpu.SemaphoreType.DMA((owners,)),
        ],
        compiler_params=pltpu.CompilerParams(vmem_limit_bytes=32 * MB),
        name="score_second",
    )(later, part)
    return best, lost


def whole_kernel(owners, got_ref, later_ref, best_ref, lost_ref, tags, rows, rest, side, top, line, sems, late_sems):
    total = rows.shape[0]
    tag_copy = load_tags(owners, got_ref, tags, sems.at[owners])
    tag_copy.start()
    moves = fetch_rows(got_ref, rows, sems) + fetch_rows(later_ref, rest, late_sems)
    tag_copy.wait()
    read_tags(owners, tags, lost_ref, side, top)
    for move in moves:
        move.wait()

    @pl.loop(0, total // STEP)
    def _(number):
        here = pl.ds(pl.multiple_of(number * STEP, STEP), STEP)
        tops = top[:, here]
        scores = product_t(rows[...], rows[here, :]) + product_t(rest[...], rest[here, :])
        pieces = []
        for part in range(STEP // LANES):
            result = jnp.full((1, LANES), -1.0, F32)
            for block in range(total // LANES):
                square = block != number * (STEP // LANES) + part
                found = masked(scores, side, tops, block, part, square)
                result = jnp.maximum(result, jnp.max(found, axis=0, keepdims=True))
            pieces.append(result)
        line[:, here] = jnp.concatenate(pieces, axis=1)

    give_back(owners, line, best_ref)


def score_whole(got, later, owners):
    early, late = got.shape[2], later.shape[2]
    total = owners * SIZE
    return pl.pallas_call(
        functools.partial(whole_kernel, owners),
        out_shape=(
            jax.ShapeDtypeStruct((owners, 1, LANES), F32),
            jax.ShapeDtypeStruct((1, 1), jnp.int32),
        ),
        in_specs=[ANY, ANY],
        out_specs=(IN_VMEM, pl.BlockSpec(memory_space=pltpu.SMEM)),
        scratch_shapes=[
            pltpu.VMEM((owners, 16, LANES), BF),
            pltpu.VMEM((total, early), BF),
            pltpu.VMEM((total, late), BF),
            pltpu.VMEM((total, LANES), F32),
            pltpu.VMEM((1, total), F32),
            pltpu.VMEM((1, total), F32),
            pltpu.SemaphoreType.DMA((owners + 1,)),
            pltpu.SemaphoreType.DMA((owners,)),
        ],
        compiler_params=pltpu.CompilerParams(vmem_limit_bytes=48 * MB),
        name="score_whole",
    )(got, later)


def place_kernel(owners, back_ref, cid_ref, code_ref, valid_ref, out_ref):
    for start in range(0, cid_ref.shape[0], 8):
        at = slice(start, start + 8)
        owner = lax.shift_right_logical(cid_ref[at, :], 3)
        code = code_ref[at, :]
        result = jnp.zeros((8, LANES), F32)
        for source in range(owners):
            line = jnp.broadcast_to(back_ref[source], (8, LANES))
            value = jnp.take_along_axis(line, code, axis=1, mode="promise_in_bounds")
            result = jnp.where(owner == source, value, result)
        out_ref[at, :] = jnp.where(valid_ref[at, :] == 1, result, 0.0)


def place(back, cluster_id, code, valid, owners):
    rows = cluster_id.shape[0]
    shape = (rows // LANES, LANES)
    return pl.pallas_call(
        functools.partial(place_kernel, owners),
        out_shape=jax.ShapeDtypeStruct(shape, F32),
        name="place",
    )(back, cluster_id.reshape(shape), code, valid.reshape(shape)).reshape(rows)


def every_slot(embeddings, cluster_id, valid, owners):
    width = embeddings.shape[1]
    clusters = CL_DEV * owners
    values = embeddings.astype(F32)
    squares = jnp.sum(values * values, axis=1, keepdims=True)
    unit_rows = (values * lax.rsqrt(squares + 1e-06)).astype(BF)
    one_hot = (cluster_id[:, None] == jnp.arange(clusters, dtype=jnp.int32)[None, :]).astype(jnp.int32)
    ranking = jnp.sum(jnp.cumsum(one_hot, axis=0) * one_hot, axis=1) - 1
    target = cluster_id * SLOT + ranking
    outgoing = jnp.zeros((clusters * SLOT, width), BF).at[target].set(unit_rows)
    live_out = jnp.zeros((clusters * SLOT,), BF).at[target].set(valid.astype(BF))
    got = lax.all_to_all(
        outgoing.reshape(owners, CL_DEV * SLOT, width), "owners", split_axis=0, concat_axis=0, tiled=True
    )
    live = lax.all_to_all(
        live_out.reshape(owners, CL_DEV, SLOT), "owners", split_axis=0, concat_axis=0, tiled=True
    )
    got = got.reshape(owners, CL_DEV, SLOT, width).transpose(1, 0, 2, 3)
    got = got.reshape(CL_DEV, owners * SLOT, width)
    live = live.transpose(1, 0, 2).reshape(CL_DEV, owners * SLOT) > 0.5
    diagonal = jnp.eye(owners * SLOT, dtype=bool)

    def one_cluster(args):
        rows, flags = args
        scores = jnp.einsum("md,nd->mn", rows, rows, preferred_element_type=F32)
        allowed = flags[:, None] & flags[None, :] & ~diagonal
        return jnp.max(jnp.where(allowed, scores, -1.0), axis=1)

    best = lax.map(one_cluster, (got, live)).reshape(CL_DEV, owners, SLOT).transpose(1, 0, 2)
    back = lax.all_to_all(best, "owners", split_axis=0, concat_axis=0, tiled=True)
    return jnp.where(valid == 1, back.reshape(-1)[target], 0.0)


def swap(blocks, owners):
    split = blocks.reshape(owners, blocks.shape[0] // owners, blocks.shape[1])
    return lax.all_to_all(split, "owners", split_axis=0, concat_axis=0, tiled=True)


def shards(embeddings, cluster_id, valid):
    owners = lax.axis_size("owners")
    blocks, later, code = pack(embeddings, cluster_id, valid, owners)
    got = swap(blocks, owners)
    later = swap(later, owners)
    scoring = score if owners * SIZE <= 2048 else score_whole
    best, lost = scoring(got, later, owners)
    back = lax.all_to_all(best, "owners", split_axis=0, concat_axis=0, tiled=True)
    nearest = place(back, cluster_id, code, valid, owners)
    return lax.cond(
        lost[0, 0] > 0,
        lambda: every_slot(embeddings, cluster_id, valid, owners),
        lambda: nearest,
    )


def solution(mesh):
    placed = (P(("groups", "owners"), None), P(("groups", "owners")), P(("groups", "owners")))
    return jax.shard_map(
        shards, mesh=mesh, in_specs=placed, out_specs=P(("groups", "owners")), check_vma=False
    )
```

```python
import functools

import jax
import jax.numpy as jnp
from jax import lax
from jax.experimental import pallas as pl
from jax.experimental.pallas import tpu as pltpu
from jax.sharding import PartitionSpec as P

CL_DEV = 8
SLOT = 16
LANES = 128
SIZE = 80
TILE = 1280
STEP = 256
MB = 1024 * 1024
BF = jnp.bfloat16
F32 = jnp.float32
ANY = pl.BlockSpec(memory_space=pltpu.HBM)
IN_VMEM = pl.BlockSpec(memory_space=pltpu.VMEM)


def iota(shape, dim):
    return lax.broadcasted_iota(jnp.int32, shape, dim)


def bits(mask):
    return mask.astype(F32).astype(BF)


def product(left, right):
    return jnp.dot(left, right, preferred_element_type=F32)


def product_t(left, right):
    return lax.dot_general(left, right, (((1,), (1,)), ((), ())), preferred_element_type=F32)


def before():
    return bits(iota((LANES, LANES), 0) < iota((LANES, LANES), 1))


def fill(choose, dest, begin):
    index = iota((choose.shape[0], LANES), 0) + begin
    for line in range(dest.shape[0]):
        at = slice(line * LANES, (line + 1) * LANES)
        choose[:, at] = bits(index == dest[line : line + 1])


def pack_kernel(
    owners, cid_ref, valid_ref, rows_ref, blocks_ref, code_ref, held, unit, choose, out, in_sems, out_sems
):
    rows, width = held.shape
    total = out.shape[0]
    tile = choose.shape[0]
    lines = rows // LANES
    parts = rows // STEP
    loads = []
    for part in range(parts):
        at = pl.ds(part * STEP, STEP)
        loads.append(pltpu.make_async_copy(rows_ref.at[at], held.at[at], in_sems.at[part]))
        loads[-1].start()

    cid = cid_ref[...]
    live = valid_ref[...] == 1
    owner = lax.shift_right_logical(cid, 3)
    name = (cid & (CL_DEV - 1)) + 1
    target = jnp.where(live, owner, -1)
    index = iota((owners, LANES), 0)
    mine = [(index == target[line : line + 1]).astype(F32) for line in range(lines)]
    stacked = jnp.concatenate(mine, axis=0).astype(BF)
    inside = product(stacked, before())
    whole = product(stacked, jnp.ones((LANES, LANES), BF))
    offset = jnp.zeros((owners, LANES), F32)
    ranks = []
    for line in range(lines):
        at = slice(line * owners, (line + 1) * owners)
        ranks.append(jnp.sum(mine[line] * (inside[at] + offset), axis=0, keepdims=True))
        offset = offset + whole[at]
    pos = jnp.concatenate(ranks, axis=0).astype(jnp.int32)
    fits = live & (pos < SIZE - 1)
    lost = jnp.max((live & (pos >= SIZE - 1)).astype(F32))
    code = jnp.where(fits, pos, LANES - 1)
    code_ref[...] = code
    dest = jnp.where(fits, owner * SIZE + pos, -1)

    names = jnp.concatenate(
        [mine[line] * name[line : line + 1].astype(F32) for line in range(lines)], axis=1
    ).astype(BF)
    index = iota((LANES, LANES), 0)
    places = jnp.concatenate([bits(index == code[line : line + 1]) for line in range(lines)], axis=1)
    meta = product_t(names, places)
    meta = jnp.where(iota((owners, LANES), 1) == LANES - 1, lost, meta).astype(BF)

    fill(choose, dest, 0)
    for part in range(parts):
        loads[part].wait()
        for chunk in range(part * STEP, (part + 1) * STEP, 64):
            values = held[chunk : chunk + 64, :].astype(F32)
            squares = jnp.sum(values * values, axis=1, keepdims=True)
            unit[chunk : chunk + 64, :] = (values * lax.rsqrt(squares + 1e-06)).astype(BF)

    stores = []
    for first in range(0, total, tile):
        if first:
            fill(choose, dest, first)
        for column in range(0, width, STEP):
            at = slice(column, column + STEP)
            packed = product(choose[...], unit[:, at])
            if column == 0:
                line = iota((tile, owners), 0) + first
                last = (iota((1, owners), 1) + 1) * SIZE - 1
                packed = jnp.concatenate(
                    [packed[:, :LANES] + product(bits(line == last), meta), packed[:, LANES:]], axis=1
                )
            out[pl.ds(first, tile), at] = packed.astype(BF)
            where = (pl.ds(first, tile), at)
            stores.append(
                pltpu.make_async_copy(out.at[where], blocks_ref.at[where], out_sems.at[len(stores)])
            )
            stores[-1].start()
    for store in stores:
        store.wait()


def pack(embeddings, cluster_id, valid, owners):
    rows, width = embeddings.shape
    total = owners * SIZE
    tile = min(total, TILE)
    lines = (rows // LANES, LANES)
    return pl.pallas_call(
        functools.partial(pack_kernel, owners),
        out_shape=(
            pltpu.HBM((total, width), BF),
            jax.ShapeDtypeStruct(lines, jnp.int32),
        ),
        in_specs=[IN_VMEM, IN_VMEM, ANY],
        out_specs=(ANY, IN_VMEM),
        scratch_shapes=[
            pltpu.VMEM((rows, width), BF),
            pltpu.VMEM((rows, width), BF),
            pltpu.VMEM((tile, rows), BF),
            pltpu.VMEM((total, width), BF),
            pltpu.SemaphoreType.DMA((rows // STEP,)),
            pltpu.SemaphoreType.DMA((total // tile * (width // STEP),)),
        ],
        compiler_params=pltpu.CompilerParams(vmem_limit_bytes=52 * MB),
        name="pack",
    )(cluster_id.reshape(lines), valid.reshape(lines), embeddings)


def score_kernel(owners, got_ref, best_ref, lost_ref, tags, rows, side, line, sems):
    total = rows.shape[0]
    tag_copy = pltpu.make_async_copy(
        got_ref.at[:, pl.ds(SIZE - 16, 16), pl.ds(0, LANES)], tags, sems.at[owners]
    )
    tag_copy.start()
    moves = []
    for source in range(owners):
        moves.append(
            pltpu.make_async_copy(
                got_ref.at[source], rows.at[pl.ds(source * SIZE, SIZE)], sems.at[source]
            )
        )
        moves[-1].start()
    tag_copy.wait()

    flat = tags[...].reshape(owners * 16, LANES)
    pick = bits(iota((owners, owners * 16), 1) == iota((owners, owners * 16), 0) * 16 + 15)
    names = product(pick, flat)
    lost = jnp.max(jnp.where(iota((owners, LANES), 1) == LANES - 1, names, 0.0))
    lost_ref[0, 0] = (lost > 0.0).astype(jnp.int32)
    same = iota((SIZE, LANES), 0) == iota((SIZE, LANES), 1)
    wide = jnp.concatenate(
        [jnp.where(same, names[source : source + 1], 0.0) for source in range(owners)], axis=0
    ).astype(BF)
    found = product(wide, jnp.ones((LANES, LANES), BF))
    side[...] = jnp.where(found == 0.0, -1.0, found)
    tops = product_t(jnp.ones((8, LANES), BF), wide)
    for move in moves:
        move.wait()

    apart = iota((8, LANES), 1) - iota((8, LANES), 0)

    def columns(here, top, diagonal):
        scores = product_t(rows[...], rows[here, :])
        for part in range(STEP // LANES):
            lanes = slice(part * LANES, (part + 1) * LANES)
            result = jnp.full((8, LANES), -1.0, F32)
            for block in range(0, total, 8):
                at = slice(block, block + 8)
                allowed = side[at, :] == top[:, lanes]
                own = diagonal(block, part)
                if own is not None:
                    allowed = allowed & (apart != own)
                result = jnp.maximum(result, jnp.where(allowed, scores[at, lanes], -1.0))
            line[:, pl.ds(here.start + part * LANES, LANES)] = jnp.max(result, axis=0, keepdims=True)

    if total <= 2048:
        for first in range(0, total, STEP):

            def diagonal(block, part):
                own = block - first - part * LANES
                return own if 0 <= own < LANES else None

            columns(pl.ds(first, STEP), tops[:, first : first + STEP], diagonal)
    else:
        line[...] = tops[0:1]

        @pl.loop(0, total // STEP)
        def _(number):
            first = pl.multiple_of(number * STEP, STEP)
            here = pl.ds(first, STEP)
            top = jnp.broadcast_to(line[:, here], (8, STEP))
            columns(here, top, lambda block, part: block - first - part * LANES)

    for source in range(owners):
        base, shift = divmod(source * SIZE, LANES)
        base *= LANES
        piece = line[:, base : min(base + 2 * LANES, total)]
        if shift:
            piece = pltpu.roll(piece, piece.shape[1] - shift, 1)
        best_ref[source] = piece[:, :LANES]


def score(got, owners):
    width = got.shape[2]
    total = owners * SIZE
    return pl.pallas_call(
        functools.partial(score_kernel, owners),
        out_shape=(
            pltpu.VMEM((owners, 1, LANES), F32),
            jax.ShapeDtypeStruct((1, 1), jnp.int32),
        ),
        in_specs=[ANY],
        out_specs=(IN_VMEM, pl.BlockSpec(memory_space=pltpu.SMEM)),
        scratch_shapes=[
            pltpu.VMEM((owners, 16, LANES), BF),
            pltpu.VMEM((total, width), BF),
            pltpu.VMEM((total, LANES), F32),
            pltpu.VMEM((1, total), F32),
            pltpu.SemaphoreType.DMA((owners + 1,)),
        ],
        compiler_params=pltpu.CompilerParams(vmem_limit_bytes=48 * MB),
        name="score",
    )(got)


def place_kernel(owners, back_ref, cid_ref, code_ref, valid_ref, out_ref, back, cid, code, valid, out, sems):
    moves = []
    for source, sink in ((back_ref, back), (cid_ref, cid), (code_ref, code), (valid_ref, valid)):
        moves.append(pltpu.make_async_copy(source, sink, sems.at[len(moves)]))
        moves[-1].start()
    for move in moves:
        move.wait()
    for start in range(0, cid.shape[0], 8):
        at = slice(start, start + 8)
        owner = lax.shift_right_logical(cid[at, :], 3)
        place = code[at, :]
        result = jnp.zeros((8, LANES), F32)
        for source in range(owners):
            line = jnp.broadcast_to(back[source], (8, LANES))
            value = jnp.take_along_axis(line, place, axis=1, mode="promise_in_bounds")
            result = jnp.where(owner == source, value, result)
        out[at, :] = jnp.where(valid[at, :] == 1, result, 0.0)
    store = pltpu.make_async_copy(out, out_ref, sems.at[4])
    store.start()
    store.wait()


def place(back, cluster_id, code, valid, owners):
    rows = cluster_id.shape[0]
    shape = (rows // LANES, LANES)
    return pl.pallas_call(
        functools.partial(place_kernel, owners),
        out_shape=pltpu.HBM(shape, F32),
        in_specs=[ANY] * 4,
        out_specs=ANY,
        scratch_shapes=[
            pltpu.VMEM((owners, 1, LANES), F32),
            pltpu.VMEM(shape, jnp.int32),
            pltpu.VMEM(shape, jnp.int32),
            pltpu.VMEM(shape, jnp.int32),
            pltpu.VMEM(shape, F32),
            pltpu.SemaphoreType.DMA((5,)),
        ],
        name="place",
    )(back, cluster_id.reshape(shape), code, valid.reshape(shape)).reshape(rows)


def every_slot(embeddings, cluster_id, valid, owners):
    width = embeddings.shape[1]
    clusters = CL_DEV * owners
    values = embeddings.astype(F32)
    squares = jnp.sum(values * values, axis=1, keepdims=True)
    unit_rows = (values * lax.rsqrt(squares + 1e-06)).astype(BF)
    one_hot = (cluster_id[:, None] == jnp.arange(clusters, dtype=jnp.int32)[None, :]).astype(jnp.int32)
    ranking = jnp.sum(jnp.cumsum(one_hot, axis=0) * one_hot, axis=1) - 1
    target = cluster_id * SLOT + ranking
    outgoing = jnp.zeros((clusters * SLOT, width), BF).at[target].set(unit_rows)
    live_out = jnp.zeros((clusters * SLOT,), BF).at[target].set(valid.astype(BF))
    got = lax.all_to_all(
        outgoing.reshape(owners, CL_DEV * SLOT, width), "owners", split_axis=0, concat_axis=0, tiled=True
    )
    live = lax.all_to_all(
        live_out.reshape(owners, CL_DEV, SLOT), "owners", split_axis=0, concat_axis=0, tiled=True
    )
    got = got.reshape(owners, CL_DEV, SLOT, width).transpose(1, 0, 2, 3)
    got = got.reshape(CL_DEV, owners * SLOT, width)
    live = live.transpose(1, 0, 2).reshape(CL_DEV, owners * SLOT) > 0.5
    diagonal = jnp.eye(owners * SLOT, dtype=bool)

    def one_cluster(args):
        rows, flags = args
        scores = jnp.einsum("md,nd->mn", rows, rows, preferred_element_type=F32)
        allowed = flags[:, None] & flags[None, :] & ~diagonal
        return jnp.max(jnp.where(allowed, scores, -1.0), axis=1)

    best = lax.map(one_cluster, (got, live)).reshape(CL_DEV, owners, SLOT).transpose(1, 0, 2)
    back = lax.all_to_all(best, "owners", split_axis=0, concat_axis=0, tiled=True)
    return jnp.where(valid == 1, back.reshape(-1)[target], 0.0)


def swap(blocks, owners):
    split = blocks.reshape(owners, blocks.shape[0] // owners, blocks.shape[1])
    return lax.all_to_all(split, "owners", split_axis=0, concat_axis=0, tiled=True)


def shards(embeddings, cluster_id, valid):
    owners = lax.axis_size("owners")
    blocks, code = pack(embeddings, cluster_id, valid, owners)
    best, lost = score(swap(blocks, owners), owners)
    back = lax.all_to_all(best, "owners", split_axis=0, concat_axis=0, tiled=True)
    nearest = place(back, cluster_id, code, valid, owners)
    return lax.cond(
        lost[0, 0] > 0,
        lambda: every_slot(embeddings, cluster_id, valid, owners),
        lambda: nearest,
    )


def solution(mesh):
    placed = (P(("groups", "owners"), None), P(("groups", "owners")), P(("groups", "owners")))
    return jax.shard_map(
        shards, mesh=mesh, in_specs=placed, out_specs=P(("groups", "owners")), check_vma=False
    )
```

```python
import functools

import jax
import jax.numpy as jnp
from jax import lax
from jax.experimental import pallas as pl
from jax.experimental.pallas import tpu as pltpu
from jax.sharding import PartitionSpec as P

CL_DEV = 8
SLOT = 16
LANES = 128
SIZE = 80
TILE = 1280
STEP = 256
MB = 1024 * 1024
BF = jnp.bfloat16
F32 = jnp.float32
ANY = pl.BlockSpec(memory_space=pltpu.HBM)
IN_VMEM = pl.BlockSpec(memory_space=pltpu.VMEM)


def iota(shape, dim):
    return lax.broadcasted_iota(jnp.int32, shape, dim)


def bits(mask):
    return mask.astype(F32).astype(BF)


def product(left, right):
    return jnp.dot(left, right, preferred_element_type=F32)


def product_t(left, right):
    return lax.dot_general(left, right, (((1,), (1,)), ((), ())), preferred_element_type=F32)


def before():
    return bits(iota((LANES, LANES), 0) < iota((LANES, LANES), 1))


def fill(choose, dest, begin):
    index = iota((choose.shape[0], LANES), 0) + begin
    for line in range(dest.shape[0]):
        at = slice(line * LANES, (line + 1) * LANES)
        choose[:, at] = bits(index == dest[line : line + 1])


def pack_kernel(
    owners, cid_ref, valid_ref, rows_ref, blocks_ref, code_ref, held, unit, choose, out, in_sems, out_sems
):
    rows, width = held.shape
    total = out.shape[0]
    tile = choose.shape[0]
    lines = rows // LANES
    parts = rows // STEP
    loads = []
    for part in range(parts):
        at = pl.ds(part * STEP, STEP)
        loads.append(pltpu.make_async_copy(rows_ref.at[at], held.at[at], in_sems.at[part]))
        loads[-1].start()

    cid = cid_ref[...]
    live = valid_ref[...] == 1
    owner = lax.shift_right_logical(cid, 3)
    name = (cid & (CL_DEV - 1)) + 1
    target = jnp.where(live, owner, -1)
    index = iota((owners, LANES), 0)
    mine = [(index == target[line : line + 1]).astype(F32) for line in range(lines)]
    stacked = jnp.concatenate(mine, axis=0).astype(BF)
    inside = product(stacked, before())
    whole = product(stacked, jnp.ones((LANES, LANES), BF))
    offset = jnp.zeros((owners, LANES), F32)
    ranks = []
    for line in range(lines):
        at = slice(line * owners, (line + 1) * owners)
        ranks.append(jnp.sum(mine[line] * (inside[at] + offset), axis=0, keepdims=True))
        offset = offset + whole[at]
    pos = jnp.concatenate(ranks, axis=0).astype(jnp.int32)
    fits = live & (pos < SIZE - 1)
    lost = jnp.max((live & (pos >= SIZE - 1)).astype(F32))
    code = jnp.where(fits, pos, LANES - 1)
    code_ref[...] = code
    dest = jnp.where(fits, owner * SIZE + pos, -1)

    names = jnp.concatenate(
        [mine[line] * name[line : line + 1].astype(F32) for line in range(lines)], axis=1
    ).astype(BF)
    index = iota((LANES, LANES), 0)
    places = jnp.concatenate([bits(index == code[line : line + 1]) for line in range(lines)], axis=1)
    meta = product_t(names, places)
    meta = jnp.where(iota((owners, LANES), 1) == LANES - 1, lost, meta).astype(BF)

    fill(choose, dest, 0)
    for part in range(parts):
        loads[part].wait()
        for chunk in range(part * STEP, (part + 1) * STEP, 64):
            values = held[chunk : chunk + 64, :].astype(F32)
            squares = jnp.sum(values * values, axis=1, keepdims=True)
            unit[chunk : chunk + 64, :] = (values * lax.rsqrt(squares + 1e-06)).astype(BF)

    stores = []
    for first in range(0, total, tile):
        if first:
            fill(choose, dest, first)
        for column in range(0, width, STEP):
            at = slice(column, column + STEP)
            packed = product(choose[...], unit[:, at])
            if column == 0:
                line = iota((tile, owners), 0) + first
                last = (iota((1, owners), 1) + 1) * SIZE - 1
                packed = jnp.concatenate(
                    [packed[:, :LANES] + product(bits(line == last), meta), packed[:, LANES:]], axis=1
                )
            out[pl.ds(first, tile), at] = packed.astype(BF)
            where = (pl.ds(first, tile), at)
            stores.append(
                pltpu.make_async_copy(out.at[where], blocks_ref.at[where], out_sems.at[len(stores)])
            )
            stores[-1].start()
    for store in stores:
        store.wait()


def pack(embeddings, cluster_id, valid, owners):
    rows, width = embeddings.shape
    total = owners * SIZE
    tile = min(total, TILE)
    lines = (rows // LANES, LANES)
    return pl.pallas_call(
        functools.partial(pack_kernel, owners),
        out_shape=(
            pltpu.HBM((total, width), BF),
            jax.ShapeDtypeStruct(lines, jnp.int32),
        ),
        in_specs=[IN_VMEM, IN_VMEM, ANY],
        out_specs=(ANY, IN_VMEM),
        scratch_shapes=[
            pltpu.VMEM((rows, width), BF),
            pltpu.VMEM((rows, width), BF),
            pltpu.VMEM((tile, rows), BF),
            pltpu.VMEM((total, width), BF),
            pltpu.SemaphoreType.DMA((rows // STEP,)),
            pltpu.SemaphoreType.DMA((total // tile * (width // STEP),)),
        ],
        compiler_params=pltpu.CompilerParams(vmem_limit_bytes=52 * MB),
        name="pack",
    )(cluster_id.reshape(lines), valid.reshape(lines), embeddings)


def on_units(size, count, multiply, use):
    def body(*accs):
        for number in range(count + 2):
            if number < count:
                multiply(number, number % 2, accs[number % 4])
            if number >= 2:
                use(number - 2, pltpu.matmul_pop(accs[(number - 2) % 4]))

    pl.run_scoped(body, *[pltpu.ACC(mxu_id=number % 2)((size, STEP), F32) for number in range(4)])


def triangle(total, rows, side, tops, line, across, down):
    width = rows.shape[1]
    blocks = total // STEP
    seen = set()

    def keep(ref, at, value):
        if (id(ref), at) in seen:
            value = jnp.maximum(value, ref[at : at + 8, :])
        seen.add((id(ref), at))
        ref[at : at + 8, :] = value

    work = []
    for column in range(blocks):
        for row in range(column, blocks, 2):
            work.append((column, row, min(2, blocks - row)))

    def run(work, count):
        def multiply(number, unit, acc):
            column, row, _ = work[number]
            for piece in range(width // STEP):
                at = slice(piece * STEP, (piece + 1) * STEP)
                pltpu.matmul_push_rhs(
                    rows[column * STEP : (column + 1) * STEP, at], piece % 2, unit, transpose=True
                )
                pltpu.matmul_acc_lhs(
                    acc, rows[row * STEP : (row + count) * STEP, at], load_staged_rhs=piece % 2
                )

        def use(number, scores):
            column, row, _ = work[number]
            apart = iota((8, LANES), 1) - iota((8, LANES), 0)
            best = [jnp.full((8, LANES), -1.0, F32)] * (STEP // LANES)
            for block in range(0, count * STEP, 8):
                start = row * STEP + block
                found = []
                for part in range(STEP // LANES):
                    first = column * STEP + part * LANES
                    allowed = side[start : start + 8, :] == tops[:, first : first + LANES]
                    if 0 <= start - first < LANES:
                        allowed = allowed & (apart != start - first)
                    here = scores[block : block + 8, part * LANES : (part + 1) * LANES]
                    found.append(jnp.where(allowed, here, -1.0))
                    best[part] = jnp.maximum(best[part], found[part])
                if start // STEP > column:
                    keep(across, start, functools.reduce(jnp.maximum, found))
            for part in range(STEP // LANES):
                keep(down, (column * (STEP // LANES) + part) * 8, best[part])

        on_units(count * STEP, len(work), multiply, use)

    run([item for item in work if item[2] == 2], 2)
    run([item for item in work if item[2] == 1], 1)
    for column in range(blocks):
        for part in range(STEP // LANES):
            first = column * STEP + part * LANES
            at = (column * (STEP // LANES) + part) * 8
            most = jnp.max(down[at : at + 8, :], axis=0, keepdims=True)
            if column:
                turned = across[first : first + LANES, :].T
                most = jnp.maximum(most, jnp.max(turned, axis=0, keepdims=True))
            line[:, first : first + LANES] = most


def score_kernel(owners, got_ref, best_ref, lost_ref, tags, rows, side, line, sems, *more):
    total = rows.shape[0]
    tag_copy = pltpu.make_async_copy(
        got_ref.at[:, pl.ds(SIZE - 16, 16), pl.ds(0, LANES)], tags, sems.at[owners]
    )
    tag_copy.start()
    moves = []
    for source in range(owners):
        moves.append(
            pltpu.make_async_copy(
                got_ref.at[source], rows.at[pl.ds(source * SIZE, SIZE)], sems.at[source]
            )
        )
        moves[-1].start()
    tag_copy.wait()

    same = iota((SIZE, LANES), 0) == iota((SIZE, LANES), 1)
    lanes = iota((1, 2 * LANES), 1)
    lost = jnp.zeros((1, LANES), F32)
    line[...] = jnp.zeros((1, total), F32)
    for source in range(owners):
        name = tags[source].astype(F32)[15:16]
        lost = jnp.maximum(lost, name)
        found = jnp.sum(jnp.where(same, name, 0.0), axis=1, keepdims=True)
        side[source * SIZE : (source + 1) * SIZE, :] = jnp.broadcast_to(
            jnp.where(found == 0.0, -1.0, found), (SIZE, LANES)
        )
        base, shift = divmod(source * SIZE, LANES)
        base *= LANES
        name = jnp.where(lanes < SIZE, jnp.concatenate([name, name], axis=1), 0.0)
        if shift:
            name = pltpu.roll(name, shift, 1)
        size = min(2 * LANES, total - base)
        line[:, base : base + size] = line[:, base : base + size] + name[:, :size]
    lost = jnp.max(jnp.where(lanes[:, :LANES] == LANES - 1, lost, 0.0))
    lost_ref[0, 0] = (lost > 0.0).astype(jnp.int32)
    tops = jnp.broadcast_to(line[...], (8, total))
    for move in moves:
        move.wait()

    if total <= 2048:
        triangle(total, rows, side, tops, line, *more)
    else:
        @pl.loop(0, total // STEP)
        def _(number):
            first = pl.multiple_of(number * STEP, STEP)
            here = pl.ds(first, STEP)
            top = jnp.broadcast_to(line[:, here], (8, STEP))
            scores = product_t(rows[...], rows[here, :])
            apart = iota((8, LANES), 1) - iota((8, LANES), 0)
            for part in range(STEP // LANES):
                lanes = slice(part * LANES, (part + 1) * LANES)
                result = jnp.full((8, LANES), -1.0, F32)
                for block in range(0, total, 8):
                    at = slice(block, block + 8)
                    allowed = (side[at, :] == top[:, lanes]) & (apart != block - first - part * LANES)
                    result = jnp.maximum(result, jnp.where(allowed, scores[at, lanes], -1.0))
                line[:, pl.ds(first + part * LANES, LANES)] = jnp.max(result, axis=0, keepdims=True)

    for source in range(owners):
        base, shift = divmod(source * SIZE, LANES)
        base *= LANES
        piece = line[:, base : min(base + 2 * LANES, total)]
        if shift:
            piece = pltpu.roll(piece, piece.shape[1] - shift, 1)
        best_ref[source] = piece[:, :LANES]


def score(got, owners):
    width = got.shape[2]
    total = owners * SIZE
    return pl.pallas_call(
        functools.partial(score_kernel, owners),
        out_shape=(
            pltpu.VMEM((owners, 1, LANES), F32),
            jax.ShapeDtypeStruct((1, 1), jnp.int32),
        ),
        in_specs=[ANY],
        out_specs=(IN_VMEM, pl.BlockSpec(memory_space=pltpu.SMEM)),
        scratch_shapes=[
            pltpu.VMEM((owners, 16, LANES), BF),
            pltpu.VMEM((total, width), BF),
            pltpu.VMEM((total, LANES), F32),
            pltpu.VMEM((1, total), F32),
            pltpu.SemaphoreType.DMA((owners + 1,)),
        ]
        + ([] if total > 2048 else [pltpu.VMEM((total, LANES), F32), pltpu.VMEM((total // 16, LANES), F32)]),
        compiler_params=pltpu.CompilerParams(vmem_limit_bytes=48 * MB),
        name="score",
    )(got)


def place_kernel(owners, back_ref, cid_ref, code_ref, valid_ref, out_ref, back, out, sems):
    move = pltpu.make_async_copy(back_ref, back, sems.at[0])
    move.start()
    move.wait()
    for start in range(0, cid_ref.shape[0], 8):
        at = slice(start, start + 8)
        owner = lax.shift_right_logical(cid_ref[at, :], 3)
        code = code_ref[at, :]
        result = jnp.zeros((8, LANES), F32)
        for source in range(owners):
            line = jnp.broadcast_to(back[source], (8, LANES))
            value = jnp.take_along_axis(line, code, axis=1, mode="promise_in_bounds")
            result = jnp.where(owner == source, value, result)
        out[at, :] = jnp.where(valid_ref[at, :] == 1, result, 0.0)
    store = pltpu.make_async_copy(out, out_ref, sems.at[1])
    store.start()
    store.wait()


def place(back, cluster_id, code, valid, owners):
    rows = cluster_id.shape[0]
    shape = (rows // LANES, LANES)
    back = pltpu.with_memory_space_constraint(back, pltpu.HBM)
    return pl.pallas_call(
        functools.partial(place_kernel, owners),
        out_shape=pltpu.HBM(shape, F32),
        in_specs=[ANY, IN_VMEM, IN_VMEM, IN_VMEM],
        out_specs=ANY,
        scratch_shapes=[
            pltpu.VMEM((owners, 1, LANES), F32),
            pltpu.VMEM(shape, F32),
            pltpu.SemaphoreType.DMA((2,)),
        ],
        name="place",
    )(back, cluster_id.reshape(shape), code, valid.reshape(shape)).reshape(rows)


def every_slot(embeddings, cluster_id, valid, owners):
    width = embeddings.shape[1]
    clusters = CL_DEV * owners
    values = embeddings.astype(F32)
    squares = jnp.sum(values * values, axis=1, keepdims=True)
    unit_rows = (values * lax.rsqrt(squares + 1e-06)).astype(BF)
    one_hot = (cluster_id[:, None] == jnp.arange(clusters, dtype=jnp.int32)[None, :]).astype(jnp.int32)
    ranking = jnp.sum(jnp.cumsum(one_hot, axis=0) * one_hot, axis=1) - 1
    target = cluster_id * SLOT + ranking
    outgoing = jnp.zeros((clusters * SLOT, width), BF).at[target].set(unit_rows)
    live_out = jnp.zeros((clusters * SLOT,), BF).at[target].set(valid.astype(BF))
    got = lax.all_to_all(
        outgoing.reshape(owners, CL_DEV * SLOT, width), "owners", split_axis=0, concat_axis=0, tiled=True
    )
    live = lax.all_to_all(
        live_out.reshape(owners, CL_DEV, SLOT), "owners", split_axis=0, concat_axis=0, tiled=True
    )
    got = got.reshape(owners, CL_DEV, SLOT, width).transpose(1, 0, 2, 3)
    got = got.reshape(CL_DEV, owners * SLOT, width)
    live = live.transpose(1, 0, 2).reshape(CL_DEV, owners * SLOT) > 0.5
    diagonal = jnp.eye(owners * SLOT, dtype=bool)

    def one_cluster(args):
        rows, flags = args
        scores = jnp.einsum("md,nd->mn", rows, rows, preferred_element_type=F32)
        allowed = flags[:, None] & flags[None, :] & ~diagonal
        return jnp.max(jnp.where(allowed, scores, -1.0), axis=1)

    best = lax.map(one_cluster, (got, live)).reshape(CL_DEV, owners, SLOT).transpose(1, 0, 2)
    back = lax.all_to_all(best, "owners", split_axis=0, concat_axis=0, tiled=True)
    return jnp.where(valid == 1, back.reshape(-1)[target], 0.0)


def swap(blocks, owners):
    split = blocks.reshape(owners, blocks.shape[0] // owners, blocks.shape[1])
    return lax.all_to_all(split, "owners", split_axis=0, concat_axis=0, tiled=True)


def shards(embeddings, cluster_id, valid):
    owners = lax.axis_size("owners")
    blocks, code = pack(embeddings, cluster_id, valid, owners)
    best, lost = score(swap(blocks, owners), owners)
    back = lax.all_to_all(best, "owners", split_axis=0, concat_axis=0, tiled=True)
    nearest = place(back, cluster_id, code, valid, owners)
    return lax.cond(
        lost[0, 0] > 0,
        lambda: every_slot(embeddings, cluster_id, valid, owners),
        lambda: nearest,
    )


def solution(mesh):
    placed = (P(("groups", "owners"), None), P(("groups", "owners")), P(("groups", "owners")))
    return jax.shard_map(
        shards, mesh=mesh, in_specs=placed, out_specs=P(("groups", "owners")), check_vma=False
    )
```

```python
import functools

import jax
import jax.numpy as jnp
from jax import lax
from jax.experimental import pallas as pl
from jax.experimental.pallas import tpu as pltpu
from jax.sharding import PartitionSpec as P

CL_DEV = 8
SLOT = 16
LANES = 128
SIZE = 80
TILE = 1280
STEP = 256
MB = 1024 * 1024
BF = jnp.bfloat16
F32 = jnp.float32
ANY = pl.BlockSpec(memory_space=pltpu.HBM)
IN_VMEM = pl.BlockSpec(memory_space=pltpu.VMEM)


def iota(shape, dim):
    return lax.broadcasted_iota(jnp.int32, shape, dim)


def bits(mask):
    return mask.astype(F32).astype(BF)


def product(left, right):
    return jnp.dot(left, right, preferred_element_type=F32)


def product_t(left, right):
    return lax.dot_general(left, right, (((1,), (1,)), ((), ())), preferred_element_type=F32)


def before():
    return bits(iota((LANES, LANES), 0) < iota((LANES, LANES), 1))


def fill(choose, dest, begin):
    index = iota((choose.shape[0], LANES), 0) + begin
    for line in range(dest.shape[0]):
        at = slice(line * LANES, (line + 1) * LANES)
        choose[:, at] = bits(index == dest[line : line + 1])


def pack_kernel(
    owners, cid_ref, valid_ref, rows_ref, blocks_ref, code_ref, held, unit, choose, out, in_sems, out_sems
):
    rows, width = held.shape
    total = out.shape[0]
    tile = choose.shape[0]
    lines = rows // LANES
    parts = rows // STEP
    loads = []
    for part in range(parts):
        at = pl.ds(part * STEP, STEP)
        loads.append(pltpu.make_async_copy(rows_ref.at[at], held.at[at], in_sems.at[part]))
        loads[-1].start()

    cid = cid_ref[...]
    live = valid_ref[...] == 1
    owner = lax.shift_right_logical(cid, 3)
    name = (cid & (CL_DEV - 1)) + 1
    target = jnp.where(live, owner, -1)
    index = iota((owners, LANES), 0)
    mine = [(index == target[line : line + 1]).astype(F32) for line in range(lines)]
    stacked = jnp.concatenate(mine, axis=0).astype(BF)
    inside = product(stacked, before())
    whole = product(stacked, jnp.ones((LANES, LANES), BF))
    offset = jnp.zeros((owners, LANES), F32)
    ranks = []
    for line in range(lines):
        at = slice(line * owners, (line + 1) * owners)
        ranks.append(jnp.sum(mine[line] * (inside[at] + offset), axis=0, keepdims=True))
        offset = offset + whole[at]
    pos = jnp.concatenate(ranks, axis=0).astype(jnp.int32)
    fits = live & (pos < SIZE - 1)
    lost = jnp.max((live & (pos >= SIZE - 1)).astype(F32))
    code = jnp.where(fits, pos, LANES - 1)
    code_ref[...] = code
    dest = jnp.where(fits, owner * SIZE + pos, -1)

    names = jnp.concatenate(
        [mine[line] * name[line : line + 1].astype(F32) for line in range(lines)], axis=1
    ).astype(BF)
    index = iota((LANES, LANES), 0)
    places = jnp.concatenate([bits(index == code[line : line + 1]) for line in range(lines)], axis=1)
    meta = product_t(names, places)
    meta = jnp.where(iota((owners, LANES), 1) == LANES - 1, lost, meta).astype(BF)

    fill(choose, dest, 0)
    for part in range(parts):
        loads[part].wait()
        for chunk in range(part * STEP, (part + 1) * STEP, 64):
            values = held[chunk : chunk + 64, :].astype(F32)
            squares = jnp.sum(values * values, axis=1, keepdims=True)
            unit[chunk : chunk + 64, :] = (values * lax.rsqrt(squares + 1e-06)).astype(BF)

    stores = []
    for first in range(0, total, tile):
        if first:
            fill(choose, dest, first)
        for column in range(0, width, STEP):
            at = slice(column, column + STEP)
            packed = product(choose[...], unit[:, at])
            if column == 0:
                line = iota((tile, owners), 0) + first
                last = (iota((1, owners), 1) + 1) * SIZE - 1
                packed = jnp.concatenate(
                    [packed[:, :LANES] + product(bits(line == last), meta), packed[:, LANES:]], axis=1
                )
            out[pl.ds(first, tile), at] = packed.astype(BF)
            where = (pl.ds(first, tile), at)
            stores.append(
                pltpu.make_async_copy(out.at[where], blocks_ref.at[where], out_sems.at[len(stores)])
            )
            stores[-1].start()
    for store in stores:
        store.wait()


def count_before(flags):
    lane = iota(flags.shape, 1)
    counts = flags
    shift = 1
    while shift < LANES:
        counts = counts + jnp.where(lane >= shift, pltpu.roll(counts, shift, 1), 0.0)
        shift *= 2
    whole = jnp.broadcast_to(jnp.sum(flags, axis=1, keepdims=True), flags.shape)
    return counts - flags, whole


def pack_direct(
    owners, cid_ref, valid_ref, rows_ref, blocks_ref, code_ref, held, unit, choose, out, tags, *sems
):
    rows, width = held.shape
    total = out.shape[0]
    lines = rows // LANES
    parts = rows // STEP
    in_sems, out_sems = sems[:parts], sems[parts:]
    loads = []
    for part in range(parts):
        at = pl.ds(part * STEP, STEP)
        loads.append(pltpu.make_async_copy(rows_ref.at[at], held.at[at], in_sems[part]))
        loads[-1].start()

    cid = cid_ref[...]
    live = valid_ref[...] == 1
    owner = lax.shift_right_logical(cid, 3)
    name = (cid & (CL_DEV - 1)) + 1
    target = jnp.where(live, owner, -1)
    index = iota((owners, LANES), 0)
    mine = [(index == target[line : line + 1]).astype(F32) for line in range(lines)]
    inside, whole = count_before(jnp.concatenate(mine, axis=0))
    offset = jnp.zeros((owners, LANES), F32)
    ranks = []
    for line in range(lines):
        at = slice(line * owners, (line + 1) * owners)
        ranks.append(jnp.sum(mine[line] * (inside[at] + offset), axis=0, keepdims=True))
        offset = offset + whole[at]
    pos = jnp.concatenate(ranks, axis=0).astype(jnp.int32)
    fits = live & (pos < SIZE - 1)
    lost = jnp.max((live & (pos >= SIZE - 1)).astype(F32))
    code = jnp.where(fits, pos, LANES - 1)
    code_ref[...] = code
    dest = jnp.where(fits, owner * SIZE + pos, -1)

    def name_rows(acc):
        index = iota((STEP, LANES), 0)
        pieces = STEP // LANES
        for piece in range(lines // pieces):
            here = range(piece * pieces, (piece + 1) * pieces)
            places = [bits(index == code[line : line + 1]) for line in here]
            names = [mine[line] * name[line : line + 1].astype(F32) for line in here]
            pltpu.matmul_push_rhs(jnp.concatenate(places, axis=1), piece % 2, 0, transpose=True)
            pltpu.matmul_acc_lhs(
                acc, jnp.concatenate(names, axis=1).astype(BF), load_staged_rhs=piece % 2
            )
        meta = pltpu.matmul_pop(acc)
        lane = iota((owners, STEP), 1)
        tags[...] = jnp.where(lane < LANES - 1, meta, jnp.where(lane == LANES - 1, lost, 0.0))

    pl.run_scoped(name_rows, pltpu.ACC(mxu_id=0)((owners, STEP), F32))
    fill(choose, dest, 0)

    def scale(part):
        loads[part].wait()
        for chunk in range(part * STEP, (part + 1) * STEP, 64):
            values = held[chunk : chunk + 64, :].astype(F32)
            squares = jnp.sum(values * values, axis=1, keepdims=True)
            unit[chunk : chunk + 64, :] = (values * lax.rsqrt(squares + 1e-06)).astype(BF)

    stores = []

    def multiply(part, number, column, chunks, accs):
        kept = slice(part * STEP, (part + 1) * STEP)
        at = slice(column * STEP, (column + 1) * STEP)
        pltpu.matmul_push_rhs(unit[kept, at], part % 2, number)
        for chunk, (first, count) in enumerate(chunks):
            pltpu.matmul_acc_lhs(
                accs[number][chunk],
                choose[first : first + count, kept],
                load_staged_rhs=part % 2 if chunk == 0 else None,
            )

    def write(column, first, count, packed):
        at = slice(column * STEP, (column + 1) * STEP)
        for row in range(first, first + count, 16):
            piece = packed[row - first : row - first + 16]
            source, place = divmod(row, SIZE)
            if column == 0 and place + 16 == SIZE:
                piece = jnp.where(iota((16, STEP), 0) == 15, tags[...][source : source + 1], piece)
            out[row : row + 16, at] = piece.astype(BF)
        where = (pl.ds(first, count), at)
        stores.append(pltpu.make_async_copy(out.at[where], blocks_ref.at[where], out_sems[len(stores)]))
        stores[-1].start()

    columns = width // STEP
    chunks = [(first, 512) for first in range(0, total - 511, 512)]
    rest = total - 512 * len(chunks)

    def wide(*accs):
        accs = (accs[:2], accs[2:])
        scaled = False
        for first in range(0, len(chunks), 2):
            some = chunks[first : first + 2]
            for column in range(0, columns, 2):
                if not scaled:
                    scale(0)
                for part in range(parts):
                    if not scaled and part + 1 < parts:
                        scale(part + 1)
                    for number in range(2):
                        multiply(part, number, column + number, some, accs)
                scaled = True
                for number in range(2):
                    for chunk, (begin, count) in enumerate(some):
                        write(column + number, begin, count, pltpu.matmul_pop(accs[number][chunk]))

    def narrow(*accs):
        accs = (accs[:2], accs[2:])
        for column in range(0, columns, 2):
            turn = column // 2 % 2
            for part in range(parts):
                for number in range(2):
                    one = ((accs[0][turn],), (accs[1][turn],))
                    multiply(part, number, column + number, [(total - rest, rest)], one)
            for number in range(2):
                write(column + number, total - rest, rest, pltpu.matmul_pop(accs[number][turn]))

    pl.run_scoped(wide, *[pltpu.ACC(mxu_id=number // 2)((512, STEP), F32) for number in range(4)])
    if rest:
        pl.run_scoped(narrow, *[pltpu.ACC(mxu_id=number // 2)((rest, STEP), F32) for number in range(4)])
    for store in stores:
        store.wait()


def pack(embeddings, cluster_id, valid, owners):
    rows, width = embeddings.shape
    total = owners * SIZE
    tile = min(total, TILE)
    lines = (rows // LANES, LANES)
    small = total <= 2048
    return pl.pallas_call(
        functools.partial(pack_direct if small else pack_kernel, owners),
        out_shape=(
            pltpu.HBM((total, width), BF),
            jax.ShapeDtypeStruct(lines, jnp.int32),
        ),
        in_specs=[IN_VMEM, IN_VMEM, ANY],
        out_specs=(ANY, IN_VMEM),
        scratch_shapes=[
            pltpu.VMEM((rows, width), BF),
            pltpu.VMEM((rows, width), BF),
            pltpu.VMEM((tile, rows), BF),
            pltpu.VMEM((total, width), BF),
        ]
        + (
            [pltpu.VMEM((owners, STEP), F32)]
            + [pltpu.SemaphoreType.DMA] * (rows // STEP + (total + 511) // 512 * (width // STEP))
            if small
            else [
                pltpu.SemaphoreType.DMA((rows // STEP,)),
                pltpu.SemaphoreType.DMA((total // tile * (width // STEP),)),
            ]
        ),
        compiler_params=pltpu.CompilerParams(vmem_limit_bytes=52 * MB),
        name="pack",
    )(cluster_id.reshape(lines), valid.reshape(lines), embeddings)


def on_units(size, count, multiply, use):
    def body(*accs):
        for number in range(count + 2):
            if number < count:
                multiply(number, number % 2, accs[number % 4])
            if number >= 2:
                use(number - 2, pltpu.matmul_pop(accs[(number - 2) % 4]))

    pl.run_scoped(body, *[pltpu.ACC(mxu_id=number % 2)((size, STEP), F32) for number in range(4)])


def triangle(total, rows, side, tops, line, across, down):
    width = rows.shape[1]
    blocks = total // STEP
    seen = set()

    def keep(ref, at, value):
        if (id(ref), at) in seen:
            value = jnp.maximum(value, ref[at : at + 8, :])
        seen.add((id(ref), at))
        ref[at : at + 8, :] = value

    work = []
    for column in range(blocks):
        for row in range(column, blocks, 2):
            work.append((column, row, min(2, blocks - row)))

    def run(work, count):
        def multiply(number, unit, acc):
            column, row, _ = work[number]
            for piece in range(width // STEP):
                at = slice(piece * STEP, (piece + 1) * STEP)
                pltpu.matmul_push_rhs(
                    rows[column * STEP : (column + 1) * STEP, at], piece % 2, unit, transpose=True
                )
                pltpu.matmul_acc_lhs(
                    acc, rows[row * STEP : (row + count) * STEP, at], load_staged_rhs=piece % 2
                )

        def use(number, scores):
            column, row, _ = work[number]
            apart = iota((8, LANES), 1) - iota((8, LANES), 0)
            best = [jnp.full((8, LANES), -1.0, F32)] * (STEP // LANES)
            for block in range(0, count * STEP, 8):
                start = row * STEP + block
                found = []
                for part in range(STEP // LANES):
                    first = column * STEP + part * LANES
                    allowed = side[start : start + 8, :] == tops[:, first : first + LANES]
                    if 0 <= start - first < LANES:
                        allowed = allowed & (apart != start - first)
                    here = scores[block : block + 8, part * LANES : (part + 1) * LANES]
                    found.append(jnp.where(allowed, here, -1.0))
                    best[part] = jnp.maximum(best[part], found[part])
                if start // STEP > column:
                    keep(across, start, functools.reduce(jnp.maximum, found))
            for part in range(STEP // LANES):
                keep(down, (column * (STEP // LANES) + part) * 8, best[part])

        on_units(count * STEP, len(work), multiply, use)

    run([item for item in work if item[2] == 2], 2)
    run([item for item in work if item[2] == 1], 1)
    for column in range(blocks):
        for part in range(STEP // LANES):
            first = column * STEP + part * LANES
            at = (column * (STEP // LANES) + part) * 8
            most = jnp.max(down[at : at + 8, :], axis=0, keepdims=True)
            if column:
                turned = across[first : first + LANES, :].T
                most = jnp.maximum(most, jnp.max(turned, axis=0, keepdims=True))
            line[:, first : first + LANES] = most


def score_kernel(owners, got_ref, best_ref, lost_ref, side, line, *more):
    total = line.shape[1]
    rows = got_ref.reshape(total, got_ref.shape[2])

    same = iota((SIZE, LANES), 0) == iota((SIZE, LANES), 1)
    lanes = iota((1, 2 * LANES), 1)
    lost = jnp.zeros((1, LANES), F32)
    line[...] = jnp.zeros((1, total), F32)
    for source in range(owners):
        name = got_ref[source, SIZE - 16 : SIZE, :LANES].astype(F32)[15:16]
        lost = jnp.maximum(lost, name)
        found = jnp.sum(jnp.where(same, name, 0.0), axis=1, keepdims=True)
        side[source * SIZE : (source + 1) * SIZE, :] = jnp.broadcast_to(
            jnp.where(found == 0.0, -1.0, found), (SIZE, LANES)
        )
        base, shift = divmod(source * SIZE, LANES)
        base *= LANES
        name = jnp.where(lanes < SIZE, jnp.concatenate([name, name], axis=1), 0.0)
        if shift:
            name = pltpu.roll(name, shift, 1)
        size = min(2 * LANES, total - base)
        line[:, base : base + size] = line[:, base : base + size] + name[:, :size]
    lost = jnp.max(jnp.where(lanes[:, :LANES] == LANES - 1, lost, 0.0))
    lost_ref[0, 0] = (lost > 0.0).astype(jnp.int32)
    tops = jnp.broadcast_to(line[...], (8, total))
    if total <= 2048:
        triangle(total, rows, side, tops, line, *more)
    else:
        @pl.loop(0, total // STEP)
        def _(number):
            first = pl.multiple_of(number * STEP, STEP)
            here = pl.ds(first, STEP)
            top = jnp.broadcast_to(line[:, here], (8, STEP))
            scores = product_t(rows[...], rows[here, :])
            apart = iota((8, LANES), 1) - iota((8, LANES), 0)
            for part in range(STEP // LANES):
                lanes = slice(part * LANES, (part + 1) * LANES)
                result = jnp.full((8, LANES), -1.0, F32)
                for block in range(0, total, 8):
                    at = slice(block, block + 8)
                    allowed = (side[at, :] == top[:, lanes]) & (apart != block - first - part * LANES)
                    result = jnp.maximum(result, jnp.where(allowed, scores[at, lanes], -1.0))
                line[:, pl.ds(first + part * LANES, LANES)] = jnp.max(result, axis=0, keepdims=True)

    for source in range(owners):
        base, shift = divmod(source * SIZE, LANES)
        base *= LANES
        piece = line[:, base : min(base + 2 * LANES, total)]
        if shift:
            piece = pltpu.roll(piece, piece.shape[1] - shift, 1)
        best_ref[source] = piece[:, :LANES]


def score(got, owners):
    width = got.shape[2]
    total = owners * SIZE
    return pl.pallas_call(
        functools.partial(score_kernel, owners),
        out_shape=(
            pltpu.VMEM((owners, 1, LANES), F32),
            jax.ShapeDtypeStruct((1, 1), jnp.int32),
        ),
        in_specs=[IN_VMEM],
        out_specs=(IN_VMEM, pl.BlockSpec(memory_space=pltpu.SMEM)),
        scratch_shapes=[
            pltpu.VMEM((total, LANES), F32),
            pltpu.VMEM((1, total), F32),
        ]
        + ([] if total > 2048 else [pltpu.VMEM((total, LANES), F32), pltpu.VMEM((total // 16, LANES), F32)]),
        compiler_params=pltpu.CompilerParams(vmem_limit_bytes=48 * MB),
        name="score",
    )(got)


def place_kernel(owners, back_ref, cid_ref, code_ref, valid_ref, out_ref, out, sem):
    for start in range(0, cid_ref.shape[0], 8):
        at = slice(start, start + 8)
        owner = lax.shift_right_logical(cid_ref[at, :], 3)
        code = code_ref[at, :]
        result = jnp.zeros((8, LANES), F32)
        for source in range(owners):
            line = jnp.broadcast_to(back_ref[source], (8, LANES))
            value = jnp.take_along_axis(line, code, axis=1, mode="promise_in_bounds")
            result = jnp.where(owner == source, value, result)
        out[at, :] = jnp.where(valid_ref[at, :] == 1, result, 0.0)
    store = pltpu.make_async_copy(out, out_ref, sem)
    store.start()
    store.wait()


def place(back, cluster_id, code, valid, owners):
    rows = cluster_id.shape[0]
    shape = (rows // LANES, LANES)
    return pl.pallas_call(
        functools.partial(place_kernel, owners),
        out_shape=pltpu.HBM(shape, F32),
        in_specs=[IN_VMEM] * 4,
        out_specs=ANY,
        scratch_shapes=[pltpu.VMEM(shape, F32), pltpu.SemaphoreType.DMA],
        compiler_params=pltpu.CompilerParams(vmem_limit_bytes=4 * MB),
        name="place",
    )(back, cluster_id.reshape(shape), code, valid.reshape(shape)).reshape(rows)


def every_slot(embeddings, cluster_id, valid, owners):
    width = embeddings.shape[1]
    clusters = CL_DEV * owners
    values = embeddings.astype(F32)
    squares = jnp.sum(values * values, axis=1, keepdims=True)
    unit_rows = (values * lax.rsqrt(squares + 1e-06)).astype(BF)
    one_hot = (cluster_id[:, None] == jnp.arange(clusters, dtype=jnp.int32)[None, :]).astype(jnp.int32)
    ranking = jnp.sum(jnp.cumsum(one_hot, axis=0) * one_hot, axis=1) - 1
    target = cluster_id * SLOT + ranking
    outgoing = jnp.zeros((clusters * SLOT, width), BF).at[target].set(unit_rows)
    live_out = jnp.zeros((clusters * SLOT,), BF).at[target].set(valid.astype(BF))
    got = lax.all_to_all(
        outgoing.reshape(owners, CL_DEV * SLOT, width), "owners", split_axis=0, concat_axis=0, tiled=True
    )
    live = lax.all_to_all(
        live_out.reshape(owners, CL_DEV, SLOT), "owners", split_axis=0, concat_axis=0, tiled=True
    )
    got = got.reshape(owners, CL_DEV, SLOT, width).transpose(1, 0, 2, 3)
    got = got.reshape(CL_DEV, owners * SLOT, width)
    live = live.transpose(1, 0, 2).reshape(CL_DEV, owners * SLOT) > 0.5
    diagonal = jnp.eye(owners * SLOT, dtype=bool)

    def one_cluster(args):
        rows, flags = args
        scores = jnp.einsum("md,nd->mn", rows, rows, preferred_element_type=F32)
        allowed = flags[:, None] & flags[None, :] & ~diagonal
        return jnp.max(jnp.where(allowed, scores, -1.0), axis=1)

    best = lax.map(one_cluster, (got, live)).reshape(CL_DEV, owners, SLOT).transpose(1, 0, 2)
    back = lax.all_to_all(best, "owners", split_axis=0, concat_axis=0, tiled=True)
    return jnp.where(valid == 1, back.reshape(-1)[target], 0.0)


def swap(blocks, owners):
    split = blocks.reshape(owners, blocks.shape[0] // owners, blocks.shape[1])
    return lax.all_to_all(split, "owners", split_axis=0, concat_axis=0, tiled=True)


def shards(embeddings, cluster_id, valid):
    owners = lax.axis_size("owners")
    blocks, code = pack(embeddings, cluster_id, valid, owners)
    best, lost = score(swap(blocks, owners), owners)
    back = lax.all_to_all(best, "owners", split_axis=0, concat_axis=0, tiled=True)
    nearest = place(back, cluster_id, code, valid, owners)
    return lax.cond(
        lost[0, 0] > 0,
        lambda: every_slot(embeddings, cluster_id, valid, owners),
        lambda: nearest,
    )


def solution(mesh):
    placed = (P(("groups", "owners"), None), P(("groups", "owners")), P(("groups", "owners")))
    return jax.shard_map(
        shards, mesh=mesh, in_specs=placed, out_specs=P(("groups", "owners")), check_vma=False
    )
```

```python
import functools

import jax
import jax.numpy as jnp
from jax import lax
from jax.experimental import pallas as pl
from jax.experimental.pallas import tpu as pltpu
from jax.sharding import PartitionSpec as P

CL_DEV = 8
SLOT = 16
LANES = 128
SIZE = 80
TILE = 1280
STEP = 256
MB = 1024 * 1024
BF = jnp.bfloat16
F32 = jnp.float32
ANY = pl.BlockSpec(memory_space=pltpu.HBM)
IN_VMEM = pl.BlockSpec(memory_space=pltpu.VMEM)


def iota(shape, dim):
    return lax.broadcasted_iota(jnp.int32, shape, dim)


def bits(mask):
    return mask.astype(F32).astype(BF)


def product(left, right):
    return jnp.dot(left, right, preferred_element_type=F32)


def product_t(left, right):
    return lax.dot_general(left, right, (((1,), (1,)), ((), ())), preferred_element_type=F32)


def before():
    return bits(iota((LANES, LANES), 0) < iota((LANES, LANES), 1))


def fill(choose, dest, begin):
    index = iota((choose.shape[0], LANES), 0) + begin
    for line in range(dest.shape[0]):
        at = slice(line * LANES, (line + 1) * LANES)
        choose[:, at] = bits(index == dest[line : line + 1])


def pack_kernel(
    owners, cid_ref, valid_ref, rows_ref, blocks_ref, code_ref, held, unit, choose, out, in_sems, out_sems
):
    rows, width = held.shape
    total = out.shape[0]
    tile = choose.shape[0]
    lines = rows // LANES
    parts = rows // STEP
    loads = []
    for part in range(parts):
        at = pl.ds(part * STEP, STEP)
        loads.append(pltpu.make_async_copy(rows_ref.at[at], held.at[at], in_sems.at[part]))
        loads[-1].start()

    cid = cid_ref[...]
    live = valid_ref[...] == 1
    owner = lax.shift_right_logical(cid, 3)
    name = (cid & (CL_DEV - 1)) + 1
    target = jnp.where(live, owner, -1)
    index = iota((owners, LANES), 0)
    mine = [(index == target[line : line + 1]).astype(F32) for line in range(lines)]
    stacked = jnp.concatenate(mine, axis=0).astype(BF)
    inside = product(stacked, before())
    whole = product(stacked, jnp.ones((LANES, LANES), BF))
    offset = jnp.zeros((owners, LANES), F32)
    ranks = []
    for line in range(lines):
        at = slice(line * owners, (line + 1) * owners)
        ranks.append(jnp.sum(mine[line] * (inside[at] + offset), axis=0, keepdims=True))
        offset = offset + whole[at]
    pos = jnp.concatenate(ranks, axis=0).astype(jnp.int32)
    fits = live & (pos < SIZE - 1)
    lost = jnp.max((live & (pos >= SIZE - 1)).astype(F32))
    code = jnp.where(fits, pos, LANES - 1)
    code_ref[...] = code
    dest = jnp.where(fits, owner * SIZE + pos, -1)

    names = jnp.concatenate(
        [mine[line] * name[line : line + 1].astype(F32) for line in range(lines)], axis=1
    ).astype(BF)
    index = iota((LANES, LANES), 0)
    places = jnp.concatenate([bits(index == code[line : line + 1]) for line in range(lines)], axis=1)
    meta = product_t(names, places)
    meta = jnp.where(iota((owners, LANES), 1) == LANES - 1, lost, meta).astype(BF)

    fill(choose, dest, 0)
    for part in range(parts):
        loads[part].wait()
        for chunk in range(part * STEP, (part + 1) * STEP, 64):
            values = held[chunk : chunk + 64, :].astype(F32)
            squares = jnp.sum(values * values, axis=1, keepdims=True)
            unit[chunk : chunk + 64, :] = (values * lax.rsqrt(squares + 1e-06)).astype(BF)

    stores = []
    for first in range(0, total, tile):
        if first:
            fill(choose, dest, first)
        for column in range(0, width, STEP):
            at = slice(column, column + STEP)
            packed = product(choose[...], unit[:, at])
            if column == 0:
                line = iota((tile, owners), 0) + first
                last = (iota((1, owners), 1) + 1) * SIZE - 1
                packed = jnp.concatenate(
                    [packed[:, :LANES] + product(bits(line == last), meta), packed[:, LANES:]], axis=1
                )
            out[pl.ds(first, tile), at] = packed.astype(BF)
            where = (pl.ds(first, tile), at)
            stores.append(
                pltpu.make_async_copy(out.at[where], blocks_ref.at[where], out_sems.at[len(stores)])
            )
            stores[-1].start()
    for store in stores:
        store.wait()


def pack_direct(
    owners, cid_ref, valid_ref, rows_ref, blocks_ref, code_ref, held, unit, choose, out, tags, *sems
):
    rows, width = held.shape
    total = out.shape[0]
    lines = rows // LANES
    parts = rows // STEP
    pairs = STEP // LANES
    chunk = 4 * SIZE
    columns = width // STEP
    in_sems, out_sems = sems[:parts], sems[parts:]
    loads = []
    for part in range(parts):
        at = pl.ds(part * STEP, STEP)
        loads.append(pltpu.make_async_copy(rows_ref.at[at], held.at[at], in_sems[part]))
        loads[-1].start()
    stores = []

    def body(count_acc, tag_acc, *accs):
        cid = cid_ref[...]
        live = valid_ref[...] == 1
        owner = lax.shift_right_logical(cid, 3)
        name = (cid & (CL_DEV - 1)) + 1
        target = jnp.where(live, owner, -1)
        index = iota((owners, LANES), 0)
        mine = [(index == target[line : line + 1]).astype(F32) for line in range(lines)]
        mine = [jnp.concatenate(mine[i : i + pairs], axis=1) for i in range(0, lines, pairs)]
        stacked = jnp.concatenate(mine, axis=0)
        pltpu.matmul_push_rhs(bits(iota((STEP, STEP), 0) < iota((STEP, STEP), 1)), 0, 0)
        pltpu.matmul_acc_lhs(count_acc, stacked.astype(BF), load_staged_rhs=0)
        whole = jnp.sum(stacked, axis=1, keepdims=True)
        inside = pltpu.matmul_pop(count_acc)
        offset = jnp.zeros((owners, 1), F32)
        ranks = []
        for part in range(parts):
            at = slice(part * owners, (part + 1) * owners)
            rank = jnp.sum(mine[part] * (inside[at] + offset), axis=0, keepdims=True)
            ranks += [rank[:, i * LANES : (i + 1) * LANES] for i in range(pairs)]
            offset = offset + whole[at]
        pos = jnp.concatenate(ranks, axis=0).astype(jnp.int32)
        fits = live & (pos < SIZE - 1)
        lost = jnp.max((live & (pos >= SIZE - 1)).astype(F32))
        code = jnp.where(fits, pos, LANES - 1)
        code_ref[...] = code
        dest = jnp.where(fits, owner * SIZE + pos, -1)

        def prepare(part):
            loads[part].wait()
            for begin in range(part * STEP, (part + 1) * STEP, 64):
                values = held[begin : begin + 64, :].astype(F32)
                squares = jnp.sum(values * values, axis=1, keepdims=True)
                unit[begin : begin + 64, :] = (values * lax.rsqrt(squares + 1e-06)).astype(BF)
            index = iota((total, LANES), 0)
            for line in range(part * pairs, (part + 1) * pairs):
                at = slice(line * LANES, (line + 1) * LANES)
                choose[:, at] = bits(index == dest[line : line + 1])

        def multiply(part, number, column, chunks):
            kept = slice(part * STEP, (part + 1) * STEP)
            at = slice(column * STEP, (column + 1) * STEP)
            pltpu.matmul_push_rhs(unit[kept, at], part % 2, number)
            first = True
            for place, slot in chunks:
                pltpu.matmul_acc_lhs(
                    accs[number * 3 + slot],
                    choose[place * chunk : (place + 1) * chunk, kept],
                    load_staged_rhs=part % 2 if first else None,
                )
                first = False

        def write(number, column, place, slot):
            packed = pltpu.matmul_pop(accs[number * 3 + slot])
            at = slice(column * STEP, (column + 1) * STEP)
            first = place * chunk
            for row in range(first, first + chunk, 16):
                piece = packed[row - first : row - first + 16]
                source, spot = divmod(row, SIZE)
                if column == 0 and spot + 16 == SIZE:
                    piece = jnp.where(iota((16, STEP), 0) == 15, tags[...][source : source + 1], piece)
                out[row : row + 16, at] = piece.astype(BF)
            where = (pl.ds(first, chunk), at)
            stores.append(
                pltpu.make_async_copy(out.at[where], blocks_ref.at[where], out_sems[len(stores)])
            )
            stores[-1].start()

        opening = [(place, place) for place in range(3)]
        for part in range(parts):
            prepare(part)
            if part:
                for number in range(2):
                    multiply(part - 1, number, number, opening)
        for number in range(2):
            multiply(parts - 1, number, number, opening)

        index = iota((STEP, LANES), 0)
        for part in range(parts):
            here = range(part * pairs, (part + 1) * pairs)
            places = [bits(index == code[line : line + 1]) for line in here]
            named = [name[line : line + 1].astype(F32) for line in here]
            pltpu.matmul_push_rhs(jnp.concatenate(places, axis=1), part % 2, 1, transpose=True)
            pltpu.matmul_acc_lhs(
                tag_acc,
                (mine[part] * jnp.concatenate(named, axis=1)).astype(BF),
                load_staged_rhs=part % 2,
            )
        lane = iota((owners, STEP), 1)
        tags[...] = jnp.where(
            lane < LANES - 1, pltpu.matmul_pop(tag_acc), jnp.where(lane == LANES - 1, lost, 0.0)
        )

        done = [(0, place) for place in range(3)]
        left = [(0, place) for place in range(3, total // chunk)]
        for column in range(2, columns, 2):
            left += [(column, place) for place in range(total // chunk)]
        for turn, (column, place) in enumerate(left):
            before = done[turn]
            for number in range(2):
                write(number, before[0] + number, before[1], turn % 3)
            for part in range(parts):
                for number in range(2):
                    multiply(part, number, column + number, [(place, turn % 3)])
            done.append((column, place))
        for turn in range(len(left), len(done)):
            for number in range(2):
                write(number, done[turn][0] + number, done[turn][1], turn % 3)

    pl.run_scoped(
        body,
        pltpu.ACC(mxu_id=0)((parts * owners, STEP), F32),
        pltpu.ACC(mxu_id=1)((owners, STEP), F32),
        *[pltpu.ACC(mxu_id=number // 3)((chunk, STEP), F32) for number in range(6)],
    )
    for store in stores:
        store.wait()


def pack(embeddings, cluster_id, valid, owners):
    rows, width = embeddings.shape
    total = owners * SIZE
    tile = min(total, TILE)
    lines = (rows // LANES, LANES)
    small = total <= 2048
    return pl.pallas_call(
        functools.partial(pack_direct if small else pack_kernel, owners),
        out_shape=(
            pltpu.HBM((total, width), BF),
            jax.ShapeDtypeStruct(lines, jnp.int32),
        ),
        in_specs=[IN_VMEM, IN_VMEM, ANY],
        out_specs=(ANY, IN_VMEM),
        scratch_shapes=[
            pltpu.VMEM((rows, width), BF),
            pltpu.VMEM((rows, width), BF),
            pltpu.VMEM((tile, rows), BF),
            pltpu.VMEM((total, width), BF),
        ]
        + (
            [pltpu.VMEM((owners, STEP), F32)]
            + [pltpu.SemaphoreType.DMA] * (rows // STEP + owners // 4 * (width // STEP))
            if small
            else [
                pltpu.SemaphoreType.DMA((rows // STEP,)),
                pltpu.SemaphoreType.DMA((total // tile * (width // STEP),)),
            ]
        ),
        compiler_params=pltpu.CompilerParams(vmem_limit_bytes=52 * MB),
        name="pack",
    )(cluster_id.reshape(lines), valid.reshape(lines), embeddings)


def on_units(size, count, multiply, use):
    def body(*accs):
        for number in range(count + 2):
            if number < count:
                multiply(number, number % 2, accs[number % 4])
            if number >= 2:
                use(number - 2, pltpu.matmul_pop(accs[(number - 2) % 4]))

    pl.run_scoped(body, *[pltpu.ACC(mxu_id=number % 2)((size, STEP), F32) for number in range(4)])


def triangle(total, rows, side, tops, line, across, down):
    width = rows.shape[1]
    blocks = total // STEP
    seen = set()

    def keep(ref, at, value):
        if (id(ref), at) in seen:
            value = jnp.maximum(value, ref[at : at + 8, :])
        seen.add((id(ref), at))
        ref[at : at + 8, :] = value

    work = []
    for column in range(blocks):
        for row in range(column, blocks, 2):
            work.append((column, row, min(2, blocks - row)))

    def run(work, count):
        def multiply(number, unit, acc):
            column, row, _ = work[number]
            for piece in range(width // STEP):
                at = slice(piece * STEP, (piece + 1) * STEP)
                pltpu.matmul_push_rhs(
                    rows[column * STEP : (column + 1) * STEP, at], piece % 2, unit, transpose=True
                )
                pltpu.matmul_acc_lhs(
                    acc, rows[row * STEP : (row + count) * STEP, at], load_staged_rhs=piece % 2
                )

        def use(number, scores):
            column, row, _ = work[number]
            apart = iota((8, LANES), 1) - iota((8, LANES), 0)
            best = [jnp.full((8, LANES), -1.0, F32)] * (STEP // LANES)
            for block in range(0, count * STEP, 8):
                start = row * STEP + block
                found = []
                for part in range(STEP // LANES):
                    first = column * STEP + part * LANES
                    allowed = side[start : start + 8, :] == tops[:, first : first + LANES]
                    if 0 <= start - first < LANES:
                        allowed = allowed & (apart != start - first)
                    here = scores[block : block + 8, part * LANES : (part + 1) * LANES]
                    found.append(jnp.where(allowed, here, -1.0))
                    best[part] = jnp.maximum(best[part], found[part])
                if start // STEP > column:
                    keep(across, start, functools.reduce(jnp.maximum, found))
            for part in range(STEP // LANES):
                keep(down, (column * (STEP // LANES) + part) * 8, best[part])

        on_units(count * STEP, len(work), multiply, use)

    run([item for item in work if item[2] == 2], 2)
    run([item for item in work if item[2] == 1], 1)
    for column in range(blocks):
        for part in range(STEP // LANES):
            first = column * STEP + part * LANES
            at = (column * (STEP // LANES) + part) * 8
            most = jnp.max(down[at : at + 8, :], axis=0, keepdims=True)
            if column:
                turned = across[first : first + LANES, :].T
                most = jnp.maximum(most, jnp.max(turned, axis=0, keepdims=True))
            line[:, first : first + LANES] = most


def score_kernel(owners, got_ref, best_ref, lost_ref, side, line, *more):
    total = line.shape[1]
    rows = got_ref.reshape(total, got_ref.shape[2])

    same = iota((SIZE, LANES), 0) == iota((SIZE, LANES), 1)
    lanes = iota((1, 2 * LANES), 1)
    lost = jnp.zeros((1, LANES), F32)
    line[...] = jnp.zeros((1, total), F32)
    for source in range(owners):
        name = got_ref[source, SIZE - 16 : SIZE, :LANES].astype(F32)[15:16]
        lost = jnp.maximum(lost, name)
        found = jnp.sum(jnp.where(same, name, 0.0), axis=1, keepdims=True)
        side[source * SIZE : (source + 1) * SIZE, :] = jnp.broadcast_to(
            jnp.where(found == 0.0, -1.0, found), (SIZE, LANES)
        )
        base, shift = divmod(source * SIZE, LANES)
        base *= LANES
        name = jnp.where(lanes < SIZE, jnp.concatenate([name, name], axis=1), 0.0)
        if shift:
            name = pltpu.roll(name, shift, 1)
        size = min(2 * LANES, total - base)
        line[:, base : base + size] = line[:, base : base + size] + name[:, :size]
    lost = jnp.max(jnp.where(lanes[:, :LANES] == LANES - 1, lost, 0.0))
    lost_ref[0, 0] = (lost > 0.0).astype(jnp.int32)
    tops = jnp.broadcast_to(line[...], (8, total))
    if total <= 2048:
        triangle(total, rows, side, tops, line, *more)
    else:
        @pl.loop(0, total // STEP)
        def _(number):
            first = pl.multiple_of(number * STEP, STEP)
            here = pl.ds(first, STEP)
            top = jnp.broadcast_to(line[:, here], (8, STEP))
            scores = product_t(rows[...], rows[here, :])
            apart = iota((8, LANES), 1) - iota((8, LANES), 0)
            for part in range(STEP // LANES):
                lanes = slice(part * LANES, (part + 1) * LANES)
                result = jnp.full((8, LANES), -1.0, F32)
                for block in range(0, total, 8):
                    at = slice(block, block + 8)
                    allowed = (side[at, :] == top[:, lanes]) & (apart != block - first - part * LANES)
                    result = jnp.maximum(result, jnp.where(allowed, scores[at, lanes], -1.0))
                line[:, pl.ds(first + part * LANES, LANES)] = jnp.max(result, axis=0, keepdims=True)

    for source in range(owners):
        base, shift = divmod(source * SIZE, LANES)
        base *= LANES
        piece = line[:, base : min(base + 2 * LANES, total)]
        if shift:
            piece = pltpu.roll(piece, piece.shape[1] - shift, 1)
        best_ref[source] = piece[:, :LANES]


def score(got, owners):
    width = got.shape[2]
    total = owners * SIZE
    return pl.pallas_call(
        functools.partial(score_kernel, owners),
        out_shape=(
            pltpu.VMEM((owners, 1, LANES), F32),
            jax.ShapeDtypeStruct((1, 1), jnp.int32),
        ),
        in_specs=[IN_VMEM],
        out_specs=(IN_VMEM, pl.BlockSpec(memory_space=pltpu.SMEM)),
        scratch_shapes=[
            pltpu.VMEM((total, LANES), F32),
            pltpu.VMEM((1, total), F32),
        ]
        + ([] if total > 2048 else [pltpu.VMEM((total, LANES), F32), pltpu.VMEM((total // 16, LANES), F32)]),
        compiler_params=pltpu.CompilerParams(vmem_limit_bytes=48 * MB),
        name="score",
    )(got)


def place_kernel(owners, back_ref, cid_ref, code_ref, valid_ref, out_ref, out, sem):
    for start in range(0, cid_ref.shape[0], 8):
        at = slice(start, start + 8)
        owner = lax.shift_right_logical(cid_ref[at, :], 3)
        code = code_ref[at, :]
        result = jnp.zeros((8, LANES), F32)
        for source in range(owners):
            line = jnp.broadcast_to(back_ref[source], (8, LANES))
            value = jnp.take_along_axis(line, code, axis=1, mode="promise_in_bounds")
            result = jnp.where(owner == source, value, result)
        out[at, :] = jnp.where(valid_ref[at, :] == 1, result, 0.0)
    store = pltpu.make_async_copy(out, out_ref, sem)
    store.start()
    store.wait()


def place(back, cluster_id, code, valid, owners):
    rows = cluster_id.shape[0]
    shape = (rows // LANES, LANES)
    return pl.pallas_call(
        functools.partial(place_kernel, owners),
        out_shape=pltpu.HBM(shape, F32),
        in_specs=[IN_VMEM] * 4,
        out_specs=ANY,
        scratch_shapes=[pltpu.VMEM(shape, F32), pltpu.SemaphoreType.DMA],
        compiler_params=pltpu.CompilerParams(vmem_limit_bytes=4 * MB),
        name="place",
    )(back, cluster_id.reshape(shape), code, valid.reshape(shape)).reshape(rows)


def every_slot(embeddings, cluster_id, valid, owners):
    width = embeddings.shape[1]
    clusters = CL_DEV * owners
    values = embeddings.astype(F32)
    squares = jnp.sum(values * values, axis=1, keepdims=True)
    unit_rows = (values * lax.rsqrt(squares + 1e-06)).astype(BF)
    one_hot = (cluster_id[:, None] == jnp.arange(clusters, dtype=jnp.int32)[None, :]).astype(jnp.int32)
    ranking = jnp.sum(jnp.cumsum(one_hot, axis=0) * one_hot, axis=1) - 1
    target = cluster_id * SLOT + ranking
    outgoing = jnp.zeros((clusters * SLOT, width), BF).at[target].set(unit_rows)
    live_out = jnp.zeros((clusters * SLOT,), BF).at[target].set(valid.astype(BF))
    got = lax.all_to_all(
        outgoing.reshape(owners, CL_DEV * SLOT, width), "owners", split_axis=0, concat_axis=0, tiled=True
    )
    live = lax.all_to_all(
        live_out.reshape(owners, CL_DEV, SLOT), "owners", split_axis=0, concat_axis=0, tiled=True
    )
    got = got.reshape(owners, CL_DEV, SLOT, width).transpose(1, 0, 2, 3)
    got = got.reshape(CL_DEV, owners * SLOT, width)
    live = live.transpose(1, 0, 2).reshape(CL_DEV, owners * SLOT) > 0.5
    diagonal = jnp.eye(owners * SLOT, dtype=bool)

    def one_cluster(args):
        rows, flags = args
        scores = jnp.einsum("md,nd->mn", rows, rows, preferred_element_type=F32)
        allowed = flags[:, None] & flags[None, :] & ~diagonal
        return jnp.max(jnp.where(allowed, scores, -1.0), axis=1)

    best = lax.map(one_cluster, (got, live)).reshape(CL_DEV, owners, SLOT).transpose(1, 0, 2)
    back = lax.all_to_all(best, "owners", split_axis=0, concat_axis=0, tiled=True)
    return jnp.where(valid == 1, back.reshape(-1)[target], 0.0)


def swap(blocks, owners):
    split = blocks.reshape(owners, blocks.shape[0] // owners, blocks.shape[1])
    return lax.all_to_all(split, "owners", split_axis=0, concat_axis=0, tiled=True)


def shards(embeddings, cluster_id, valid):
    owners = lax.axis_size("owners")
    blocks, code = pack(embeddings, cluster_id, valid, owners)
    best, lost = score(swap(blocks, owners), owners)
    back = lax.all_to_all(best, "owners", split_axis=0, concat_axis=0, tiled=True)
    nearest = place(back, cluster_id, code, valid, owners)
    return lax.cond(
        lost[0, 0] > 0,
        lambda: every_slot(embeddings, cluster_id, valid, owners),
        lambda: nearest,
    )


def solution(mesh):
    placed = (P(("groups", "owners"), None), P(("groups", "owners")), P(("groups", "owners")))
    return jax.shard_map(
        shards, mesh=mesh, in_specs=placed, out_specs=P(("groups", "owners")), check_vma=False
    )
```

```python
import functools

import jax
import jax.numpy as jnp
from jax import lax
from jax.experimental import pallas as pl
from jax.experimental.pallas import tpu as pltpu
from jax.sharding import PartitionSpec as P

CL_DEV = 8
SLOT = 16
LANES = 128
SIZE = 80
TILE = 1280
STEP = 256
MB = 1024 * 1024
BF = jnp.bfloat16
F32 = jnp.float32
ANY = pl.BlockSpec(memory_space=pltpu.HBM)
IN_VMEM = pl.BlockSpec(memory_space=pltpu.VMEM)


def iota(shape, dim):
    return lax.broadcasted_iota(jnp.int32, shape, dim)


def bits(mask):
    return mask.astype(F32).astype(BF)


def product(left, right):
    return jnp.dot(left, right, preferred_element_type=F32)


def product_t(left, right):
    return lax.dot_general(left, right, (((1,), (1,)), ((), ())), preferred_element_type=F32)


def before():
    return bits(iota((LANES, LANES), 0) < iota((LANES, LANES), 1))


def fill(choose, dest, begin):
    index = iota((choose.shape[0], LANES), 0) + begin
    for line in range(dest.shape[0]):
        at = slice(line * LANES, (line + 1) * LANES)
        choose[:, at] = bits(index == dest[line : line + 1])


def pack_kernel(
    owners, cid_ref, valid_ref, rows_ref, blocks_ref, code_ref, held, unit, choose, out, in_sems, out_sems
):
    rows, width = held.shape
    total = out.shape[0]
    tile = choose.shape[0]
    lines = rows // LANES
    parts = rows // STEP
    loads = []
    for part in range(parts):
        at = pl.ds(part * STEP, STEP)
        loads.append(pltpu.make_async_copy(rows_ref.at[at], held.at[at], in_sems.at[part]))
        loads[-1].start()

    cid = cid_ref[...]
    live = valid_ref[...] == 1
    owner = lax.shift_right_logical(cid, 3)
    name = (cid & (CL_DEV - 1)) + 1
    target = jnp.where(live, owner, -1)
    index = iota((owners, LANES), 0)
    mine = [(index == target[line : line + 1]).astype(F32) for line in range(lines)]
    stacked = jnp.concatenate(mine, axis=0).astype(BF)
    inside = product(stacked, before())
    whole = product(stacked, jnp.ones((LANES, LANES), BF))
    offset = jnp.zeros((owners, LANES), F32)
    ranks = []
    for line in range(lines):
        at = slice(line * owners, (line + 1) * owners)
        ranks.append(jnp.sum(mine[line] * (inside[at] + offset), axis=0, keepdims=True))
        offset = offset + whole[at]
    pos = jnp.concatenate(ranks, axis=0).astype(jnp.int32)
    fits = live & (pos < SIZE - 1)
    lost = jnp.max((live & (pos >= SIZE - 1)).astype(F32))
    code = jnp.where(fits, pos, LANES - 1)
    code_ref[...] = code
    dest = jnp.where(fits, owner * SIZE + pos, -1)

    names = jnp.concatenate(
        [mine[line] * name[line : line + 1].astype(F32) for line in range(lines)], axis=1
    ).astype(BF)
    index = iota((LANES, LANES), 0)
    places = jnp.concatenate([bits(index == code[line : line + 1]) for line in range(lines)], axis=1)
    meta = product_t(names, places)
    meta = jnp.where(iota((owners, LANES), 1) == LANES - 1, lost, meta).astype(BF)

    fill(choose, dest, 0)
    for part in range(parts):
        loads[part].wait()
        for chunk in range(part * STEP, (part + 1) * STEP, 64):
            values = held[chunk : chunk + 64, :].astype(F32)
            squares = jnp.sum(values * values, axis=1, keepdims=True)
            unit[chunk : chunk + 64, :] = (values * lax.rsqrt(squares + 1e-06)).astype(BF)

    stores = []
    for first in range(0, total, tile):
        if first:
            fill(choose, dest, first)
        for column in range(0, width, STEP):
            at = slice(column, column + STEP)
            packed = product(choose[...], unit[:, at])
            if column == 0:
                line = iota((tile, owners), 0) + first
                last = (iota((1, owners), 1) + 1) * SIZE - 1
                packed = jnp.concatenate(
                    [packed[:, :LANES] + product(bits(line == last), meta), packed[:, LANES:]], axis=1
                )
            out[pl.ds(first, tile), at] = packed.astype(BF)
            where = (pl.ds(first, tile), at)
            stores.append(
                pltpu.make_async_copy(out.at[where], blocks_ref.at[where], out_sems.at[len(stores)])
            )
            stores[-1].start()
    for store in stores:
        store.wait()


def pack_direct(
    owners, cid_ref, valid_ref, rows_ref, blocks_ref, code_ref, held, unit, choose, out, tags, *sems
):
    rows, width = held.shape
    total = out.shape[0]
    lines = rows // LANES
    parts = rows // STEP
    pairs = STEP // LANES
    chunk = 4 * SIZE
    columns = width // STEP
    in_sems, out_sems = sems[:parts], sems[parts:]
    loads = []
    for part in range(parts):
        at = pl.ds(part * STEP, STEP)
        loads.append(pltpu.make_async_copy(rows_ref.at[at], held.at[at], in_sems[part]))
        loads[-1].start()
    stores = []

    def body(count_acc, tag_acc, *accs):
        cid = cid_ref[...]
        live = valid_ref[...] == 1
        owner = lax.shift_right_logical(cid, 3)
        name = (cid & (CL_DEV - 1)) + 1
        target = jnp.where(live, owner, -1)
        index = iota((owners, LANES), 0)
        mine = [(index == target[line : line + 1]).astype(F32) for line in range(lines)]
        mine = [jnp.concatenate(mine[i : i + pairs], axis=1) for i in range(0, lines, pairs)]
        stacked = jnp.concatenate(mine, axis=0)
        pltpu.matmul_push_rhs(bits(iota((STEP, STEP), 0) < iota((STEP, STEP), 1)), 0, 0)
        pltpu.matmul_acc_lhs(count_acc, stacked.astype(BF), load_staged_rhs=0)
        whole = jnp.sum(stacked, axis=1, keepdims=True)
        inside = pltpu.matmul_pop(count_acc)
        offset = jnp.zeros((owners, 1), F32)
        ranks = []
        for part in range(parts):
            at = slice(part * owners, (part + 1) * owners)
            rank = jnp.sum(mine[part] * (inside[at] + offset), axis=0, keepdims=True)
            ranks += [rank[:, i * LANES : (i + 1) * LANES] for i in range(pairs)]
            offset = offset + whole[at]
        pos = jnp.concatenate(ranks, axis=0).astype(jnp.int32)
        fits = live & (pos < SIZE - 1)
        lost = jnp.max((live & (pos >= SIZE - 1)).astype(F32))
        code = jnp.where(fits, pos, LANES - 1)
        code_ref[...] = code
        dest = jnp.where(fits, owner * SIZE + pos, -1)

        def prepare(part):
            loads[part].wait()
            for begin in range(part * STEP, (part + 1) * STEP, 16):
                values = held[begin : begin + 16, :].astype(F32)
                squares = jnp.sum(values * values, axis=1, keepdims=True)
                unit[begin : begin + 16, :] = (values * lax.rsqrt(squares + 1e-06)).astype(BF)
            index = iota((total, LANES), 0)
            for line in range(part * pairs, (part + 1) * pairs):
                at = slice(line * LANES, (line + 1) * LANES)
                choose[:, at] = bits(index == dest[line : line + 1])

        def multiply(part, number, column, chunks):
            kept = slice(part * STEP, (part + 1) * STEP)
            at = slice(column * STEP, (column + 1) * STEP)
            pltpu.matmul_push_rhs(unit[kept, at], part % 2, number)
            first = True
            for place, slot in chunks:
                pltpu.matmul_acc_lhs(
                    accs[number * 3 + slot],
                    choose[place * chunk : (place + 1) * chunk, kept],
                    load_staged_rhs=part % 2 if first else None,
                )
                first = False

        def write(number, column, place, slot):
            packed = pltpu.matmul_pop(accs[number * 3 + slot])
            at = slice(column * STEP, (column + 1) * STEP)
            first = place * chunk
            for row in range(first, first + chunk, 16):
                piece = packed[row - first : row - first + 16]
                source, spot = divmod(row, SIZE)
                if column == 0 and spot + 16 == SIZE:
                    piece = jnp.where(iota((16, STEP), 0) == 15, tags[...][source : source + 1], piece)
                out[row : row + 16, at] = piece.astype(BF)
            where = (pl.ds(first, chunk), at)
            stores.append(
                pltpu.make_async_copy(out.at[where], blocks_ref.at[where], out_sems[len(stores)])
            )
            stores[-1].start()

        opening = [(place, place) for place in range(3)]
        for part in range(parts):
            prepare(part)
            if part:
                for number in range(2):
                    multiply(part - 1, number, number, opening)
        for number in range(2):
            multiply(parts - 1, number, number, opening)

        index = iota((STEP, LANES), 0)
        for part in range(parts):
            here = range(part * pairs, (part + 1) * pairs)
            places = [bits(index == code[line : line + 1]) for line in here]
            named = [name[line : line + 1].astype(F32) for line in here]
            pltpu.matmul_push_rhs(jnp.concatenate(places, axis=1), part % 2, 1, transpose=True)
            pltpu.matmul_acc_lhs(
                tag_acc,
                (mine[part] * jnp.concatenate(named, axis=1)).astype(BF),
                load_staged_rhs=part % 2,
            )
        lane = iota((owners, STEP), 1)
        tags[...] = jnp.where(
            lane < LANES - 1, pltpu.matmul_pop(tag_acc), jnp.where(lane == LANES - 1, lost, 0.0)
        )

        done = [(0, place) for place in range(3)]
        left = [(0, place) for place in range(3, total // chunk)]
        for column in range(2, columns, 2):
            left += [(column, place) for place in range(total // chunk)]
        for turn, (column, place) in enumerate(left):
            before = done[turn]
            for number in range(2):
                write(number, before[0] + number, before[1], turn % 3)
            for part in range(parts):
                for number in range(2):
                    multiply(part, number, column + number, [(place, turn % 3)])
            done.append((column, place))
        for turn in range(len(left), len(done)):
            for number in range(2):
                write(number, done[turn][0] + number, done[turn][1], turn % 3)

    pl.run_scoped(
        body,
        pltpu.ACC(mxu_id=0)((parts * owners, STEP), F32),
        pltpu.ACC(mxu_id=1)((owners, STEP), F32),
        *[pltpu.ACC(mxu_id=number // 3)((chunk, STEP), F32) for number in range(6)],
    )
    for store in stores:
        store.wait()


def pack(embeddings, cluster_id, valid, owners):
    rows, width = embeddings.shape
    total = owners * SIZE
    tile = min(total, TILE)
    lines = (rows // LANES, LANES)
    small = total <= 2048
    return pl.pallas_call(
        functools.partial(pack_direct if small else pack_kernel, owners),
        out_shape=(
            pltpu.HBM((total, width), BF),
            jax.ShapeDtypeStruct(lines, jnp.int32),
        ),
        in_specs=[IN_VMEM, IN_VMEM, ANY],
        out_specs=(ANY, IN_VMEM),
        scratch_shapes=[
            pltpu.VMEM((rows, width), BF),
            pltpu.VMEM((rows, width), BF),
            pltpu.VMEM((tile, rows), BF),
            pltpu.VMEM((total, width), BF),
        ]
        + (
            [pltpu.VMEM((owners, STEP), F32)]
            + [pltpu.SemaphoreType.DMA] * (rows // STEP + owners // 4 * (width // STEP))
            if small
            else [
                pltpu.SemaphoreType.DMA((rows // STEP,)),
                pltpu.SemaphoreType.DMA((total // tile * (width // STEP),)),
            ]
        ),
        compiler_params=pltpu.CompilerParams(vmem_limit_bytes=52 * MB),
        name="pack",
    )(cluster_id.reshape(lines), valid.reshape(lines), embeddings)


def on_units(size, count, multiply, use):
    def body(*accs):
        for number in range(count + 2):
            if number < count:
                multiply(number, number % 2, accs[number % 4])
            if number >= 2:
                use(number - 2, pltpu.matmul_pop(accs[(number - 2) % 4]))

    pl.run_scoped(body, *[pltpu.ACC(mxu_id=number % 2)((size, STEP), F32) for number in range(4)])


def triangle(total, rows, side, tops, line, across, down):
    width = rows.shape[1]
    blocks = total // STEP
    seen = set()

    def keep(ref, at, value):
        if (id(ref), at) in seen:
            value = jnp.maximum(value, ref[at : at + 8, :])
        seen.add((id(ref), at))
        ref[at : at + 8, :] = value

    work = []
    for column in range(blocks):
        for row in range(column, blocks, 2):
            work.append((column, row, min(2, blocks - row)))

    def run(work, count):
        def multiply(number, unit, acc):
            column, row, _ = work[number]
            for piece in range(width // STEP):
                at = slice(piece * STEP, (piece + 1) * STEP)
                pltpu.matmul_push_rhs(
                    rows[column * STEP : (column + 1) * STEP, at], piece % 2, unit, transpose=True
                )
                pltpu.matmul_acc_lhs(
                    acc, rows[row * STEP : (row + count) * STEP, at], load_staged_rhs=piece % 2
                )

        def use(number, scores):
            column, row, _ = work[number]
            apart = iota((8, LANES), 1) - iota((8, LANES), 0)
            best = [jnp.full((8, LANES), -1.0, F32)] * (STEP // LANES)
            for block in range(0, count * STEP, 8):
                start = row * STEP + block
                found = []
                for part in range(STEP // LANES):
                    first = column * STEP + part * LANES
                    allowed = side[start : start + 8, :] == tops[:, first : first + LANES]
                    if 0 <= start - first < LANES:
                        allowed = allowed & (apart != start - first)
                    here = scores[block : block + 8, part * LANES : (part + 1) * LANES]
                    found.append(jnp.where(allowed, here, -1.0))
                    best[part] = jnp.maximum(best[part], found[part])
                if start // STEP > column:
                    keep(across, start, functools.reduce(jnp.maximum, found))
            for part in range(STEP // LANES):
                keep(down, (column * (STEP // LANES) + part) * 8, best[part])

        on_units(count * STEP, len(work), multiply, use)

    run([item for item in work if item[2] == 2], 2)
    run([item for item in work if item[2] == 1], 1)
    for column in range(blocks):
        for part in range(STEP // LANES):
            first = column * STEP + part * LANES
            at = (column * (STEP // LANES) + part) * 8
            most = jnp.max(down[at : at + 8, :], axis=0, keepdims=True)
            if column:
                turned = across[first : first + LANES, :].T
                most = jnp.maximum(most, jnp.max(turned, axis=0, keepdims=True))
            line[:, first : first + LANES] = most


def score_kernel(owners, got_ref, best_ref, lost_ref, side, line, *more):
    total = line.shape[1]
    rows = got_ref.reshape(total, got_ref.shape[2])

    same = iota((SIZE, LANES), 0) == iota((SIZE, LANES), 1)
    lanes = iota((1, 2 * LANES), 1)
    lost = jnp.zeros((1, LANES), F32)
    line[...] = jnp.zeros((1, total), F32)
    for source in range(owners):
        name = got_ref[source, SIZE - 16 : SIZE, :LANES].astype(F32)[15:16]
        lost = jnp.maximum(lost, name)
        found = jnp.sum(jnp.where(same, name, 0.0), axis=1, keepdims=True)
        side[source * SIZE : (source + 1) * SIZE, :] = jnp.broadcast_to(
            jnp.where(found == 0.0, -1.0, found), (SIZE, LANES)
        )
        base, shift = divmod(source * SIZE, LANES)
        base *= LANES
        name = jnp.where(lanes < SIZE, jnp.concatenate([name, name], axis=1), 0.0)
        if shift:
            name = pltpu.roll(name, shift, 1)
        size = min(2 * LANES, total - base)
        line[:, base : base + size] = line[:, base : base + size] + name[:, :size]
    lost = jnp.max(jnp.where(lanes[:, :LANES] == LANES - 1, lost, 0.0))
    lost_ref[0, 0] = (lost > 0.0).astype(jnp.int32)
    tops = jnp.broadcast_to(line[...], (8, total))
    if total <= 2048:
        triangle(total, rows, side, tops, line, *more)
    else:
        @pl.loop(0, total // STEP)
        def _(number):
            first = pl.multiple_of(number * STEP, STEP)
            here = pl.ds(first, STEP)
            top = jnp.broadcast_to(line[:, here], (8, STEP))
            scores = product_t(rows[...], rows[here, :])
            apart = iota((8, LANES), 1) - iota((8, LANES), 0)
            for part in range(STEP // LANES):
                lanes = slice(part * LANES, (part + 1) * LANES)
                result = jnp.full((8, LANES), -1.0, F32)
                for block in range(0, total, 8):
                    at = slice(block, block + 8)
                    allowed = (side[at, :] == top[:, lanes]) & (apart != block - first - part * LANES)
                    result = jnp.maximum(result, jnp.where(allowed, scores[at, lanes], -1.0))
                line[:, pl.ds(first + part * LANES, LANES)] = jnp.max(result, axis=0, keepdims=True)

    for source in range(owners):
        base, shift = divmod(source * SIZE, LANES)
        base *= LANES
        piece = line[:, base : min(base + 2 * LANES, total)]
        if shift:
            piece = pltpu.roll(piece, piece.shape[1] - shift, 1)
        best_ref[source] = piece[:, :LANES]


def score(got, owners):
    width = got.shape[2]
    total = owners * SIZE
    return pl.pallas_call(
        functools.partial(score_kernel, owners),
        out_shape=(
            pltpu.VMEM((owners, 1, LANES), F32),
            jax.ShapeDtypeStruct((1, 1), jnp.int32),
        ),
        in_specs=[IN_VMEM],
        out_specs=(IN_VMEM, pl.BlockSpec(memory_space=pltpu.SMEM)),
        scratch_shapes=[
            pltpu.VMEM((total, LANES), F32),
            pltpu.VMEM((1, total), F32),
        ]
        + ([] if total > 2048 else [pltpu.VMEM((total, LANES), F32), pltpu.VMEM((total // 16, LANES), F32)]),
        compiler_params=pltpu.CompilerParams(vmem_limit_bytes=48 * MB),
        name="score",
    )(got)


def place_kernel(owners, back_ref, cid_ref, code_ref, valid_ref, out_ref, out, sem):
    for start in range(0, cid_ref.shape[0], 8):
        at = slice(start, start + 8)
        owner = lax.shift_right_logical(cid_ref[at, :], 3)
        code = code_ref[at, :]
        result = jnp.zeros((8, LANES), F32)
        for source in range(owners):
            line = jnp.broadcast_to(back_ref[source], (8, LANES))
            value = jnp.take_along_axis(line, code, axis=1, mode="promise_in_bounds")
            result = jnp.where(owner == source, value, result)
        out[at, :] = jnp.where(valid_ref[at, :] == 1, result, 0.0)
    store = pltpu.make_async_copy(out, out_ref, sem)
    store.start()
    store.wait()


def place(back, cluster_id, code, valid, owners):
    rows = cluster_id.shape[0]
    shape = (rows // LANES, LANES)
    return pl.pallas_call(
        functools.partial(place_kernel, owners),
        out_shape=pltpu.HBM(shape, F32),
        in_specs=[IN_VMEM] * 4,
        out_specs=ANY,
        scratch_shapes=[pltpu.VMEM(shape, F32), pltpu.SemaphoreType.DMA],
        compiler_params=pltpu.CompilerParams(vmem_limit_bytes=4 * MB),
        name="place",
    )(back, cluster_id.reshape(shape), code, valid.reshape(shape)).reshape(rows)


def every_slot(embeddings, cluster_id, valid, owners):
    width = embeddings.shape[1]
    clusters = CL_DEV * owners
    values = embeddings.astype(F32)
    squares = jnp.sum(values * values, axis=1, keepdims=True)
    unit_rows = (values * lax.rsqrt(squares + 1e-06)).astype(BF)
    one_hot = (cluster_id[:, None] == jnp.arange(clusters, dtype=jnp.int32)[None, :]).astype(jnp.int32)
    ranking = jnp.sum(jnp.cumsum(one_hot, axis=0) * one_hot, axis=1) - 1
    target = cluster_id * SLOT + ranking
    outgoing = jnp.zeros((clusters * SLOT, width), BF).at[target].set(unit_rows)
    live_out = jnp.zeros((clusters * SLOT,), BF).at[target].set(valid.astype(BF))
    got = lax.all_to_all(
        outgoing.reshape(owners, CL_DEV * SLOT, width), "owners", split_axis=0, concat_axis=0, tiled=True
    )
    live = lax.all_to_all(
        live_out.reshape(owners, CL_DEV, SLOT), "owners", split_axis=0, concat_axis=0, tiled=True
    )
    got = got.reshape(owners, CL_DEV, SLOT, width).transpose(1, 0, 2, 3)
    got = got.reshape(CL_DEV, owners * SLOT, width)
    live = live.transpose(1, 0, 2).reshape(CL_DEV, owners * SLOT) > 0.5
    diagonal = jnp.eye(owners * SLOT, dtype=bool)

    def one_cluster(args):
        rows, flags = args
        scores = jnp.einsum("md,nd->mn", rows, rows, preferred_element_type=F32)
        allowed = flags[:, None] & flags[None, :] & ~diagonal
        return jnp.max(jnp.where(allowed, scores, -1.0), axis=1)

    best = lax.map(one_cluster, (got, live)).reshape(CL_DEV, owners, SLOT).transpose(1, 0, 2)
    back = lax.all_to_all(best, "owners", split_axis=0, concat_axis=0, tiled=True)
    return jnp.where(valid == 1, back.reshape(-1)[target], 0.0)


def swap(blocks, owners):
    split = blocks.reshape(owners, blocks.shape[0] // owners, blocks.shape[1])
    return lax.all_to_all(split, "owners", split_axis=0, concat_axis=0, tiled=True)


def shards(embeddings, cluster_id, valid):
    owners = lax.axis_size("owners")
    blocks, code = pack(embeddings, cluster_id, valid, owners)
    best, lost = score(swap(blocks, owners), owners)
    back = lax.all_to_all(best, "owners", split_axis=0, concat_axis=0, tiled=True)
    nearest = place(back, cluster_id, code, valid, owners)
    return lax.cond(
        lost[0, 0] > 0,
        lambda: every_slot(embeddings, cluster_id, valid, owners),
        lambda: nearest,
    )


def solution(mesh):
    placed = (P(("groups", "owners"), None), P(("groups", "owners")), P(("groups", "owners")))
    return jax.shard_map(
        shards, mesh=mesh, in_specs=placed, out_specs=P(("groups", "owners")), check_vma=False
    )
```

```python
import functools

import jax
import jax.numpy as jnp
from jax import lax
from jax.experimental import pallas as pl
from jax.experimental.pallas import tpu as pltpu
from jax.sharding import PartitionSpec as P

CL_DEV = 8
SLOT = 16
LANES = 128
SIZE = 80
TILE = 1280
STEP = 256
MB = 1024 * 1024
BF = jnp.bfloat16
F32 = jnp.float32
ANY = pl.BlockSpec(memory_space=pltpu.HBM)
IN_VMEM = pl.BlockSpec(memory_space=pltpu.VMEM)


def iota(shape, dim):
    return lax.broadcasted_iota(jnp.int32, shape, dim)


def bits(mask):
    return mask.astype(F32).astype(BF)


def product(left, right):
    return jnp.dot(left, right, preferred_element_type=F32)


def product_t(left, right):
    return lax.dot_general(left, right, (((1,), (1,)), ((), ())), preferred_element_type=F32)


def before():
    return bits(iota((LANES, LANES), 0) < iota((LANES, LANES), 1))


def fill(choose, dest, begin):
    index = iota((choose.shape[0], LANES), 0) + begin
    for line in range(dest.shape[0]):
        at = slice(line * LANES, (line + 1) * LANES)
        choose[:, at] = bits(index == dest[line : line + 1])


def pack_kernel(
    owners, cid_ref, valid_ref, rows_ref, blocks_ref, code_ref, held, unit, choose, out, in_sems, out_sems
):
    rows, width = held.shape
    total = out.shape[0]
    tile = choose.shape[0]
    lines = rows // LANES
    parts = rows // STEP
    loads = []
    for part in range(parts):
        at = pl.ds(part * STEP, STEP)
        loads.append(pltpu.make_async_copy(rows_ref.at[at], held.at[at], in_sems.at[part]))
        loads[-1].start()

    cid = cid_ref[...]
    live = valid_ref[...] == 1
    owner = lax.shift_right_logical(cid, 3)
    name = (cid & (CL_DEV - 1)) + 1
    target = jnp.where(live, owner, -1)
    index = iota((owners, LANES), 0)
    mine = [(index == target[line : line + 1]).astype(F32) for line in range(lines)]
    stacked = jnp.concatenate(mine, axis=0).astype(BF)
    inside = product(stacked, before())
    whole = product(stacked, jnp.ones((LANES, LANES), BF))
    offset = jnp.zeros((owners, LANES), F32)
    ranks = []
    for line in range(lines):
        at = slice(line * owners, (line + 1) * owners)
        ranks.append(jnp.sum(mine[line] * (inside[at] + offset), axis=0, keepdims=True))
        offset = offset + whole[at]
    pos = jnp.concatenate(ranks, axis=0).astype(jnp.int32)
    fits = live & (pos < SIZE - 1)
    lost = jnp.max((live & (pos >= SIZE - 1)).astype(F32))
    code = jnp.where(fits, pos, LANES - 1)
    code_ref[...] = code
    dest = jnp.where(fits, owner * SIZE + pos, -1)

    names = jnp.concatenate(
        [mine[line] * name[line : line + 1].astype(F32) for line in range(lines)], axis=1
    ).astype(BF)
    index = iota((LANES, LANES), 0)
    places = jnp.concatenate([bits(index == code[line : line + 1]) for line in range(lines)], axis=1)
    meta = product_t(names, places)
    meta = jnp.where(iota((owners, LANES), 1) == LANES - 1, lost, meta).astype(BF)

    fill(choose, dest, 0)
    for part in range(parts):
        loads[part].wait()
        for chunk in range(part * STEP, (part + 1) * STEP, 64):
            values = held[chunk : chunk + 64, :].astype(F32)
            squares = jnp.sum(values * values, axis=1, keepdims=True)
            unit[chunk : chunk + 64, :] = (values * lax.rsqrt(squares + 1e-06)).astype(BF)

    stores = []
    for first in range(0, total, tile):
        if first:
            fill(choose, dest, first)
        for column in range(0, width, STEP):
            at = slice(column, column + STEP)
            packed = product(choose[...], unit[:, at])
            if column == 0:
                line = iota((tile, owners), 0) + first
                last = (iota((1, owners), 1) + 1) * SIZE - 1
                packed = jnp.concatenate(
                    [packed[:, :LANES] + product(bits(line == last), meta), packed[:, LANES:]], axis=1
                )
            out[pl.ds(first, tile), at] = packed.astype(BF)
            where = (pl.ds(first, tile), at)
            stores.append(
                pltpu.make_async_copy(out.at[where], blocks_ref.at[where], out_sems.at[len(stores)])
            )
            stores[-1].start()
    for store in stores:
        store.wait()


def pack_direct(
    owners, cid_ref, valid_ref, rows_ref, blocks_ref, code_ref, held, unit, choose, out, tags, marks, *sems
):
    rows, width = held.shape
    total = out.shape[0]
    lines = rows // LANES
    parts = rows // STEP
    pairs = STEP // LANES
    chunk = 4 * SIZE
    columns = width // STEP
    in_sems, mark_sems, out_sems = sems[:parts], sems[parts : parts + 2], sems[parts + 2 :]
    fetches = []
    for number, source in enumerate((cid_ref, valid_ref)):
        fetches.append(pltpu.make_async_copy(source, marks.at[number], mark_sems[number]))
        fetches[-1].start()
    loads = []
    for part in range(parts):
        at = pl.ds(part * STEP, STEP)
        loads.append(pltpu.make_async_copy(rows_ref.at[at], held.at[at], in_sems[part]))
        loads[-1].start()
    stores = []
    for fetch in fetches:
        fetch.wait()

    def body(count_acc, tag_acc, *accs):
        cid = marks[0]
        live = marks[1] == 1
        owner = lax.shift_right_logical(cid, 3)
        name = (cid & (CL_DEV - 1)) + 1
        target = jnp.where(live, owner, -1)
        index = iota((owners, LANES), 0)
        mine = [(index == target[line : line + 1]).astype(F32) for line in range(lines)]
        mine = [jnp.concatenate(mine[i : i + pairs], axis=1) for i in range(0, lines, pairs)]
        stacked = jnp.concatenate(mine, axis=0)
        pltpu.matmul_push_rhs(bits(iota((STEP, STEP), 0) < iota((STEP, STEP), 1)), 0, 0)
        pltpu.matmul_acc_lhs(count_acc, stacked.astype(BF), load_staged_rhs=0)
        whole = jnp.sum(stacked, axis=1, keepdims=True)
        inside = pltpu.matmul_pop(count_acc)
        offset = jnp.zeros((owners, 1), F32)
        ranks = []
        for part in range(parts):
            at = slice(part * owners, (part + 1) * owners)
            rank = jnp.sum(mine[part] * (inside[at] + offset), axis=0, keepdims=True)
            ranks += [rank[:, i * LANES : (i + 1) * LANES] for i in range(pairs)]
            offset = offset + whole[at]
        pos = jnp.concatenate(ranks, axis=0).astype(jnp.int32)
        fits = live & (pos < SIZE - 1)
        lost = jnp.max((live & (pos >= SIZE - 1)).astype(F32))
        code = jnp.where(fits, pos, LANES - 1)
        code_ref[...] = code
        marks[2] = jnp.where(fits, owner * SIZE + pos, -1)

        def quarter(part):
            if isinstance(part, int):
                return pl.ds(part * STEP, STEP)
            return pl.ds(pl.multiple_of(part * STEP, STEP), STEP)

        def prepare(part):
            first = quarter(part).start
            for begin in range(0, STEP, 32):
                at = pl.ds(first + begin, 32)
                values = held[at, :].astype(F32)
                squares = jnp.sum(values * values, axis=1, keepdims=True)
                unit[at, :] = (values * lax.rsqrt(squares + 1e-06)).astype(BF)
            index = iota((total, LANES), 0)
            for line in range(pairs):
                dest = marks[2, pl.ds(part * pairs + line, 1), :]
                choose[:, pl.ds(first + line * LANES, LANES)] = bits(index == dest)

        def multiply(part, number, column, chunks, turn):
            kept = quarter(part)
            at = slice(column * STEP, (column + 1) * STEP)
            pltpu.matmul_push_rhs(unit[kept, at], turn, number)
            first = True
            for place, slot in chunks:
                pltpu.matmul_acc_lhs(
                    accs[number * 3 + slot],
                    choose[place * chunk : (place + 1) * chunk, kept],
                    load_staged_rhs=turn if first else None,
                )
                first = False

        def write(number, column, place, slot):
            packed = pltpu.matmul_pop(accs[number * 3 + slot])
            at = slice(column * STEP, (column + 1) * STEP)
            first = place * chunk
            for row in range(first, first + chunk, 16):
                piece = packed[row - first : row - first + 16]
                source, spot = divmod(row, SIZE)
                if column == 0 and spot + 16 == SIZE:
                    piece = jnp.where(iota((16, STEP), 0) == 15, tags[...][source : source + 1], piece)
                out[row : row + 16, at] = piece.astype(BF)
            where = (pl.ds(first, chunk), at)
            stores.append(
                pltpu.make_async_copy(out.at[where], blocks_ref.at[where], out_sems[len(stores)])
            )
            stores[-1].start()

        opening = [(place, place) for place in range(3)]
        for load in loads:
            load.wait()
        prepare(0)

        def next_part(part, carry):
            prepare(part)
            for number in range(2):
                multiply(part - 1, number, number, opening, 0)
            return carry

        lax.fori_loop(1, parts, next_part, 0)
        for number in range(2):
            multiply(parts - 1, number, number, opening, 0)

        index = iota((STEP, LANES), 0)
        for part in range(parts):
            here = range(part * pairs, (part + 1) * pairs)
            places = [bits(index == code[line : line + 1]) for line in here]
            named = [name[line : line + 1].astype(F32) for line in here]
            pltpu.matmul_push_rhs(jnp.concatenate(places, axis=1), part % 2, 1, transpose=True)
            pltpu.matmul_acc_lhs(
                tag_acc,
                (mine[part] * jnp.concatenate(named, axis=1)).astype(BF),
                load_staged_rhs=part % 2,
            )
        lane = iota((owners, STEP), 1)
        tags[...] = jnp.where(
            lane < LANES - 1, pltpu.matmul_pop(tag_acc), jnp.where(lane == LANES - 1, lost, 0.0)
        )

        done = [(0, place) for place in range(3)]
        left = [(0, place) for place in range(3, total // chunk)]
        for column in range(2, columns, 2):
            left += [(column, place) for place in range(total // chunk)]
        for turn, (column, place) in enumerate(left):
            before = done[turn]
            for number in range(2):
                write(number, before[0] + number, before[1], turn % 3)
            for part in range(parts):
                for number in range(2):
                    multiply(part, number, column + number, [(place, turn % 3)], part % 2)
            done.append((column, place))
        for turn in range(len(left), len(done)):
            for number in range(2):
                write(number, done[turn][0] + number, done[turn][1], turn % 3)

    pl.run_scoped(
        body,
        pltpu.ACC(mxu_id=0)((parts * owners, STEP), F32),
        pltpu.ACC(mxu_id=1)((owners, STEP), F32),
        *[pltpu.ACC(mxu_id=number // 3)((chunk, STEP), F32) for number in range(6)],
    )
    for store in stores:
        store.wait()


def pack(embeddings, cluster_id, valid, owners):
    rows, width = embeddings.shape
    total = owners * SIZE
    tile = min(total, TILE)
    lines = (rows // LANES, LANES)
    small = total <= 2048
    return pl.pallas_call(
        functools.partial(pack_direct if small else pack_kernel, owners),
        out_shape=(
            pltpu.HBM((total, width), BF),
            jax.ShapeDtypeStruct(lines, jnp.int32),
        ),
        in_specs=[ANY if small else IN_VMEM] * 2 + [ANY],
        out_specs=(ANY, IN_VMEM),
        scratch_shapes=[
            pltpu.VMEM((rows, width), BF),
            pltpu.VMEM((rows, width), BF),
            pltpu.VMEM((tile, rows), BF),
            pltpu.VMEM((total, width), BF),
        ]
        + (
            [pltpu.VMEM((owners, STEP), F32), pltpu.VMEM((3,) + lines, jnp.int32)]
            + [pltpu.SemaphoreType.DMA] * (rows // STEP + 2 + owners // 4 * (width // STEP))
            if small
            else [
                pltpu.SemaphoreType.DMA((rows // STEP,)),
                pltpu.SemaphoreType.DMA((total // tile * (width // STEP),)),
            ]
        ),
        compiler_params=pltpu.CompilerParams(vmem_limit_bytes=52 * MB),
        name="pack",
    )(cluster_id.reshape(lines), valid.reshape(lines), embeddings)


def on_units(size, count, multiply, use):
    def body(*accs):
        for number in range(count + 2):
            if number < count:
                multiply(number, number % 2, accs[number % 4])
            if number >= 2:
                use(number - 2, pltpu.matmul_pop(accs[(number - 2) % 4]))

    pl.run_scoped(body, *[pltpu.ACC(mxu_id=number % 2)((size, STEP), F32) for number in range(4)])


def triangle(total, rows, side, tops, line, across, down):
    width = rows.shape[1]
    blocks = total // STEP
    seen = set()

    def keep(ref, at, value):
        if (id(ref), at) in seen:
            value = jnp.maximum(value, ref[at : at + 8, :])
        seen.add((id(ref), at))
        ref[at : at + 8, :] = value

    work = []
    for column in range(blocks):
        for row in range(column, blocks, 2):
            work.append((column, row, min(2, blocks - row)))

    def run(work, count):
        def multiply(number, unit, acc):
            column, row, _ = work[number]
            for piece in range(width // STEP):
                at = slice(piece * STEP, (piece + 1) * STEP)
                pltpu.matmul_push_rhs(
                    rows[column * STEP : (column + 1) * STEP, at], piece % 2, unit, transpose=True
                )
                pltpu.matmul_acc_lhs(
                    acc, rows[row * STEP : (row + count) * STEP, at], load_staged_rhs=piece % 2
                )

        def use(number, scores):
            column, row, _ = work[number]
            apart = iota((8, LANES), 1) - iota((8, LANES), 0)
            best = [jnp.full((8, LANES), -1.0, F32)] * (STEP // LANES)
            for block in range(0, count * STEP, 8):
                start = row * STEP + block
                found = []
                for part in range(STEP // LANES):
                    first = column * STEP + part * LANES
                    allowed = side[start : start + 8, :] == tops[:, first : first + LANES]
                    if 0 <= start - first < LANES:
                        allowed = allowed & (apart != start - first)
                    here = scores[block : block + 8, part * LANES : (part + 1) * LANES]
                    found.append(jnp.where(allowed, here, -1.0))
                    best[part] = jnp.maximum(best[part], found[part])
                if start // STEP > column:
                    keep(across, start, functools.reduce(jnp.maximum, found))
            for part in range(STEP // LANES):
                keep(down, (column * (STEP // LANES) + part) * 8, best[part])

        on_units(count * STEP, len(work), multiply, use)

    run([item for item in work if item[2] == 2], 2)
    run([item for item in work if item[2] == 1], 1)
    for column in range(blocks):
        for part in range(STEP // LANES):
            first = column * STEP + part * LANES
            at = (column * (STEP // LANES) + part) * 8
            most = jnp.max(down[at : at + 8, :], axis=0, keepdims=True)
            if column:
                turned = across[first : first + LANES, :].T
                most = jnp.maximum(most, jnp.max(turned, axis=0, keepdims=True))
            line[:, first : first + LANES] = most


def score_kernel(owners, got_ref, best_ref, lost_ref, side, line, *more):
    total = line.shape[1]
    rows = got_ref.reshape(total, got_ref.shape[2])

    same = iota((SIZE, LANES), 0) == iota((SIZE, LANES), 1)
    lanes = iota((1, 2 * LANES), 1)
    lost = jnp.zeros((1, LANES), F32)
    line[...] = jnp.zeros((1, total), F32)
    for source in range(owners):
        name = got_ref[source, SIZE - 16 : SIZE, :LANES].astype(F32)[15:16]
        lost = jnp.maximum(lost, name)
        found = jnp.sum(jnp.where(same, name, 0.0), axis=1, keepdims=True)
        side[source * SIZE : (source + 1) * SIZE, :] = jnp.broadcast_to(
            jnp.where(found == 0.0, -1.0, found), (SIZE, LANES)
        )
        base, shift = divmod(source * SIZE, LANES)
        base *= LANES
        name = jnp.where(lanes < SIZE, jnp.concatenate([name, name], axis=1), 0.0)
        if shift:
            name = pltpu.roll(name, shift, 1)
        size = min(2 * LANES, total - base)
        line[:, base : base + size] = line[:, base : base + size] + name[:, :size]
    lost = jnp.max(jnp.where(lanes[:, :LANES] == LANES - 1, lost, 0.0))
    lost_ref[0, 0] = (lost > 0.0).astype(jnp.int32)
    tops = jnp.broadcast_to(line[...], (8, total))
    if total <= 2048:
        triangle(total, rows, side, tops, line, *more)
    else:
        @pl.loop(0, total // STEP)
        def _(number):
            first = pl.multiple_of(number * STEP, STEP)
            here = pl.ds(first, STEP)
            top = jnp.broadcast_to(line[:, here], (8, STEP))
            scores = product_t(rows[...], rows[here, :])
            apart = iota((8, LANES), 1) - iota((8, LANES), 0)
            for part in range(STEP // LANES):
                lanes = slice(part * LANES, (part + 1) * LANES)
                result = jnp.full((8, LANES), -1.0, F32)
                for block in range(0, total, 8):
                    at = slice(block, block + 8)
                    allowed = (side[at, :] == top[:, lanes]) & (apart != block - first - part * LANES)
                    result = jnp.maximum(result, jnp.where(allowed, scores[at, lanes], -1.0))
                line[:, pl.ds(first + part * LANES, LANES)] = jnp.max(result, axis=0, keepdims=True)

    for source in range(owners):
        base, shift = divmod(source * SIZE, LANES)
        base *= LANES
        piece = line[:, base : min(base + 2 * LANES, total)]
        if shift:
            piece = pltpu.roll(piece, piece.shape[1] - shift, 1)
        best_ref[source] = piece[:, :LANES]


def score(got, owners):
    width = got.shape[2]
    total = owners * SIZE
    return pl.pallas_call(
        functools.partial(score_kernel, owners),
        out_shape=(
            pltpu.VMEM((owners, 1, LANES), F32),
            jax.ShapeDtypeStruct((1, 1), jnp.int32),
        ),
        in_specs=[IN_VMEM],
        out_specs=(IN_VMEM, pl.BlockSpec(memory_space=pltpu.SMEM)),
        scratch_shapes=[
            pltpu.VMEM((total, LANES), F32),
            pltpu.VMEM((1, total), F32),
        ]
        + ([] if total > 2048 else [pltpu.VMEM((total, LANES), F32), pltpu.VMEM((total // 16, LANES), F32)]),
        compiler_params=pltpu.CompilerParams(vmem_limit_bytes=48 * MB),
        name="score",
    )(got)


def place_kernel(owners, back_ref, cid_ref, code_ref, valid_ref, out_ref, out, sem):
    for start in range(0, cid_ref.shape[0], 8):
        at = slice(start, start + 8)
        owner = lax.shift_right_logical(cid_ref[at, :], 3)
        code = code_ref[at, :]
        result = jnp.zeros((8, LANES), F32)
        for source in range(owners):
            line = jnp.broadcast_to(back_ref[source], (8, LANES))
            value = jnp.take_along_axis(line, code, axis=1, mode="promise_in_bounds")
            result = jnp.where(owner == source, value, result)
        out[at, :] = jnp.where(valid_ref[at, :] == 1, result, 0.0)
    store = pltpu.make_async_copy(out, out_ref, sem)
    store.start()
    store.wait()


def place(back, cluster_id, code, valid, owners):
    rows = cluster_id.shape[0]
    shape = (rows // LANES, LANES)
    return pl.pallas_call(
        functools.partial(place_kernel, owners),
        out_shape=pltpu.HBM(shape, F32),
        in_specs=[IN_VMEM] * 4,
        out_specs=ANY,
        scratch_shapes=[pltpu.VMEM(shape, F32), pltpu.SemaphoreType.DMA],
        compiler_params=pltpu.CompilerParams(vmem_limit_bytes=4 * MB),
        name="place",
    )(back, cluster_id.reshape(shape), code, valid.reshape(shape)).reshape(rows)


def every_slot(embeddings, cluster_id, valid, owners):
    width = embeddings.shape[1]
    clusters = CL_DEV * owners
    values = embeddings.astype(F32)
    squares = jnp.sum(values * values, axis=1, keepdims=True)
    unit_rows = (values * lax.rsqrt(squares + 1e-06)).astype(BF)
    one_hot = (cluster_id[:, None] == jnp.arange(clusters, dtype=jnp.int32)[None, :]).astype(jnp.int32)
    ranking = jnp.sum(jnp.cumsum(one_hot, axis=0) * one_hot, axis=1) - 1
    target = cluster_id * SLOT + ranking
    outgoing = jnp.zeros((clusters * SLOT, width), BF).at[target].set(unit_rows)
    live_out = jnp.zeros((clusters * SLOT,), BF).at[target].set(valid.astype(BF))
    got = lax.all_to_all(
        outgoing.reshape(owners, CL_DEV * SLOT, width), "owners", split_axis=0, concat_axis=0, tiled=True
    )
    live = lax.all_to_all(
        live_out.reshape(owners, CL_DEV, SLOT), "owners", split_axis=0, concat_axis=0, tiled=True
    )
    got = got.reshape(owners, CL_DEV, SLOT, width).transpose(1, 0, 2, 3)
    got = got.reshape(CL_DEV, owners * SLOT, width)
    live = live.transpose(1, 0, 2).reshape(CL_DEV, owners * SLOT) > 0.5
    diagonal = jnp.eye(owners * SLOT, dtype=bool)

    def one_cluster(args):
        rows, flags = args
        scores = jnp.einsum("md,nd->mn", rows, rows, preferred_element_type=F32)
        allowed = flags[:, None] & flags[None, :] & ~diagonal
        return jnp.max(jnp.where(allowed, scores, -1.0), axis=1)

    best = lax.map(one_cluster, (got, live)).reshape(CL_DEV, owners, SLOT).transpose(1, 0, 2)
    back = lax.all_to_all(best, "owners", split_axis=0, concat_axis=0, tiled=True)
    return jnp.where(valid == 1, back.reshape(-1)[target], 0.0)


def swap(blocks, owners):
    split = blocks.reshape(owners, blocks.shape[0] // owners, blocks.shape[1])
    return lax.all_to_all(split, "owners", split_axis=0, concat_axis=0, tiled=True)


def shards(embeddings, cluster_id, valid):
    owners = lax.axis_size("owners")
    blocks, code = pack(embeddings, cluster_id, valid, owners)
    best, lost = score(swap(blocks, owners), owners)
    back = lax.all_to_all(best, "owners", split_axis=0, concat_axis=0, tiled=True)
    nearest = place(back, cluster_id, code, valid, owners)
    return lax.cond(
        lost[0, 0] > 0,
        lambda: every_slot(embeddings, cluster_id, valid, owners),
        lambda: nearest,
    )


def solution(mesh):
    placed = (P(("groups", "owners"), None), P(("groups", "owners")), P(("groups", "owners")))
    return jax.shard_map(
        shards, mesh=mesh, in_specs=placed, out_specs=P(("groups", "owners")), check_vma=False
    )
```

```python
import functools

import jax
import jax.numpy as jnp
from jax import lax
from jax.experimental import pallas as pl
from jax.experimental.pallas import tpu as pltpu
from jax.sharding import PartitionSpec as P

CL_DEV = 8
SLOT = 16
LANES = 128
SIZE = 80
TILE = 1280
STEP = 256
MB = 1024 * 1024
BF = jnp.bfloat16
F32 = jnp.float32
ANY = pl.BlockSpec(memory_space=pltpu.HBM)
IN_VMEM = pl.BlockSpec(memory_space=pltpu.VMEM)


def iota(shape, dim):
    return lax.broadcasted_iota(jnp.int32, shape, dim)


def bits(mask):
    return mask.astype(F32).astype(BF)


def product(left, right):
    return jnp.dot(left, right, preferred_element_type=F32)


def product_t(left, right):
    return lax.dot_general(left, right, (((1,), (1,)), ((), ())), preferred_element_type=F32)


def before():
    return bits(iota((LANES, LANES), 0) < iota((LANES, LANES), 1))


def fill(choose, dest, begin):
    index = iota((choose.shape[0], LANES), 0) + begin
    for line in range(dest.shape[0]):
        at = slice(line * LANES, (line + 1) * LANES)
        choose[:, at] = bits(index == dest[line : line + 1])


def pack_kernel(
    owners, cid_ref, valid_ref, rows_ref, blocks_ref, code_ref, held, unit, choose, out, in_sems, out_sems
):
    rows, width = held.shape
    total = out.shape[0]
    tile = choose.shape[0]
    lines = rows // LANES
    parts = rows // STEP
    loads = []
    for part in range(parts):
        at = pl.ds(part * STEP, STEP)
        loads.append(pltpu.make_async_copy(rows_ref.at[at], held.at[at], in_sems.at[part]))
        loads[-1].start()

    cid = cid_ref[...]
    live = valid_ref[...] == 1
    owner = lax.shift_right_logical(cid, 3)
    name = (cid & (CL_DEV - 1)) + 1
    target = jnp.where(live, owner, -1)
    index = iota((owners, LANES), 0)
    mine = [(index == target[line : line + 1]).astype(F32) for line in range(lines)]
    stacked = jnp.concatenate(mine, axis=0).astype(BF)
    inside = product(stacked, before())
    whole = product(stacked, jnp.ones((LANES, LANES), BF))
    offset = jnp.zeros((owners, LANES), F32)
    ranks = []
    for line in range(lines):
        at = slice(line * owners, (line + 1) * owners)
        ranks.append(jnp.sum(mine[line] * (inside[at] + offset), axis=0, keepdims=True))
        offset = offset + whole[at]
    pos = jnp.concatenate(ranks, axis=0).astype(jnp.int32)
    fits = live & (pos < SIZE - 1)
    lost = jnp.max((live & (pos >= SIZE - 1)).astype(F32))
    code = jnp.where(fits, pos, LANES - 1)
    code_ref[...] = code
    dest = jnp.where(fits, owner * SIZE + pos, -1)

    names = jnp.concatenate(
        [mine[line] * name[line : line + 1].astype(F32) for line in range(lines)], axis=1
    ).astype(BF)
    index = iota((LANES, LANES), 0)
    places = jnp.concatenate([bits(index == code[line : line + 1]) for line in range(lines)], axis=1)
    meta = product_t(names, places)
    meta = jnp.where(iota((owners, LANES), 1) == LANES - 1, lost, meta).astype(BF)

    fill(choose, dest, 0)
    for part in range(parts):
        loads[part].wait()
        for chunk in range(part * STEP, (part + 1) * STEP, 64):
            values = held[chunk : chunk + 64, :].astype(F32)
            squares = jnp.sum(values * values, axis=1, keepdims=True)
            unit[chunk : chunk + 64, :] = (values * lax.rsqrt(squares + 1e-06)).astype(BF)

    stores = []
    for first in range(0, total, tile):
        if first:
            fill(choose, dest, first)
        for column in range(0, width, STEP):
            at = slice(column, column + STEP)
            packed = product(choose[...], unit[:, at])
            if column == 0:
                line = iota((tile, owners), 0) + first
                last = (iota((1, owners), 1) + 1) * SIZE - 1
                packed = jnp.concatenate(
                    [packed[:, :LANES] + product(bits(line == last), meta), packed[:, LANES:]], axis=1
                )
            out[pl.ds(first, tile), at] = packed.astype(BF)
            where = (pl.ds(first, tile), at)
            stores.append(
                pltpu.make_async_copy(out.at[where], blocks_ref.at[where], out_sems.at[len(stores)])
            )
            stores[-1].start()
    for store in stores:
        store.wait()


def pack_direct(
    owners, cid_ref, valid_ref, rows_ref, blocks_ref, code_ref, held, unit, choose, out, tags, marks, *sems
):
    rows, width = held.shape
    total = out.shape[0]
    lines = rows // LANES
    parts = rows // STEP
    pairs = STEP // LANES
    chunk = 4 * SIZE
    columns = width // STEP
    in_sems, mark_sems, out_sems = sems[:parts], sems[parts : parts + 2], sems[parts + 2 :]
    fetches = []
    for number, source in enumerate((cid_ref, valid_ref)):
        fetches.append(pltpu.make_async_copy(source, marks.at[number], mark_sems[number]))
        fetches[-1].start()
    loads = []
    for part in range(parts):
        at = pl.ds(part * STEP, STEP)
        loads.append(pltpu.make_async_copy(rows_ref.at[at], held.at[at], in_sems[part]))
        loads[-1].start()
    stores = []
    for fetch in fetches:
        fetch.wait()

    def body(count_acc, tag_acc, *accs):
        cid = marks[0]
        live = marks[1] == 1
        owner = lax.shift_right_logical(cid, 3)
        name = (cid & (CL_DEV - 1)) + 1
        target = jnp.where(live, owner, -1)
        index = iota((owners, LANES), 0)
        mine = [(index == target[line : line + 1]).astype(F32) for line in range(lines)]
        mine = [jnp.concatenate(mine[i : i + pairs], axis=1) for i in range(0, lines, pairs)]
        stacked = jnp.concatenate(mine, axis=0)
        pltpu.matmul_push_rhs(bits(iota((STEP, STEP), 0) < iota((STEP, STEP), 1)), 0, 0)
        pltpu.matmul_acc_lhs(count_acc, stacked.astype(BF), load_staged_rhs=0)
        whole = jnp.sum(stacked, axis=1, keepdims=True)
        inside = pltpu.matmul_pop(count_acc)
        offset = jnp.zeros((owners, 1), F32)
        ranks = []
        for part in range(parts):
            at = slice(part * owners, (part + 1) * owners)
            rank = jnp.sum(mine[part] * (inside[at] + offset), axis=0, keepdims=True)
            ranks += [rank[:, i * LANES : (i + 1) * LANES] for i in range(pairs)]
            offset = offset + whole[at]
        pos = jnp.concatenate(ranks, axis=0).astype(jnp.int32)
        fits = live & (pos < SIZE - 1)
        lost = jnp.max((live & (pos >= SIZE - 1)).astype(F32))
        code = jnp.where(fits, pos, LANES - 1)
        code_ref[...] = code
        dest = jnp.where(fits, owner * SIZE + pos, -1)

        def prepare(part):
            loads[part].wait()
            for begin in range(part * STEP, (part + 1) * STEP, 64):
                values = held[begin : begin + 64, :].astype(F32)
                squares = jnp.sum(values * values, axis=1, keepdims=True)
                unit[begin : begin + 64, :] = (values * lax.rsqrt(squares + 1e-06)).astype(BF)
            index = iota((total, LANES), 0)
            for line in range(part * pairs, (part + 1) * pairs):
                at = slice(line * LANES, (line + 1) * LANES)
                choose[:, at] = bits(index == dest[line : line + 1])

        def multiply(part, number, column, chunks):
            kept = slice(part * STEP, (part + 1) * STEP)
            at = slice(column * STEP, (column + 1) * STEP)
            pltpu.matmul_push_rhs(unit[kept, at], part % 2, number)
            first = True
            for place, slot in chunks:
                pltpu.matmul_acc_lhs(
                    accs[number * 3 + slot],
                    choose[place * chunk : (place + 1) * chunk, kept],
                    load_staged_rhs=part % 2 if first else None,
                )
                first = False

        def write(number, column, place, slot):
            packed = pltpu.matmul_pop(accs[number * 3 + slot])
            at = slice(column * STEP, (column + 1) * STEP)
            first = place * chunk
            for row in range(first, first + chunk, 16):
                piece = packed[row - first : row - first + 16]
                source, spot = divmod(row, SIZE)
                if column == 0 and spot + 16 == SIZE:
                    piece = jnp.where(iota((16, STEP), 0) == 15, tags[...][source : source + 1], piece)
                out[row : row + 16, at] = piece.astype(BF)
            where = (pl.ds(first, chunk), at)
            stores.append(
                pltpu.make_async_copy(out.at[where], blocks_ref.at[where], out_sems[len(stores)])
            )
            stores[-1].start()

        opening = [(place, place) for place in range(3)]
        for part in range(parts):
            prepare(part)
            if part:
                for number in range(2):
                    multiply(part - 1, number, number, opening)
        for number in range(2):
            multiply(parts - 1, number, number, opening)

        index = iota((STEP, LANES), 0)
        for part in range(parts):
            here = range(part * pairs, (part + 1) * pairs)
            places = [bits(index == code[line : line + 1]) for line in here]
            named = [name[line : line + 1].astype(F32) for line in here]
            pltpu.matmul_push_rhs(jnp.concatenate(places, axis=1), part % 2, 1, transpose=True)
            pltpu.matmul_acc_lhs(
                tag_acc,
                (mine[part] * jnp.concatenate(named, axis=1)).astype(BF),
                load_staged_rhs=part % 2,
            )
        lane = iota((owners, STEP), 1)
        tags[...] = jnp.where(
            lane < LANES - 1, pltpu.matmul_pop(tag_acc), jnp.where(lane == LANES - 1, lost, 0.0)
        )

        done = [(0, place) for place in range(3)]
        left = [(0, place) for place in range(3, total // chunk)]
        for column in range(2, columns, 2):
            left += [(column, place) for place in range(total // chunk)]
        for turn, (column, place) in enumerate(left):
            before = done[turn]
            for number in range(2):
                write(number, before[0] + number, before[1], turn % 3)
            for part in range(parts):
                for number in range(2):
                    multiply(part, number, column + number, [(place, turn % 3)])
            done.append((column, place))
        for turn in range(len(left), len(done)):
            for number in range(2):
                write(number, done[turn][0] + number, done[turn][1], turn % 3)

    pl.run_scoped(
        body,
        pltpu.ACC(mxu_id=0)((parts * owners, STEP), F32),
        pltpu.ACC(mxu_id=1)((owners, STEP), F32),
        *[pltpu.ACC(mxu_id=number // 3)((chunk, STEP), F32) for number in range(6)],
    )
    for store in stores:
        store.wait()


def pack(embeddings, cluster_id, valid, owners):
    rows, width = embeddings.shape
    total = owners * SIZE
    tile = min(total, TILE)
    lines = (rows // LANES, LANES)
    small = total <= 2048
    return pl.pallas_call(
        functools.partial(pack_direct if small else pack_kernel, owners),
        out_shape=(
            pltpu.HBM((total, width), BF),
            jax.ShapeDtypeStruct(lines, jnp.int32),
        ),
        in_specs=[ANY if small else IN_VMEM] * 2 + [ANY],
        out_specs=(ANY, IN_VMEM),
        scratch_shapes=[
            pltpu.VMEM((rows, width), BF),
            pltpu.VMEM((rows, width), BF),
            pltpu.VMEM((tile, rows), BF),
            pltpu.VMEM((total, width), BF),
        ]
        + (
            [pltpu.VMEM((owners, STEP), F32), pltpu.VMEM((2,) + lines, jnp.int32)]
            + [pltpu.SemaphoreType.DMA] * (rows // STEP + 2 + owners // 4 * (width // STEP))
            if small
            else [
                pltpu.SemaphoreType.DMA((rows // STEP,)),
                pltpu.SemaphoreType.DMA((total // tile * (width // STEP),)),
            ]
        ),
        compiler_params=pltpu.CompilerParams(vmem_limit_bytes=52 * MB),
        name="pack",
    )(cluster_id.reshape(lines), valid.reshape(lines), embeddings)


def on_units(size, count, multiply, use):
    def body(*accs):
        for number in range(count + 2):
            if number < count:
                multiply(number, number % 2, accs[number % 4])
            if number >= 2:
                use(number - 2, pltpu.matmul_pop(accs[(number - 2) % 4]))

    pl.run_scoped(body, *[pltpu.ACC(mxu_id=number % 2)((size, STEP), F32) for number in range(4)])


def triangle(total, rows, side, tops, line, across, down):
    width = rows.shape[1]
    blocks = total // STEP
    seen = set()

    def keep(ref, at, value):
        if (id(ref), at) in seen:
            value = jnp.maximum(value, ref[at : at + 8, :])
        seen.add((id(ref), at))
        ref[at : at + 8, :] = value

    work = []
    for column in range(blocks):
        for row in range(column, blocks, 2):
            work.append((column, row, min(2, blocks - row)))

    def run(work, count):
        def multiply(number, unit, acc):
            column, row, _ = work[number]
            for piece in range(width // STEP):
                at = slice(piece * STEP, (piece + 1) * STEP)
                pltpu.matmul_push_rhs(
                    rows[column * STEP : (column + 1) * STEP, at], piece % 2, unit, transpose=True
                )
                pltpu.matmul_acc_lhs(
                    acc, rows[row * STEP : (row + count) * STEP, at], load_staged_rhs=piece % 2
                )

        def use(number, scores):
            column, row, _ = work[number]
            apart = iota((8, LANES), 1) - iota((8, LANES), 0)
            best = [jnp.full((8, LANES), -1.0, F32)] * (STEP // LANES)
            for block in range(0, count * STEP, 8):
                start = row * STEP + block
                found = []
                for part in range(STEP // LANES):
                    first = column * STEP + part * LANES
                    allowed = side[start : start + 8, :] == tops[:, first : first + LANES]
                    if 0 <= start - first < LANES:
                        allowed = allowed & (apart != start - first)
                    here = scores[block : block + 8, part * LANES : (part + 1) * LANES]
                    found.append(jnp.where(allowed, here, -1.0))
                    best[part] = jnp.maximum(best[part], found[part])
                if start // STEP > column:
                    keep(across, start, functools.reduce(jnp.maximum, found))
            for part in range(STEP // LANES):
                keep(down, (column * (STEP // LANES) + part) * 8, best[part])

        on_units(count * STEP, len(work), multiply, use)

    run([item for item in work if item[2] == 2], 2)
    run([item for item in work if item[2] == 1], 1)
    for column in range(blocks):
        for part in range(STEP // LANES):
            first = column * STEP + part * LANES
            at = (column * (STEP // LANES) + part) * 8
            most = jnp.max(down[at : at + 8, :], axis=0, keepdims=True)
            if column:
                turned = across[first : first + LANES, :].T
                most = jnp.maximum(most, jnp.max(turned, axis=0, keepdims=True))
            line[:, first : first + LANES] = most


def score_kernel(owners, got_ref, best_ref, lost_ref, side, line, *more):
    total = line.shape[1]
    rows = got_ref.reshape(total, got_ref.shape[2])

    same = iota((SIZE, LANES), 0) == iota((SIZE, LANES), 1)
    lanes = iota((1, 2 * LANES), 1)
    lost = jnp.zeros((1, LANES), F32)
    line[...] = jnp.zeros((1, total), F32)
    for source in range(owners):
        name = got_ref[source, SIZE - 16 : SIZE, :LANES].astype(F32)[15:16]
        lost = jnp.maximum(lost, name)
        found = jnp.sum(jnp.where(same, name, 0.0), axis=1, keepdims=True)
        side[source * SIZE : (source + 1) * SIZE, :] = jnp.broadcast_to(
            jnp.where(found == 0.0, -1.0, found), (SIZE, LANES)
        )
        base, shift = divmod(source * SIZE, LANES)
        base *= LANES
        name = jnp.where(lanes < SIZE, jnp.concatenate([name, name], axis=1), 0.0)
        if shift:
            name = pltpu.roll(name, shift, 1)
        size = min(2 * LANES, total - base)
        line[:, base : base + size] = line[:, base : base + size] + name[:, :size]
    lost = jnp.max(jnp.where(lanes[:, :LANES] == LANES - 1, lost, 0.0))
    lost_ref[0, 0] = (lost > 0.0).astype(jnp.int32)
    tops = jnp.broadcast_to(line[...], (8, total))
    if total <= 2048:
        triangle(total, rows, side, tops, line, *more)
    else:
        @pl.loop(0, total // STEP)
        def _(number):
            first = pl.multiple_of(number * STEP, STEP)
            here = pl.ds(first, STEP)
            top = jnp.broadcast_to(line[:, here], (8, STEP))
            scores = product_t(rows[...], rows[here, :])
            apart = iota((8, LANES), 1) - iota((8, LANES), 0)
            for part in range(STEP // LANES):
                lanes = slice(part * LANES, (part + 1) * LANES)
                result = jnp.full((8, LANES), -1.0, F32)
                for block in range(0, total, 8):
                    at = slice(block, block + 8)
                    allowed = (side[at, :] == top[:, lanes]) & (apart != block - first - part * LANES)
                    result = jnp.maximum(result, jnp.where(allowed, scores[at, lanes], -1.0))
                line[:, pl.ds(first + part * LANES, LANES)] = jnp.max(result, axis=0, keepdims=True)

    for source in range(owners):
        base, shift = divmod(source * SIZE, LANES)
        base *= LANES
        piece = line[:, base : min(base + 2 * LANES, total)]
        if shift:
            piece = pltpu.roll(piece, piece.shape[1] - shift, 1)
        best_ref[source] = piece[:, :LANES]


def score(got, owners):
    width = got.shape[2]
    total = owners * SIZE
    return pl.pallas_call(
        functools.partial(score_kernel, owners),
        out_shape=(
            pltpu.VMEM((owners, 1, LANES), F32),
            jax.ShapeDtypeStruct((1, 1), jnp.int32),
        ),
        in_specs=[IN_VMEM],
        out_specs=(IN_VMEM, pl.BlockSpec(memory_space=pltpu.SMEM)),
        scratch_shapes=[
            pltpu.VMEM((total, LANES), F32),
            pltpu.VMEM((1, total), F32),
        ]
        + ([] if total > 2048 else [pltpu.VMEM((total, LANES), F32), pltpu.VMEM((total // 16, LANES), F32)]),
        compiler_params=pltpu.CompilerParams(vmem_limit_bytes=48 * MB),
        name="score",
    )(got)


def place_kernel(owners, back_ref, cid_ref, code_ref, valid_ref, out_ref, out, sem):
    for start in range(0, cid_ref.shape[0], 8):
        at = slice(start, start + 8)
        owner = lax.shift_right_logical(cid_ref[at, :], 3)
        code = code_ref[at, :]
        result = jnp.zeros((8, LANES), F32)
        for source in range(owners):
            line = jnp.broadcast_to(back_ref[source], (8, LANES))
            value = jnp.take_along_axis(line, code, axis=1, mode="promise_in_bounds")
            result = jnp.where(owner == source, value, result)
        out[at, :] = jnp.where(valid_ref[at, :] == 1, result, 0.0)
    store = pltpu.make_async_copy(out, out_ref, sem)
    store.start()
    store.wait()


def place(back, cluster_id, code, valid, owners):
    rows = cluster_id.shape[0]
    shape = (rows // LANES, LANES)
    return pl.pallas_call(
        functools.partial(place_kernel, owners),
        out_shape=pltpu.HBM(shape, F32),
        in_specs=[IN_VMEM] * 4,
        out_specs=ANY,
        scratch_shapes=[pltpu.VMEM(shape, F32), pltpu.SemaphoreType.DMA],
        compiler_params=pltpu.CompilerParams(vmem_limit_bytes=4 * MB),
        name="place",
    )(back, cluster_id.reshape(shape), code, valid.reshape(shape)).reshape(rows)


def every_slot(embeddings, cluster_id, valid, owners):
    width = embeddings.shape[1]
    clusters = CL_DEV * owners
    values = embeddings.astype(F32)
    squares = jnp.sum(values * values, axis=1, keepdims=True)
    unit_rows = (values * lax.rsqrt(squares + 1e-06)).astype(BF)
    one_hot = (cluster_id[:, None] == jnp.arange(clusters, dtype=jnp.int32)[None, :]).astype(jnp.int32)
    ranking = jnp.sum(jnp.cumsum(one_hot, axis=0) * one_hot, axis=1) - 1
    target = cluster_id * SLOT + ranking
    outgoing = jnp.zeros((clusters * SLOT, width), BF).at[target].set(unit_rows)
    live_out = jnp.zeros((clusters * SLOT,), BF).at[target].set(valid.astype(BF))
    got = lax.all_to_all(
        outgoing.reshape(owners, CL_DEV * SLOT, width), "owners", split_axis=0, concat_axis=0, tiled=True
    )
    live = lax.all_to_all(
        live_out.reshape(owners, CL_DEV, SLOT), "owners", split_axis=0, concat_axis=0, tiled=True
    )
    got = got.reshape(owners, CL_DEV, SLOT, width).transpose(1, 0, 2, 3)
    got = got.reshape(CL_DEV, owners * SLOT, width)
    live = live.transpose(1, 0, 2).reshape(CL_DEV, owners * SLOT) > 0.5
    diagonal = jnp.eye(owners * SLOT, dtype=bool)

    def one_cluster(args):
        rows, flags = args
        scores = jnp.einsum("md,nd->mn", rows, rows, preferred_element_type=F32)
        allowed = flags[:, None] & flags[None, :] & ~diagonal
        return jnp.max(jnp.where(allowed, scores, -1.0), axis=1)

    best = lax.map(one_cluster, (got, live)).reshape(CL_DEV, owners, SLOT).transpose(1, 0, 2)
    back = lax.all_to_all(best, "owners", split_axis=0, concat_axis=0, tiled=True)
    return jnp.where(valid == 1, back.reshape(-1)[target], 0.0)


def swap(blocks, owners):
    split = blocks.reshape(owners, blocks.shape[0] // owners, blocks.shape[1])
    return lax.all_to_all(split, "owners", split_axis=0, concat_axis=0, tiled=True)


def shards(embeddings, cluster_id, valid):
    owners = lax.axis_size("owners")
    blocks, code = pack(embeddings, cluster_id, valid, owners)
    best, lost = score(swap(blocks, owners), owners)
    back = lax.all_to_all(best, "owners", split_axis=0, concat_axis=0, tiled=True)
    nearest = place(back, cluster_id, code, valid, owners)
    return lax.cond(
        lost[0, 0] > 0,
        lambda: every_slot(embeddings, cluster_id, valid, owners),
        lambda: nearest,
    )


def solution(mesh):
    placed = (P(("groups", "owners"), None), P(("groups", "owners")), P(("groups", "owners")))
    return jax.shard_map(
        shards, mesh=mesh, in_specs=placed, out_specs=P(("groups", "owners")), check_vma=False
    )
```

```python
import functools

import jax
import jax.numpy as jnp
from jax import lax
from jax.experimental import pallas as pl
from jax.experimental.pallas import tpu as pltpu
from jax.sharding import PartitionSpec as P

CL_DEV = 8
SLOT = 16
LANES = 128
SIZE = 80
TILE = 1280
STEP = 256
MB = 1024 * 1024
BF = jnp.bfloat16
F32 = jnp.float32
ANY = pl.BlockSpec(memory_space=pltpu.HBM)
IN_VMEM = pl.BlockSpec(memory_space=pltpu.VMEM)


def iota(shape, dim):
    return lax.broadcasted_iota(jnp.int32, shape, dim)


def bits(mask):
    return mask.astype(F32).astype(BF)


def product(left, right):
    return jnp.dot(left, right, preferred_element_type=F32)


def product_t(left, right):
    return lax.dot_general(left, right, (((1,), (1,)), ((), ())), preferred_element_type=F32)


def before():
    return bits(iota((LANES, LANES), 0) < iota((LANES, LANES), 1))


def fill(choose, dest, begin):
    index = iota((choose.shape[0], LANES), 0) + begin
    for line in range(dest.shape[0]):
        at = slice(line * LANES, (line + 1) * LANES)
        choose[:, at] = bits(index == dest[line : line + 1])


def pack_kernel(
    owners, cid_ref, valid_ref, rows_ref, blocks_ref, code_ref, held, unit, choose, out, in_sems, out_sems
):
    rows, width = held.shape
    total = out.shape[0]
    tile = choose.shape[0]
    lines = rows // LANES
    parts = rows // STEP
    loads = []
    for part in range(parts):
        at = pl.ds(part * STEP, STEP)
        loads.append(pltpu.make_async_copy(rows_ref.at[at], held.at[at], in_sems.at[part]))
        loads[-1].start()

    cid = cid_ref[...]
    live = valid_ref[...] == 1
    owner = lax.shift_right_logical(cid, 3)
    name = (cid & (CL_DEV - 1)) + 1
    target = jnp.where(live, owner, -1)
    index = iota((owners, LANES), 0)
    mine = [(index == target[line : line + 1]).astype(F32) for line in range(lines)]
    stacked = jnp.concatenate(mine, axis=0).astype(BF)
    inside = product(stacked, before())
    whole = product(stacked, jnp.ones((LANES, LANES), BF))
    offset = jnp.zeros((owners, LANES), F32)
    ranks = []
    for line in range(lines):
        at = slice(line * owners, (line + 1) * owners)
        ranks.append(jnp.sum(mine[line] * (inside[at] + offset), axis=0, keepdims=True))
        offset = offset + whole[at]
    pos = jnp.concatenate(ranks, axis=0).astype(jnp.int32)
    fits = live & (pos < SIZE - 1)
    lost = jnp.max((live & (pos >= SIZE - 1)).astype(F32))
    code = jnp.where(fits, pos, LANES - 1)
    code_ref[...] = code
    dest = jnp.where(fits, owner * SIZE + pos, -1)

    names = jnp.concatenate(
        [mine[line] * name[line : line + 1].astype(F32) for line in range(lines)], axis=1
    ).astype(BF)
    index = iota((LANES, LANES), 0)
    places = jnp.concatenate([bits(index == code[line : line + 1]) for line in range(lines)], axis=1)
    meta = product_t(names, places)
    meta = jnp.where(iota((owners, LANES), 1) == LANES - 1, lost, meta).astype(BF)

    fill(choose, dest, 0)
    for part in range(parts):
        loads[part].wait()
        for chunk in range(part * STEP, (part + 1) * STEP, 64):
            values = held[chunk : chunk + 64, :].astype(F32)
            squares = jnp.sum(values * values, axis=1, keepdims=True)
            unit[chunk : chunk + 64, :] = (values * lax.rsqrt(squares + 1e-06)).astype(BF)

    stores = []
    for first in range(0, total, tile):
        if first:
            fill(choose, dest, first)
        for column in range(0, width, STEP):
            at = slice(column, column + STEP)
            packed = product(choose[...], unit[:, at])
            if column == 0:
                line = iota((tile, owners), 0) + first
                last = (iota((1, owners), 1) + 1) * SIZE - 1
                packed = jnp.concatenate(
                    [packed[:, :LANES] + product(bits(line == last), meta), packed[:, LANES:]], axis=1
                )
            out[pl.ds(first, tile), at] = packed.astype(BF)
            where = (pl.ds(first, tile), at)
            stores.append(
                pltpu.make_async_copy(out.at[where], blocks_ref.at[where], out_sems.at[len(stores)])
            )
            stores[-1].start()
    for store in stores:
        store.wait()


def pack_direct(
    owners, cid_ref, valid_ref, rows_ref, blocks_ref, code_ref, held, unit, choose, out, tags, marks, *sems
):
    rows, width = held.shape
    total = out.shape[0]
    lines = rows // LANES
    parts = rows // STEP
    pairs = STEP // LANES
    chunk = 4 * SIZE
    columns = width // STEP
    in_sems, mark_sems, out_sems = sems[:parts], sems[parts : parts + 2], sems[parts + 2 :]
    fetches = []
    for number, source in enumerate((cid_ref, valid_ref)):
        fetches.append(pltpu.make_async_copy(source, marks.at[number], mark_sems[number]))
        fetches[-1].start()
    loads = []
    for part in range(parts):
        at = pl.ds(part * STEP, STEP)
        loads.append(pltpu.make_async_copy(rows_ref.at[at], held.at[at], in_sems[part]))
        loads[-1].start()
    stores = []
    for fetch in fetches:
        fetch.wait()

    def body(count_acc, tag_acc, *accs):
        cid = marks[0]
        live = marks[1] == 1
        owner = lax.shift_right_logical(cid, 3)
        name = (cid & (CL_DEV - 1)) + 1
        target = jnp.where(live, owner, -1)
        index = iota((owners, LANES), 0)
        mine = [(index == target[line : line + 1]).astype(F32) for line in range(lines)]
        mine = [jnp.concatenate(mine[i : i + pairs], axis=1) for i in range(0, lines, pairs)]
        stacked = jnp.concatenate(mine, axis=0)
        pltpu.matmul_push_rhs(bits(iota((STEP, STEP), 0) < iota((STEP, STEP), 1)), 0, 0)
        pltpu.matmul_acc_lhs(count_acc, stacked.astype(BF), load_staged_rhs=0)
        whole = jnp.sum(stacked, axis=1, keepdims=True)
        inside = pltpu.matmul_pop(count_acc)
        offset = jnp.zeros((owners, 1), F32)
        ranks = []
        for part in range(parts):
            at = slice(part * owners, (part + 1) * owners)
            rank = jnp.sum(mine[part] * (inside[at] + offset), axis=0, keepdims=True)
            ranks += [rank[:, i * LANES : (i + 1) * LANES] for i in range(pairs)]
            offset = offset + whole[at]
        pos = jnp.concatenate(ranks, axis=0).astype(jnp.int32)
        fits = live & (pos < SIZE - 1)
        lost = jnp.max((live & (pos >= SIZE - 1)).astype(F32))
        code = jnp.where(fits, pos, LANES - 1)
        code_ref[...] = code
        dest = jnp.where(fits, owner * SIZE + pos, -1)

        def prepare(part):
            loads[part].wait()
            for begin in range(part * STEP, (part + 1) * STEP, 64):
                values = held[begin : begin + 64, :].astype(F32)
                squares = jnp.sum(values * values, axis=1, keepdims=True)
                unit[begin : begin + 64, :] = (values * lax.rsqrt(squares + 1e-06)).astype(BF)
            index = iota((total, LANES), 0)
            for line in range(part * pairs, (part + 1) * pairs):
                at = slice(line * LANES, (line + 1) * LANES)
                choose[:, at] = bits(index == dest[line : line + 1])

        def multiply(part, number, column, chunks):
            kept = slice(part * STEP, (part + 1) * STEP)
            at = slice(column * STEP, (column + 1) * STEP)
            pltpu.matmul_push_rhs(unit[kept, at], part % 2, number)
            first = True
            for place, slot in chunks:
                pltpu.matmul_acc_lhs(
                    accs[number * 3 + slot],
                    choose[place * chunk : (place + 1) * chunk, kept],
                    load_staged_rhs=part % 2 if first else None,
                )
                first = False

        def write(number, column, place, slot):
            packed = pltpu.matmul_pop(accs[number * 3 + slot])
            at = slice(column * STEP, (column + 1) * STEP)
            first = place * chunk
            for row in range(first, first + chunk, 16):
                piece = packed[row - first : row - first + 16]
                source, spot = divmod(row, SIZE)
                if column == 0 and spot + 16 == SIZE:
                    piece = jnp.where(iota((16, STEP), 0) == 15, tags[...][source : source + 1], piece)
                out[row : row + 16, at] = piece.astype(BF)
            where = (pl.ds(first, chunk), at)
            stores.append(
                pltpu.make_async_copy(out.at[where], blocks_ref.at[where], out_sems[len(stores)])
            )
            stores[-1].start()

        opening = [(place, place) for place in range(3)]
        for part in range(parts):
            prepare(part)
            if part:
                for number in range(2):
                    multiply(part - 1, number, number, opening)
        for number in range(2):
            multiply(parts - 1, number, number, opening)

        index = iota((STEP, LANES), 0)
        for part in range(parts):
            here = range(part * pairs, (part + 1) * pairs)
            places = [bits(index == code[line : line + 1]) for line in here]
            named = [name[line : line + 1].astype(F32) for line in here]
            pltpu.matmul_push_rhs(jnp.concatenate(places, axis=1), part % 2, 1, transpose=True)
            pltpu.matmul_acc_lhs(
                tag_acc,
                (mine[part] * jnp.concatenate(named, axis=1)).astype(BF),
                load_staged_rhs=part % 2,
            )
        lane = iota((owners, STEP), 1)
        tags[...] = jnp.where(
            lane < LANES - 1, pltpu.matmul_pop(tag_acc), jnp.where(lane == LANES - 1, lost, 0.0)
        )

        done = [(0, place) for place in range(3)]
        left = [(0, place) for place in range(3, total // chunk)]
        for column in range(2, columns, 2):
            left += [(column, place) for place in range(total // chunk)]
        for turn, (column, place) in enumerate(left):
            before = done[turn]
            for number in range(2):
                write(number, before[0] + number, before[1], turn % 3)
            for part in range(parts):
                for number in range(2):
                    multiply(part, number, column + number, [(place, turn % 3)])
            done.append((column, place))
        for turn in range(len(left), len(done)):
            for number in range(2):
                write(number, done[turn][0] + number, done[turn][1], turn % 3)

    pl.run_scoped(
        body,
        pltpu.ACC(mxu_id=0)((parts * owners, STEP), F32),
        pltpu.ACC(mxu_id=1)((owners, STEP), F32),
        *[pltpu.ACC(mxu_id=number // 3)((chunk, STEP), F32) for number in range(6)],
    )
    for store in stores:
        store.wait()


def pack(embeddings, cluster_id, valid, owners):
    rows, width = embeddings.shape
    total = owners * SIZE
    tile = min(total, TILE)
    lines = (rows // LANES, LANES)
    small = total <= 2048
    return pl.pallas_call(
        functools.partial(pack_direct if small else pack_kernel, owners),
        out_shape=(
            pltpu.HBM((total, width), BF),
            jax.ShapeDtypeStruct(lines, jnp.int32),
        ),
        in_specs=[ANY if small else IN_VMEM] * 2 + [ANY],
        out_specs=(ANY, IN_VMEM),
        scratch_shapes=[
            pltpu.VMEM((rows, width), BF),
            pltpu.VMEM((rows, width), BF),
            pltpu.VMEM((tile, rows), BF),
            pltpu.VMEM((total, width), BF),
        ]
        + (
            [pltpu.VMEM((owners, STEP), F32), pltpu.VMEM((2,) + lines, jnp.int32)]
            + [pltpu.SemaphoreType.DMA] * (rows // STEP + 2 + owners // 4 * (width // STEP))
            if small
            else [
                pltpu.SemaphoreType.DMA((rows // STEP,)),
                pltpu.SemaphoreType.DMA((total // tile * (width // STEP),)),
            ]
        ),
        compiler_params=pltpu.CompilerParams(vmem_limit_bytes=52 * MB),
        name="pack",
    )(cluster_id.reshape(lines), valid.reshape(lines), embeddings)


def on_units(size, count, multiply, use, meanwhile=None):
    def body(*accs):
        for number in range(count + 2):
            if number < count:
                multiply(number, number % 2, accs[number % 4])
            if number == 1 and meanwhile is not None:
                meanwhile()
            if number >= 2:
                use(number - 2, pltpu.matmul_pop(accs[(number - 2) % 4]))

    pl.run_scoped(body, *[pltpu.ACC(mxu_id=number % 2)((size, STEP), F32) for number in range(4)])


def triangle(total, rows, side, mark, line, across, down):
    width = rows.shape[1]
    blocks = total // STEP
    seen = set()

    def keep(ref, at, value):
        if (id(ref), at) in seen:
            value = jnp.maximum(value, ref[at : at + 8, :])
        seen.add((id(ref), at))
        ref[at : at + 8, :] = value

    work = []
    for column in range(blocks):
        for row in range(column, blocks, 2):
            work.append((column, row, min(2, blocks - row)))

    def run(work, count, meanwhile=None):
        def multiply(number, unit, acc):
            column, row, _ = work[number]
            for piece in range(width // STEP):
                at = slice(piece * STEP, (piece + 1) * STEP)
                pltpu.matmul_push_rhs(
                    rows[column * STEP : (column + 1) * STEP, at], piece % 2, unit, transpose=True
                )
                pltpu.matmul_acc_lhs(
                    acc, rows[row * STEP : (row + count) * STEP, at], load_staged_rhs=piece % 2
                )

        def use(number, scores):
            column, row, _ = work[number]
            apart = iota((8, LANES), 1) - iota((8, LANES), 0)
            best = [jnp.full((8, LANES), -1.0, F32)] * (STEP // LANES)
            tops = jnp.broadcast_to(line[:, column * STEP : (column + 1) * STEP], (8, STEP))
            for block in range(0, count * STEP, 8):
                start = row * STEP + block
                found = []
                for part in range(STEP // LANES):
                    first = column * STEP + part * LANES
                    allowed = side[start : start + 8, :] == tops[:, part * LANES : (part + 1) * LANES]
                    if 0 <= start - first < LANES:
                        allowed = allowed & (apart != start - first)
                    here = scores[block : block + 8, part * LANES : (part + 1) * LANES]
                    found.append(jnp.where(allowed, here, -1.0))
                    best[part] = jnp.maximum(best[part], found[part])
                if start // STEP > column:
                    keep(across, start, functools.reduce(jnp.maximum, found))
            for part in range(STEP // LANES):
                keep(down, (column * (STEP // LANES) + part) * 8, best[part])

        on_units(count * STEP, len(work), multiply, use, meanwhile)

    run([item for item in work if item[2] == 2], 2, mark)
    run([item for item in work if item[2] == 1], 1)
    for column in range(blocks):
        for part in range(STEP // LANES):
            first = column * STEP + part * LANES
            at = (column * (STEP // LANES) + part) * 8
            most = jnp.max(down[at : at + 8, :], axis=0, keepdims=True)
            if column:
                turned = across[first : first + LANES, :].T
                most = jnp.maximum(most, jnp.max(turned, axis=0, keepdims=True))
            line[:, first : first + LANES] = most


def score_kernel(owners, got_ref, best_ref, lost_ref, side, line, *more):
    total = line.shape[1]
    rows = got_ref.reshape(total, got_ref.shape[2])

    def mark():
        same = iota((SIZE, LANES), 0) == iota((SIZE, LANES), 1)
        lanes = iota((1, 2 * LANES), 1)
        lost = jnp.zeros((1, LANES), F32)
        line[...] = jnp.zeros((1, total), F32)
        for source in range(owners):
            name = got_ref[source, SIZE - 16 : SIZE, :LANES].astype(F32)[15:16]
            lost = jnp.maximum(lost, name)
            found = jnp.sum(jnp.where(same, name, 0.0), axis=1, keepdims=True)
            side[source * SIZE : (source + 1) * SIZE, :] = jnp.broadcast_to(
                jnp.where(found == 0.0, -1.0, found), (SIZE, LANES)
            )
            base, shift = divmod(source * SIZE, LANES)
            base *= LANES
            name = jnp.where(lanes < SIZE, jnp.concatenate([name, name], axis=1), 0.0)
            if shift:
                name = pltpu.roll(name, shift, 1)
            size = min(2 * LANES, total - base)
            line[:, base : base + size] = line[:, base : base + size] + name[:, :size]
        lost = jnp.max(jnp.where(lanes[:, :LANES] == LANES - 1, lost, 0.0))
        lost_ref[0, 0] = (lost > 0.0).astype(jnp.int32)

    if total <= 2048:
        triangle(total, rows, side, mark, line, *more)
    else:
        mark()
        @pl.loop(0, total // STEP)
        def _(number):
            first = pl.multiple_of(number * STEP, STEP)
            here = pl.ds(first, STEP)
            top = jnp.broadcast_to(line[:, here], (8, STEP))
            scores = product_t(rows[...], rows[here, :])
            apart = iota((8, LANES), 1) - iota((8, LANES), 0)
            for part in range(STEP // LANES):
                lanes = slice(part * LANES, (part + 1) * LANES)
                result = jnp.full((8, LANES), -1.0, F32)
                for block in range(0, total, 8):
                    at = slice(block, block + 8)
                    allowed = (side[at, :] == top[:, lanes]) & (apart != block - first - part * LANES)
                    result = jnp.maximum(result, jnp.where(allowed, scores[at, lanes], -1.0))
                line[:, pl.ds(first + part * LANES, LANES)] = jnp.max(result, axis=0, keepdims=True)

    for source in range(owners):
        base, shift = divmod(source * SIZE, LANES)
        base *= LANES
        piece = line[:, base : min(base + 2 * LANES, total)]
        if shift:
            piece = pltpu.roll(piece, piece.shape[1] - shift, 1)
        best_ref[source] = piece[:, :LANES]


def score(got, owners):
    width = got.shape[2]
    total = owners * SIZE
    return pl.pallas_call(
        functools.partial(score_kernel, owners),
        out_shape=(
            pltpu.VMEM((owners, 1, LANES), F32),
            jax.ShapeDtypeStruct((1, 1), jnp.int32),
        ),
        in_specs=[IN_VMEM],
        out_specs=(IN_VMEM, pl.BlockSpec(memory_space=pltpu.SMEM)),
        scratch_shapes=[
            pltpu.VMEM((total, LANES), F32),
            pltpu.VMEM((1, total), F32),
        ]
        + ([] if total > 2048 else [pltpu.VMEM((total, LANES), F32), pltpu.VMEM((total // 16, LANES), F32)]),
        compiler_params=pltpu.CompilerParams(vmem_limit_bytes=48 * MB),
        name="score",
    )(got)


def place_kernel(owners, back_ref, cid_ref, code_ref, valid_ref, out_ref, out, sem):
    for start in range(0, cid_ref.shape[0], 8):
        at = slice(start, start + 8)
        owner = lax.shift_right_logical(cid_ref[at, :], 3)
        code = code_ref[at, :]
        result = jnp.zeros((8, LANES), F32)
        for source in range(owners):
            line = jnp.broadcast_to(back_ref[source], (8, LANES))
            value = jnp.take_along_axis(line, code, axis=1, mode="promise_in_bounds")
            result = jnp.where(owner == source, value, result)
        out[at, :] = jnp.where(valid_ref[at, :] == 1, result, 0.0)
    store = pltpu.make_async_copy(out, out_ref, sem)
    store.start()
    store.wait()


def place(back, cluster_id, code, valid, owners):
    rows = cluster_id.shape[0]
    shape = (rows // LANES, LANES)
    return pl.pallas_call(
        functools.partial(place_kernel, owners),
        out_shape=pltpu.HBM(shape, F32),
        in_specs=[IN_VMEM] * 4,
        out_specs=ANY,
        scratch_shapes=[pltpu.VMEM(shape, F32), pltpu.SemaphoreType.DMA],
        compiler_params=pltpu.CompilerParams(vmem_limit_bytes=4 * MB),
        name="place",
    )(back, cluster_id.reshape(shape), code, valid.reshape(shape)).reshape(rows)


def every_slot(embeddings, cluster_id, valid, owners):
    width = embeddings.shape[1]
    clusters = CL_DEV * owners
    values = embeddings.astype(F32)
    squares = jnp.sum(values * values, axis=1, keepdims=True)
    unit_rows = (values * lax.rsqrt(squares + 1e-06)).astype(BF)
    one_hot = (cluster_id[:, None] == jnp.arange(clusters, dtype=jnp.int32)[None, :]).astype(jnp.int32)
    ranking = jnp.sum(jnp.cumsum(one_hot, axis=0) * one_hot, axis=1) - 1
    target = cluster_id * SLOT + ranking
    outgoing = jnp.zeros((clusters * SLOT, width), BF).at[target].set(unit_rows)
    live_out = jnp.zeros((clusters * SLOT,), BF).at[target].set(valid.astype(BF))
    got = lax.all_to_all(
        outgoing.reshape(owners, CL_DEV * SLOT, width), "owners", split_axis=0, concat_axis=0, tiled=True
    )
    live = lax.all_to_all(
        live_out.reshape(owners, CL_DEV, SLOT), "owners", split_axis=0, concat_axis=0, tiled=True
    )
    got = got.reshape(owners, CL_DEV, SLOT, width).transpose(1, 0, 2, 3)
    got = got.reshape(CL_DEV, owners * SLOT, width)
    live = live.transpose(1, 0, 2).reshape(CL_DEV, owners * SLOT) > 0.5
    diagonal = jnp.eye(owners * SLOT, dtype=bool)

    def one_cluster(args):
        rows, flags = args
        scores = jnp.einsum("md,nd->mn", rows, rows, preferred_element_type=F32)
        allowed = flags[:, None] & flags[None, :] & ~diagonal
        return jnp.max(jnp.where(allowed, scores, -1.0), axis=1)

    best = lax.map(one_cluster, (got, live)).reshape(CL_DEV, owners, SLOT).transpose(1, 0, 2)
    back = lax.all_to_all(best, "owners", split_axis=0, concat_axis=0, tiled=True)
    return jnp.where(valid == 1, back.reshape(-1)[target], 0.0)


def swap(blocks, owners):
    split = blocks.reshape(owners, blocks.shape[0] // owners, blocks.shape[1])
    return lax.all_to_all(split, "owners", split_axis=0, concat_axis=0, tiled=True)


def shards(embeddings, cluster_id, valid):
    owners = lax.axis_size("owners")
    blocks, code = pack(embeddings, cluster_id, valid, owners)
    best, lost = score(swap(blocks, owners), owners)
    back = lax.all_to_all(best, "owners", split_axis=0, concat_axis=0, tiled=True)
    nearest = place(back, cluster_id, code, valid, owners)
    return lax.cond(
        lost[0, 0] > 0,
        lambda: every_slot(embeddings, cluster_id, valid, owners),
        lambda: nearest,
    )


def solution(mesh):
    placed = (P(("groups", "owners"), None), P(("groups", "owners")), P(("groups", "owners")))
    return jax.shard_map(
        shards, mesh=mesh, in_specs=placed, out_specs=P(("groups", "owners")), check_vma=False
    )
```

```python
import functools

import jax
import jax.numpy as jnp
from jax import lax
from jax.experimental import pallas as pl
from jax.experimental.pallas import tpu as pltpu
from jax.sharding import PartitionSpec as P

CL_DEV = 8
SLOT = 16
LANES = 128
SIZE = 80
TILE = 1280
STEP = 256
MB = 1024 * 1024
BF = jnp.bfloat16
F32 = jnp.float32
ANY = pl.BlockSpec(memory_space=pltpu.HBM)
IN_VMEM = pl.BlockSpec(memory_space=pltpu.VMEM)


def iota(shape, dim):
    return lax.broadcasted_iota(jnp.int32, shape, dim)


def bits(mask):
    return mask.astype(F32).astype(BF)


def product(left, right):
    return jnp.dot(left, right, preferred_element_type=F32)


def product_t(left, right):
    return lax.dot_general(left, right, (((1,), (1,)), ((), ())), preferred_element_type=F32)


def before():
    return bits(iota((LANES, LANES), 0) < iota((LANES, LANES), 1))


def fill(choose, dest, begin):
    index = iota((choose.shape[0], LANES), 0) + begin
    for line in range(dest.shape[0]):
        at = slice(line * LANES, (line + 1) * LANES)
        choose[:, at] = bits(index == dest[line : line + 1])


def pack_kernel(
    owners, cid_ref, valid_ref, rows_ref, blocks_ref, code_ref, held, unit, choose, out, in_sems, out_sems
):
    rows, width = held.shape
    total = out.shape[0]
    tile = choose.shape[0]
    lines = rows // LANES
    parts = rows // STEP
    loads = []
    for part in range(parts):
        at = pl.ds(part * STEP, STEP)
        loads.append(pltpu.make_async_copy(rows_ref.at[at], held.at[at], in_sems.at[part]))
        loads[-1].start()

    cid = cid_ref[...]
    live = valid_ref[...] == 1
    owner = lax.shift_right_logical(cid, 3)
    name = (cid & (CL_DEV - 1)) + 1
    target = jnp.where(live, owner, -1)
    index = iota((owners, LANES), 0)
    mine = [(index == target[line : line + 1]).astype(F32) for line in range(lines)]
    stacked = jnp.concatenate(mine, axis=0).astype(BF)
    inside = product(stacked, before())
    whole = product(stacked, jnp.ones((LANES, LANES), BF))
    offset = jnp.zeros((owners, LANES), F32)
    ranks = []
    for line in range(lines):
        at = slice(line * owners, (line + 1) * owners)
        ranks.append(jnp.sum(mine[line] * (inside[at] + offset), axis=0, keepdims=True))
        offset = offset + whole[at]
    pos = jnp.concatenate(ranks, axis=0).astype(jnp.int32)
    fits = live & (pos < SIZE - 1)
    lost = jnp.max((live & (pos >= SIZE - 1)).astype(F32))
    code = jnp.where(fits, pos, LANES - 1)
    code_ref[...] = code
    dest = jnp.where(fits, owner * SIZE + pos, -1)

    names = jnp.concatenate(
        [mine[line] * name[line : line + 1].astype(F32) for line in range(lines)], axis=1
    ).astype(BF)
    index = iota((LANES, LANES), 0)
    places = jnp.concatenate([bits(index == code[line : line + 1]) for line in range(lines)], axis=1)
    meta = product_t(names, places)
    meta = jnp.where(iota((owners, LANES), 1) == LANES - 1, lost, meta).astype(BF)

    fill(choose, dest, 0)
    for part in range(parts):
        loads[part].wait()
        for chunk in range(part * STEP, (part + 1) * STEP, 64):
            values = held[chunk : chunk + 64, :].astype(F32)
            squares = jnp.sum(values * values, axis=1, keepdims=True)
            unit[chunk : chunk + 64, :] = (values * lax.rsqrt(squares + 1e-06)).astype(BF)

    stores = []
    for first in range(0, total, tile):
        if first:
            fill(choose, dest, first)
        for column in range(0, width, STEP):
            at = slice(column, column + STEP)
            packed = product(choose[...], unit[:, at])
            if column == 0:
                line = iota((tile, owners), 0) + first
                last = (iota((1, owners), 1) + 1) * SIZE - 1
                packed = jnp.concatenate(
                    [packed[:, :LANES] + product(bits(line == last), meta), packed[:, LANES:]], axis=1
                )
            out[pl.ds(first, tile), at] = packed.astype(BF)
            where = (pl.ds(first, tile), at)
            stores.append(
                pltpu.make_async_copy(out.at[where], blocks_ref.at[where], out_sems.at[len(stores)])
            )
            stores[-1].start()
    for store in stores:
        store.wait()


def pack_direct(
    owners, cid_ref, valid_ref, rows_ref, blocks_ref, code_ref, held, unit, choose, out, tags, marks, *sems
):
    rows, width = held.shape
    total = out.shape[0]
    lines = rows // LANES
    parts = rows // STEP
    pairs = STEP // LANES
    chunk = 4 * SIZE
    columns = width // STEP
    in_sems, mark_sems, out_sems = sems[:parts], sems[parts : parts + 2], sems[parts + 2 :]
    fetches = []
    for number, source in enumerate((cid_ref, valid_ref)):
        fetches.append(pltpu.make_async_copy(source, marks.at[number], mark_sems[number]))
        fetches[-1].start()
    loads = []
    for part in range(parts):
        at = pl.ds(part * STEP, STEP)
        loads.append(pltpu.make_async_copy(rows_ref.at[at], held.at[at], in_sems[part]))
        loads[-1].start()
    stores = []
    for fetch in fetches:
        fetch.wait()

    def body(count_acc, tag_acc, *accs):
        cid = marks[0]
        live = marks[1] == 1
        owner = lax.shift_right_logical(cid, 3)
        name = (cid & (CL_DEV - 1)) + 1
        target = jnp.where(live, owner, -1)
        index = iota((owners, LANES), 0)
        mine = [(index == target[line : line + 1]).astype(F32) for line in range(lines)]
        mine = [jnp.concatenate(mine[i : i + pairs], axis=1) for i in range(0, lines, pairs)]
        stacked = jnp.concatenate(mine, axis=0)
        pltpu.matmul_push_rhs(bits(iota((STEP, STEP), 0) < iota((STEP, STEP), 1)), 0, 0)
        pltpu.matmul_acc_lhs(count_acc, stacked.astype(BF), load_staged_rhs=0)
        whole = jnp.sum(stacked, axis=1, keepdims=True)
        inside = pltpu.matmul_pop(count_acc)
        offset = jnp.zeros((owners, 1), F32)
        ranks = []
        for part in range(parts):
            at = slice(part * owners, (part + 1) * owners)
            rank = jnp.sum(mine[part] * (inside[at] + offset), axis=0, keepdims=True)
            ranks += [rank[:, i * LANES : (i + 1) * LANES] for i in range(pairs)]
            offset = offset + whole[at]
        pos = jnp.concatenate(ranks, axis=0).astype(jnp.int32)
        fits = live & (pos < SIZE - 1)
        lost = jnp.max((live & (pos >= SIZE - 1)).astype(F32))
        code = jnp.where(fits, pos, LANES - 1)
        code_ref[...] = code
        dest = jnp.where(fits, owner * SIZE + pos, -1)

        def prepare(part):
            index = iota((total, LANES), 0)
            for line in range(part * pairs, (part + 1) * pairs):
                at = slice(line * LANES, (line + 1) * LANES)
                choose[:, at] = bits(index == dest[line : line + 1])
            loads[part].wait()
            for begin in range(part * STEP, (part + 1) * STEP, 64):
                values = held[begin : begin + 64, :].astype(F32)
                squares = jnp.sum(values * values, axis=1, keepdims=True)
                unit[begin : begin + 64, :] = (values * lax.rsqrt(squares + 1e-06)).astype(BF)

        def multiply(part, number, column, chunks):
            kept = slice(part * STEP, (part + 1) * STEP)
            at = slice(column * STEP, (column + 1) * STEP)
            pltpu.matmul_push_rhs(unit[kept, at], part % 2, number)
            first = True
            for place, slot in chunks:
                pltpu.matmul_acc_lhs(
                    accs[number * 3 + slot],
                    choose[place * chunk : (place + 1) * chunk, kept],
                    load_staged_rhs=part % 2 if first else None,
                )
                first = False

        def write(number, column, place, slot):
            packed = pltpu.matmul_pop(accs[number * 3 + slot])
            at = slice(column * STEP, (column + 1) * STEP)
            first = place * chunk
            for row in range(first, first + chunk, 16):
                piece = packed[row - first : row - first + 16]
                source, spot = divmod(row, SIZE)
                if column == 0 and spot + 16 == SIZE:
                    piece = jnp.where(iota((16, STEP), 0) == 15, tags[...][source : source + 1], piece)
                out[row : row + 16, at] = piece.astype(BF)
            where = (pl.ds(first, chunk), at)
            stores.append(
                pltpu.make_async_copy(out.at[where], blocks_ref.at[where], out_sems[len(stores)])
            )
            stores[-1].start()

        opening = [(place, place) for place in range(3)]
        for part in range(parts):
            prepare(part)
            if part:
                for number in range(2):
                    multiply(part - 1, number, number, opening)
        for number in range(2):
            multiply(parts - 1, number, number, opening)

        index = iota((STEP, LANES), 0)
        for part in range(parts):
            here = range(part * pairs, (part + 1) * pairs)
            places = [bits(index == code[line : line + 1]) for line in here]
            named = [name[line : line + 1].astype(F32) for line in here]
            pltpu.matmul_push_rhs(jnp.concatenate(places, axis=1), part % 2, 1, transpose=True)
            pltpu.matmul_acc_lhs(
                tag_acc,
                (mine[part] * jnp.concatenate(named, axis=1)).astype(BF),
                load_staged_rhs=part % 2,
            )
        lane = iota((owners, STEP), 1)
        tags[...] = jnp.where(
            lane < LANES - 1, pltpu.matmul_pop(tag_acc), jnp.where(lane == LANES - 1, lost, 0.0)
        )

        done = [(0, place) for place in range(3)]
        left = [(0, place) for place in range(3, total // chunk)]
        for column in range(2, columns, 2):
            left += [(column, place) for place in range(total // chunk)]
        for turn, (column, place) in enumerate(left):
            before = done[turn]
            for number in range(2):
                write(number, before[0] + number, before[1], turn % 3)
            for part in range(parts):
                for number in range(2):
                    multiply(part, number, column + number, [(place, turn % 3)])
            done.append((column, place))
        for turn in range(len(left), len(done)):
            for number in range(2):
                write(number, done[turn][0] + number, done[turn][1], turn % 3)

    pl.run_scoped(
        body,
        pltpu.ACC(mxu_id=0)((parts * owners, STEP), F32),
        pltpu.ACC(mxu_id=1)((owners, STEP), F32),
        *[pltpu.ACC(mxu_id=number // 3)((chunk, STEP), F32) for number in range(6)],
    )
    for store in stores:
        store.wait()


def pack(embeddings, cluster_id, valid, owners):
    rows, width = embeddings.shape
    total = owners * SIZE
    tile = min(total, TILE)
    lines = (rows // LANES, LANES)
    small = total <= 2048
    return pl.pallas_call(
        functools.partial(pack_direct if small else pack_kernel, owners),
        out_shape=(
            pltpu.HBM((total, width), BF),
            jax.ShapeDtypeStruct(lines, jnp.int32),
        ),
        in_specs=[ANY if small else IN_VMEM] * 2 + [ANY],
        out_specs=(ANY, IN_VMEM),
        scratch_shapes=[
            pltpu.VMEM((rows, width), BF),
            pltpu.VMEM((rows, width), BF),
            pltpu.VMEM((tile, rows), BF),
            pltpu.VMEM((total, width), BF),
        ]
        + (
            [pltpu.VMEM((owners, STEP), F32), pltpu.VMEM((2,) + lines, jnp.int32)]
            + [pltpu.SemaphoreType.DMA] * (rows // STEP + 2 + owners // 4 * (width // STEP))
            if small
            else [
                pltpu.SemaphoreType.DMA((rows // STEP,)),
                pltpu.SemaphoreType.DMA((total // tile * (width // STEP),)),
            ]
        ),
        compiler_params=pltpu.CompilerParams(vmem_limit_bytes=52 * MB),
        name="pack",
    )(cluster_id.reshape(lines), valid.reshape(lines), embeddings)


def on_units(size, count, multiply, use):
    def body(*accs):
        for number in range(count + 2):
            if number < count:
                multiply(number, number % 2, accs[number % 4])
            if number >= 2:
                use(number - 2, pltpu.matmul_pop(accs[(number - 2) % 4]))

    pl.run_scoped(body, *[pltpu.ACC(mxu_id=number % 2)((size, STEP), F32) for number in range(4)])


def triangle(total, rows, side, tops, line, across, down):
    width = rows.shape[1]
    blocks = total // STEP
    seen = set()

    def keep(ref, at, value):
        if (id(ref), at) in seen:
            value = jnp.maximum(value, ref[at : at + 8, :])
        seen.add((id(ref), at))
        ref[at : at + 8, :] = value

    work = []
    for column in range(blocks):
        for row in range(column, blocks, 2):
            work.append((column, row, min(2, blocks - row)))

    def run(work, count):
        def multiply(number, unit, acc):
            column, row, _ = work[number]
            for piece in range(width // STEP):
                at = slice(piece * STEP, (piece + 1) * STEP)
                pltpu.matmul_push_rhs(
                    rows[column * STEP : (column + 1) * STEP, at], piece % 2, unit, transpose=True
                )
                pltpu.matmul_acc_lhs(
                    acc, rows[row * STEP : (row + count) * STEP, at], load_staged_rhs=piece % 2
                )

        def use(number, scores):
            column, row, _ = work[number]
            apart = iota((8, LANES), 1) - iota((8, LANES), 0)
            best = [jnp.full((8, LANES), -1.0, F32)] * (STEP // LANES)
            for block in range(0, count * STEP, 8):
                start = row * STEP + block
                found = []
                for part in range(STEP // LANES):
                    first = column * STEP + part * LANES
                    allowed = side[start : start + 8, :] == tops[:, first : first + LANES]
                    if 0 <= start - first < LANES:
                        allowed = allowed & (apart != start - first)
                    here = scores[block : block + 8, part * LANES : (part + 1) * LANES]
                    found.append(jnp.where(allowed, here, -1.0))
                    best[part] = jnp.maximum(best[part], found[part])
                if start // STEP > column:
                    keep(across, start, functools.reduce(jnp.maximum, found))
            for part in range(STEP // LANES):
                keep(down, (column * (STEP // LANES) + part) * 8, best[part])

        on_units(count * STEP, len(work), multiply, use)

    run([item for item in work if item[2] == 2], 2)
    run([item for item in work if item[2] == 1], 1)
    for column in range(blocks):
        for part in range(STEP // LANES):
            first = column * STEP + part * LANES
            at = (column * (STEP // LANES) + part) * 8
            most = jnp.max(down[at : at + 8, :], axis=0, keepdims=True)
            if column:
                turned = across[first : first + LANES, :].T
                most = jnp.maximum(most, jnp.max(turned, axis=0, keepdims=True))
            line[:, first : first + LANES] = most


def score_kernel(owners, got_ref, best_ref, lost_ref, side, line, *more):
    total = line.shape[1]
    rows = got_ref.reshape(total, got_ref.shape[2])

    same = iota((SIZE, LANES), 0) == iota((SIZE, LANES), 1)
    lanes = iota((1, 2 * LANES), 1)
    lost = jnp.zeros((1, LANES), F32)
    line[...] = jnp.zeros((1, total), F32)
    for source in range(owners):
        name = got_ref[source, SIZE - 16 : SIZE, :LANES].astype(F32)[15:16]
        lost = jnp.maximum(lost, name)
        found = jnp.sum(jnp.where(same, name, 0.0), axis=1, keepdims=True)
        side[source * SIZE : (source + 1) * SIZE, :] = jnp.broadcast_to(
            jnp.where(found == 0.0, -1.0, found), (SIZE, LANES)
        )
        base, shift = divmod(source * SIZE, LANES)
        base *= LANES
        name = jnp.where(lanes < SIZE, jnp.concatenate([name, name], axis=1), 0.0)
        if shift:
            name = pltpu.roll(name, shift, 1)
        size = min(2 * LANES, total - base)
        line[:, base : base + size] = line[:, base : base + size] + name[:, :size]
    lost = jnp.max(jnp.where(lanes[:, :LANES] == LANES - 1, lost, 0.0))
    lost_ref[0, 0] = (lost > 0.0).astype(jnp.int32)
    tops = jnp.broadcast_to(line[...], (8, total))
    if total <= 2048:
        triangle(total, rows, side, tops, line, *more)
    else:
        @pl.loop(0, total // STEP)
        def _(number):
            first = pl.multiple_of(number * STEP, STEP)
            here = pl.ds(first, STEP)
            top = jnp.broadcast_to(line[:, here], (8, STEP))
            scores = product_t(rows[...], rows[here, :])
            apart = iota((8, LANES), 1) - iota((8, LANES), 0)
            for part in range(STEP // LANES):
                lanes = slice(part * LANES, (part + 1) * LANES)
                result = jnp.full((8, LANES), -1.0, F32)
                for block in range(0, total, 8):
                    at = slice(block, block + 8)
                    allowed = (side[at, :] == top[:, lanes]) & (apart != block - first - part * LANES)
                    result = jnp.maximum(result, jnp.where(allowed, scores[at, lanes], -1.0))
                line[:, pl.ds(first + part * LANES, LANES)] = jnp.max(result, axis=0, keepdims=True)

    for source in range(owners):
        base, shift = divmod(source * SIZE, LANES)
        base *= LANES
        piece = line[:, base : min(base + 2 * LANES, total)]
        if shift:
            piece = pltpu.roll(piece, piece.shape[1] - shift, 1)
        best_ref[source] = piece[:, :LANES]


def score(got, owners):
    width = got.shape[2]
    total = owners * SIZE
    return pl.pallas_call(
        functools.partial(score_kernel, owners),
        out_shape=(
            pltpu.VMEM((owners, 1, LANES), F32),
            jax.ShapeDtypeStruct((1, 1), jnp.int32),
        ),
        in_specs=[IN_VMEM],
        out_specs=(IN_VMEM, pl.BlockSpec(memory_space=pltpu.SMEM)),
        scratch_shapes=[
            pltpu.VMEM((total, LANES), F32),
            pltpu.VMEM((1, total), F32),
        ]
        + ([] if total > 2048 else [pltpu.VMEM((total, LANES), F32), pltpu.VMEM((total // 16, LANES), F32)]),
        compiler_params=pltpu.CompilerParams(vmem_limit_bytes=48 * MB),
        name="score",
    )(got)


def place_kernel(owners, back_ref, cid_ref, code_ref, valid_ref, out_ref, out, sem):
    for start in range(0, cid_ref.shape[0], 8):
        at = slice(start, start + 8)
        owner = lax.shift_right_logical(cid_ref[at, :], 3)
        code = code_ref[at, :]
        result = jnp.zeros((8, LANES), F32)
        for source in range(owners):
            line = jnp.broadcast_to(back_ref[source], (8, LANES))
            value = jnp.take_along_axis(line, code, axis=1, mode="promise_in_bounds")
            result = jnp.where(owner == source, value, result)
        out[at, :] = jnp.where(valid_ref[at, :] == 1, result, 0.0)
    store = pltpu.make_async_copy(out, out_ref, sem)
    store.start()
    store.wait()


def place(back, cluster_id, code, valid, owners):
    rows = cluster_id.shape[0]
    shape = (rows // LANES, LANES)
    return pl.pallas_call(
        functools.partial(place_kernel, owners),
        out_shape=pltpu.HBM(shape, F32),
        in_specs=[IN_VMEM] * 4,
        out_specs=ANY,
        scratch_shapes=[pltpu.VMEM(shape, F32), pltpu.SemaphoreType.DMA],
        compiler_params=pltpu.CompilerParams(vmem_limit_bytes=4 * MB),
        name="place",
    )(back, cluster_id.reshape(shape), code, valid.reshape(shape)).reshape(rows)


def every_slot(embeddings, cluster_id, valid, owners):
    width = embeddings.shape[1]
    clusters = CL_DEV * owners
    values = embeddings.astype(F32)
    squares = jnp.sum(values * values, axis=1, keepdims=True)
    unit_rows = (values * lax.rsqrt(squares + 1e-06)).astype(BF)
    one_hot = (cluster_id[:, None] == jnp.arange(clusters, dtype=jnp.int32)[None, :]).astype(jnp.int32)
    ranking = jnp.sum(jnp.cumsum(one_hot, axis=0) * one_hot, axis=1) - 1
    target = cluster_id * SLOT + ranking
    outgoing = jnp.zeros((clusters * SLOT, width), BF).at[target].set(unit_rows)
    live_out = jnp.zeros((clusters * SLOT,), BF).at[target].set(valid.astype(BF))
    got = lax.all_to_all(
        outgoing.reshape(owners, CL_DEV * SLOT, width), "owners", split_axis=0, concat_axis=0, tiled=True
    )
    live = lax.all_to_all(
        live_out.reshape(owners, CL_DEV, SLOT), "owners", split_axis=0, concat_axis=0, tiled=True
    )
    got = got.reshape(owners, CL_DEV, SLOT, width).transpose(1, 0, 2, 3)
    got = got.reshape(CL_DEV, owners * SLOT, width)
    live = live.transpose(1, 0, 2).reshape(CL_DEV, owners * SLOT) > 0.5
    diagonal = jnp.eye(owners * SLOT, dtype=bool)

    def one_cluster(args):
        rows, flags = args
        scores = jnp.einsum("md,nd->mn", rows, rows, preferred_element_type=F32)
        allowed = flags[:, None] & flags[None, :] & ~diagonal
        return jnp.max(jnp.where(allowed, scores, -1.0), axis=1)

    best = lax.map(one_cluster, (got, live)).reshape(CL_DEV, owners, SLOT).transpose(1, 0, 2)
    back = lax.all_to_all(best, "owners", split_axis=0, concat_axis=0, tiled=True)
    return jnp.where(valid == 1, back.reshape(-1)[target], 0.0)


def swap(blocks, owners):
    split = blocks.reshape(owners, blocks.shape[0] // owners, blocks.shape[1])
    return lax.all_to_all(split, "owners", split_axis=0, concat_axis=0, tiled=True)


def shards(embeddings, cluster_id, valid):
    owners = lax.axis_size("owners")
    blocks, code = pack(embeddings, cluster_id, valid, owners)
    best, lost = score(swap(blocks, owners), owners)
    back = lax.all_to_all(best, "owners", split_axis=0, concat_axis=0, tiled=True)
    nearest = place(back, cluster_id, code, valid, owners)
    return lax.cond(
        lost[0, 0] > 0,
        lambda: every_slot(embeddings, cluster_id, valid, owners),
        lambda: nearest,
    )


def solution(mesh):
    placed = (P(("groups", "owners"), None), P(("groups", "owners")), P(("groups", "owners")))
    return jax.shard_map(
        shards, mesh=mesh, in_specs=placed, out_specs=P(("groups", "owners")), check_vma=False
    )
```
